32 devices in a mesh: fsdp: 4 (over y, x), ctx: 4 (over z), tp: 2 (over core).
Axes of the slice: x: 2, y: 2, z: 4, core: 2. Of those that a mesh axis runs over, the one named last changes fastest.
Arguments:
- tokens: bfloat16 [8, 1024, 2048], P('fsdp', 'ctx'), may hold values from -6 to 6
- lengths: int32 [8], P('fsdp'), may hold values from 256 to 1024, as said below
- cotangent: bfloat16 [8, 1024, 2048], P('fsdp', 'ctx'), may hold values from -6 to 6
- pre_gain: bfloat16 [2048], P(('fsdp', 'ctx')), may hold values from 0.5 to 1.5
- pre_bias: bfloat16 [2048], P(('fsdp', 'ctx')), may hold values from -1 to 1
- query_weight: bfloat16 [2048, 2048], P(('fsdp', 'ctx'), 'tp'), may hold values from -0.125 to 0.125
- key_weight: bfloat16 [2048, 2048], P(('fsdp', 'ctx'), 'tp'), may hold values from -0.125 to 0.125
- value_weight: bfloat16 [2048, 4096], P(('fsdp', 'ctx'), 'tp'), may hold values from -0.125 to 0.125
- swish_weight: bfloat16 [2048, 4096], P(('fsdp', 'ctx'), 'tp'), may hold values from -0.125 to 0.125
- out_weight: bfloat16 [4096, 2048], P('tp', ('fsdp', 'ctx')), may hold values from -0.125 to 0.125
- group_gain: bfloat16 [8, 512], P('tp', ('fsdp', 'ctx')), may hold values from 0.5 to 1.5
- group_bias: bfloat16 [8, 512], P('tp', ('fsdp', 'ctx')), may hold values from -1 to 1
- mlp_gain: bfloat16 [2048], P(('fsdp', 'ctx')), may hold values from 0.5 to 1.5
- mlp_bias: bfloat16 [2048], P(('fsdp', 'ctx')), may hold values from -1 to 1
- gelu_weight: bfloat16 [2048, 4096], P(('fsdp', 'ctx'), 'tp'), may hold values from -0.125 to 0.125
- up_weight: bfloat16 [2048, 4096], P(('fsdp', 'ctx'), 'tp'), may hold values from -0.125 to 0.125
- down_weight: bfloat16 [4096, 2048], P('tp', ('fsdp', 'ctx')), may hold values from -0.125 to 0.125
Outputs:
- block_out: bfloat16 [8, 1024, 2048], P('fsdp', 'ctx')
- grad_tokens: bfloat16 [8, 1024, 2048], P('fsdp', 'ctx')
- grad_pre_gain: float32 [2048], P(('fsdp', 'ctx'))
- grad_pre_bias: float32 [2048], P(('fsdp', 'ctx'))
- grad_query: float32 [2048, 2048], P(('fsdp', 'ctx'), 'tp')
- grad_key: float32 [2048, 2048], P(('fsdp', 'ctx'), 'tp')
- grad_value: float32 [2048, 4096], P(('fsdp', 'ctx'), 'tp')
- grad_swish: float32 [2048, 4096], P(('fsdp', 'ctx'), 'tp')
- grad_out: float32 [4096, 2048], P('tp', ('fsdp', 'ctx'))
- grad_group_gain: float32 [8, 512], P('tp', ('fsdp', 'ctx'))
- grad_group_bias: float32 [8, 512], P('tp', ('fsdp', 'ctx'))
- grad_mlp_gain: float32 [2048], P(('fsdp', 'ctx'))
- grad_mlp_bias: float32 [2048], P(('fsdp', 'ctx'))
- grad_gelu: float32 [2048, 4096], P(('fsdp', 'ctx'), 'tp')
- grad_up: float32 [2048, 4096], P(('fsdp', 'ctx'), 'tp')
- grad_down: float32 [4096, 2048], P('tp', ('fsdp', 'ctx'))
The draws below stay inside these ranges and needn't reach their ends.
Inputs may be any that keep to these rules, and one draw needn't show every extreme that they name: `lengths`: valid tokens stand at the start of a sequence; in each group of 2 consecutive sequences one sequence has 1024 valid tokens, and one sequence of the batch has 256.
All inputs are finite; a program needn't handle non-finite values.
Results may differ from the reference program's by a relative error of at most 0.018.
Values may be sent and summed in bfloat16 or wider, within the bound.
A program may use at most 256 MiB of HBM per device.

```python
import jax
import jax.numpy as jnp
from jax import lax

D = 2048
HEADS = 8
KDIM = 256
VDIM = 512
FF = 4096
SPAN = 256
SEQ_DEV = 2
LEN = 1024
SEQS = 8


def draw_lengths(key, part):
    key = jax.random.fold_in(key, 11)
    base_key, full_key, short_key = jax.random.split(key, 3)
    groups = SEQS // SEQ_DEV
    drawn = jax.random.randint(base_key, (SEQS,), LEN // 4, LEN + 1)
    full_pick = jax.random.randint(full_key, (groups,), 0, SEQ_DEV)
    short_group = jax.random.randint(short_key, (), 0, groups)
    index = jnp.arange(SEQS)
    group_of = index // SEQ_DEV
    member = index % SEQ_DEV
    chosen = full_pick[group_of]
    drawn = jnp.where((group_of == short_group) & (member == (chosen + 1) % SEQ_DEV), LEN // 4, drawn)
    return jnp.where(member == chosen, LEN, drawn).astype(jnp.int32)


def block_levels(own_key, shape, shards, smallest, largest):
    def one(position, shards_of):
        heights = jax.random.uniform(jax.random.fold_in(jax.random.fold_in(own_key, 6), position), (shards_of,), jnp.float32, smallest / len(shards), largest / len(shards))
        return jnp.repeat(jnp.exp(heights), shape[position] // shards_of).reshape((-1,) + (1,) * (len(shape) - position - 1))

    level = one(*shards[0])
    for cut in shards[1:]:
        level = level * one(*cut)
    return level


def normal_values(key, extent, scale, reach, shards=(), kind=jnp.bfloat16):
    values = jax.random.normal(key, extent, jnp.float32) * scale
    if len(shards) > 0:
        values = block_levels(key, extent, shards, -0.22, 0.18) * values
    return jnp.clip(values, min=-reach, max=reach).astype(kind)


def setup_inputs(seed: int = 0) -> dict:
    splits = jax.random.split(jax.random.key(seed), 18)
    tokens = normal_values(splits[0], (SEQS, LEN, D), 1.0, 6.0, ((0, 4), (1, 4)))
    lengths = draw_lengths(jax.random.fold_in(splits[17], 71), 0)
    cotangent = normal_values(splits[2], (SEQS, LEN, D), 1.0, 6.0, ((0, 4), (1, 4)))
    pre_gain = jnp.clip(1.0 + 0.1 * jax.random.normal(splits[3], (D,), jnp.float32), 0.5, 1.5).astype(jnp.bfloat16)
    pre_bias = normal_values(splits[4], (D,), 0.2, 1.0, ((0, 16),))
    query_weight = normal_values(splits[5], (D, HEADS * KDIM), D ** -0.5, 0.125, ((0, 16), (1, 2)))
    key_weight = normal_values(splits[6], (D, HEADS * KDIM), D ** -0.5, 0.125, ((0, 16), (1, 2)))
    value_weight = normal_values(splits[7], (D, HEADS * VDIM), D ** -0.5, 0.125, ((0, 16), (1, 2)))
    swish_weight = normal_values(splits[8], (D, HEADS * VDIM), D ** -0.5, 0.125, ((0, 16), (1, 2)))
    out_weight = normal_values(splits[9], (HEADS * VDIM, D), (HEADS * VDIM // 2) ** -0.5, 0.125, ((0, 2), (1, 16)))
    group_gain = jnp.clip(1.0 + 0.1 * jax.random.normal(splits[10], (HEADS, VDIM), jnp.float32), 0.5, 1.5).astype(jnp.bfloat16)
    group_bias = normal_values(splits[11], (HEADS, VDIM), 0.2, 1.0, ((0, 2), (1, 16)))
    mlp_gain = jnp.clip(1.0 + 0.1 * jax.random.normal(splits[12], (D,), jnp.float32), 0.5, 1.5).astype(jnp.bfloat16)
    mlp_bias = normal_values(splits[13], (D,), 0.2, 1.0, ((0, 16),))
    gelu_weight = normal_values(splits[14], (D, FF), D ** -0.5, 0.125, ((0, 16), (1, 2)))
    up_weight = normal_values(splits[15], (D, FF), D ** -0.5, 0.125, ((0, 16), (1, 2)))
    down_weight = normal_values(splits[16], (FF, D), (FF // 2) ** -0.5, 0.125, ((0, 2), (1, 16)))
    return dict(tokens=tokens, lengths=lengths, cotangent=cotangent, pre_gain=pre_gain, pre_bias=pre_bias, query_weight=query_weight, key_weight=key_weight, value_weight=value_weight, swish_weight=swish_weight, out_weight=out_weight, group_gain=group_gain, group_bias=group_bias, mlp_gain=mlp_gain, mlp_bias=mlp_bias, gelu_weight=gelu_weight, up_weight=up_weight, down_weight=down_weight)


eps = 1e-05
group_floor = 1.0
highest = lax.Precision.HIGHEST

@jax.custom_vjp
def low(v):
    return lax.optimization_barrier(v.astype(jnp.bfloat16)).astype(jnp.float32)

@jax.custom_vjp
def low_back(v):
    return v

def low_keep(v):
    return (low(v), None)

def low_pass(kept, grad):
    return (grad,)

def back_keep(v):
    return (v, None)

def back_low(kept, grad):
    return (low(grad),)
low.defvjp(low_keep, low_pass)
low_back.defvjp(back_keep, back_low)

def layer_norm(values, norm_gain, norm_shift):
    centred = values - lax.optimization_barrier(jnp.mean(values, -1, keepdims=True))
    spread = lax.optimization_barrier(jnp.mean(centred * centred, -1, keepdims=True))
    return centred * lax.rsqrt(spread + eps) * norm_gain + norm_shift

def turn_tables(positions, half_size):
    frequency = jnp.power(10000.0, -jnp.arange(half_size).astype(jnp.float32) / half_size)
    angles = positions.astype(jnp.float32)[:, None] * frequency[None, :]
    return (jnp.cos(angles)[:, None, :], jnp.sin(angles)[:, None, :])

def rotate(values, cosine, sine_table):
    half_size = values.shape[-1] // 2
    first_half = values[..., :half_size]
    second = values[..., half_size:]
    return jnp.concatenate([first_half * cosine - second * sine_table, second * cosine + first_half * sine_table], -1)

def decay_logs(first_head, head_count):
    head_ids = (first_head + jnp.arange(head_count)).astype(jnp.float32)
    return jnp.log1p(-jnp.exp2(-5.0 - head_ids))

def decay_tables(log_decay, span_len):
    offsets = jnp.arange(span_len)
    distance = (offsets[:, None] - offsets[None, :]).astype(jnp.float32)
    within_fade = jnp.where(distance[None] >= 0, jnp.exp(jnp.maximum(distance, 0.0)[None] * log_decay[:, None, None]), 0.0)
    key_fade = jnp.exp((span_len - 1 - offsets).astype(jnp.float32)[:, None] * log_decay[None, :])
    query_fade = jnp.exp((offsets + 1).astype(jnp.float32)[:, None] * log_decay[None, :])
    block_fade = jnp.exp(span_len * log_decay)
    return (within_fade, key_fade, query_fade, block_fade)

def gate_mix(mixed, swish_pre, norm_gain, norm_shift):
    centred = mixed - lax.optimization_barrier(jnp.mean(mixed, -1, keepdims=True))
    spread = lax.optimization_barrier(jnp.mean(centred * centred, -1, keepdims=True))
    return jax.nn.silu(swish_pre) * (centred * lax.rsqrt(spread + group_floor) * norm_gain + norm_shift)

def mlp_mix(gelu_pre, up_pre):
    return jax.nn.gelu(gelu_pre) * up_pre

def matmul(left, right):
    return jnp.dot(left, right, precision=highest, preferred_element_type=jnp.float32)

def retention(queries, keys, values, log_decay):
    blocks = queries.shape[0] // SPAN
    query_blocks = queries.reshape(blocks, SPAN, HEADS, KDIM)
    key_blocks = keys.reshape(blocks, SPAN, HEADS, KDIM)
    value_blocks = values.reshape(blocks, SPAN, HEADS, VDIM)
    within_fade, key_fade, query_fade, block_fade = decay_tables(log_decay, SPAN)
    scores = low_back(jnp.einsum('bihd,bjhd->bhij', query_blocks, key_blocks, precision=highest))
    probs = low(scores * within_fade[None])
    inner = jnp.einsum('bhij,bjhe->bihe', probs, value_blocks, precision=highest)
    local_state = jnp.einsum('bjhd,bjhe->bhde', key_blocks * key_fade[None, :, :, None], value_blocks, precision=highest)

    def carry_state(state, piece):
        return (block_fade[:, None, None] * state + piece, state)
    _, entering = lax.scan(carry_state, jnp.zeros((HEADS, KDIM, VDIM), jnp.float32), local_state)
    outer = jnp.einsum('bihd,bhde->bihe', query_blocks * query_fade[None, :, :, None], entering, precision=highest)
    return (inner + outer).reshape(blocks * SPAN, HEADS, VDIM)

def sequence_forward(params, seq_inputs, seq_length):
    pre_gain, pre_bias, query_weight, key_weight, value_weight, swish_weight, out_weight, group_gain, group_bias, mlp_gain, mlp_bias, gelu_weight, up_weight, down_weight = params
    positions = jnp.arange(LEN)
    valid_mask = (positions < seq_length).astype(jnp.float32)[:, None]
    normed = low(layer_norm(seq_inputs, pre_gain, pre_bias))
    query_pre = low_back(matmul(normed, query_weight)).reshape(LEN, HEADS, KDIM)
    key_pre = low_back(matmul(normed, key_weight)).reshape(LEN, HEADS, KDIM)
    value_pre = low_back(matmul(normed, value_weight))
    swish_pre = low_back(matmul(normed, swish_weight)).reshape(LEN, HEADS, VDIM)
    cosine, sine_table = turn_tables(positions, KDIM // 2)
    queries = low(rotate(query_pre, cosine, sine_table))
    keys = low(rotate(key_pre, cosine, sine_table) * KDIM ** (-0.5) * valid_mask[:, :, None])
    values = low(value_pre).reshape(LEN, HEADS, VDIM)
    mixed = low_back(retention(queries, keys, values, decay_logs(0, HEADS)))
    gated = low(gate_mix(mixed, swish_pre, group_gain, group_bias).reshape(LEN, HEADS * VDIM))
    branch = low_back(matmul(gated, out_weight))
    hidden = seq_inputs + branch
    mlp_in = low(layer_norm(hidden, mlp_gain, mlp_bias))
    gelu_pre = low_back(matmul(mlp_in, gelu_weight))
    up_pre = low_back(matmul(mlp_in, up_weight))
    inner = low(mlp_mix(gelu_pre, up_pre))
    mlp_out = low_back(matmul(inner, down_weight))
    return valid_mask * (hidden + mlp_out)

def reference(tokens, lengths, cotangent, pre_gain, pre_bias, query_weight, key_weight, value_weight, swish_weight, out_weight, group_gain, group_bias, mlp_gain, mlp_bias, gelu_weight, up_weight, down_weight):
    params = tuple((weight.astype(jnp.float32) for weight in (pre_gain, pre_bias, query_weight, key_weight, value_weight, swish_weight, out_weight, group_gain, group_bias, mlp_gain, mlp_bias, gelu_weight, up_weight, down_weight)))
    inputs = tokens.astype(jnp.float32)

    def forward(inputs, params):

        def visit(carried, pieces):
            return (carried, jax.checkpoint(sequence_forward)(params, pieces[0], pieces[1]))
        _, result = lax.scan(visit, jnp.zeros((), jnp.float32), (inputs, lengths))
        return result
    result, pull = jax.vjp(forward, inputs, params)
    grad_inputs, grads = pull(cotangent.astype(jnp.float32))
    return (result.astype(jnp.bfloat16), grad_inputs.astype(jnp.bfloat16), grads[0], grads[1], grads[2], grads[3], grads[4], grads[5], grads[6], grads[7], grads[8], grads[9], grads[10], grads[11], grads[12], grads[13])
```

```python
import jax
import jax.numpy as jnp
from jax import lax
from jax.sharding import PartitionSpec as P

eps = 1e-05
group_floor = 1.0
f32 = jnp.float32
bf16 = jnp.bfloat16


def layer_norm(values, norm_gain, norm_shift):
    centred = values - jnp.mean(values, -1, keepdims=True)
    spread = jnp.mean(centred * centred, -1, keepdims=True)
    return centred * lax.rsqrt(spread + eps) * norm_gain + norm_shift


def turn_tables(positions, half_size):
    frequency = jnp.power(10000.0, -jnp.arange(half_size).astype(f32) / half_size)
    angles = positions.astype(f32)[:, None] * frequency[None, :]
    return jnp.cos(angles), jnp.sin(angles)


def rotate(values, cosine, sine):
    half_size = values.shape[-1] // 2
    first = values[..., :half_size]
    second = values[..., half_size:]
    return jnp.concatenate([first * cosine - second * sine, second * cosine + first * sine], -1)


def rotate_back(values, cosine, sine):
    return rotate(values, cosine, -sine)


def gate_mix(mixed, swish_pre, norm_gain, norm_shift):
    centred = mixed - jnp.mean(mixed, -1, keepdims=True)
    spread = jnp.mean(centred * centred, -1, keepdims=True)
    return jax.nn.silu(swish_pre) * (
        centred * lax.rsqrt(spread + group_floor) * norm_gain + norm_shift
    )


def mlp_mix(gelu_pre, up_pre):
    return jax.nn.gelu(gelu_pre) * up_pre


def product(left, right):
    return jnp.dot(left, right, preferred_element_type=f32)


def product_left(left, right):
    return lax.dot_general(left, right, (((0,), (0,)), ((), ())), preferred_element_type=f32)


def product_right(left, right):
    return lax.dot_general(left, right, (((1,), (1,)), ((), ())), preferred_element_type=f32)


def blocks(spec, left, right):
    return jnp.einsum(spec, left, right, preferred_element_type=f32)


def gather_rows(own):
    return lax.all_gather(own, ("fsdp", "tp"), axis=0, tiled=True)


def scatter_rows(partial):
    return lax.psum_scatter(partial, ("fsdp", "tp"), scatter_dimension=0, tiled=True)


def pass_states(local, fade, by):
    length = lax.axis_size("ctx")
    pairs = [(i, i + by) for i in range(length) if 0 <= i + by < length]

    def step(turn, received):
        return lax.ppermute((fade * received.astype(f32) + local).astype(bf16), "ctx", pairs)

    return lax.fori_loop(0, length - 1, step, jnp.zeros(local.shape, bf16))


def shards(
    tokens,
    lengths,
    cotangent,
    pre_gain,
    pre_bias,
    query_weight,
    key_weight,
    value_weight,
    swish_weight,
    out_weight,
    group_gain,
    group_bias,
    mlp_gain,
    mlp_bias,
    gelu_weight,
    up_weight,
    down_weight,
):
    seq_count, span, width = tokens.shape
    nf, nc, nt = lax.axis_size("fsdp"), lax.axis_size("ctx"), lax.axis_size("tp")
    f, c, t = lax.axis_index("fsdp"), lax.axis_index("ctx"), lax.axis_index("tp")
    block_rows = seq_count * span
    own_rows = block_rows // nt
    depth = query_weight.shape[0]
    heads_local = group_gain.shape[0]
    assert heads_local == nf
    key_size = query_weight.shape[1] // heads_local
    value_size = value_weight.shape[1] // heads_local
    hidden_size = gelu_weight.shape[1] // nf
    seqs = nf * seq_count
    rows = seqs * span
    head = t * heads_local + f

    def perm(v):
        return v.reshape(-1, nf, nc, depth).transpose(0, 2, 1, 3).reshape(-1, width)

    def unperm(v):
        return v.reshape(-1, nc, nf, depth).transpose(0, 2, 1, 3).reshape(-1, width)

    def own_part(v):
        return lax.dynamic_slice_in_dim(v.reshape(block_rows, width), t * own_rows, own_rows, 0)

    def spread(w):
        return w.reshape(depth, nf, -1).transpose(1, 0, 2)

    def full_weights(*ws):
        mine = jnp.concatenate([spread(w) for w in ws], -1)
        mine = lax.all_to_all(mine, "fsdp", 0, 0, tiled=True)
        return lax.all_gather(mine, "ctx", axis=0, tiled=True).reshape(width, -1)

    attn_w = full_weights(query_weight, key_weight, value_weight, swish_weight)
    rest_w = full_weights(out_weight.T, gelu_weight, up_weight, down_weight.T)
    out_t = rest_w[:, :value_size]
    gelu_up = rest_w[:, value_size : value_size + 2 * hidden_size]
    down_t = rest_w[:, value_size + 2 * hidden_size :]

    small = jnp.concatenate(
        [
            jnp.stack([pre_gain, pre_bias, mlp_gain, mlp_bias]).astype(f32).reshape(-1),
            group_gain.astype(f32).reshape(-1),
            group_bias.astype(f32).reshape(-1),
            lengths.astype(f32),
        ]
    )
    small = lax.all_gather(small, ("fsdp", "ctx"), axis=0)
    pre_gain_full, pre_bias_full, mlp_gain_full, mlp_bias_full = (
        small[:, i * depth : (i + 1) * depth].reshape(width) for i in range(4)
    )
    group = small[:, 4 * depth : 4 * depth + 2 * group_gain.size].reshape(
        nf * nc, 2, heads_local, -1
    )
    group = lax.dynamic_index_in_dim(group, f, 2, False).transpose(1, 0, 2).reshape(2, value_size)
    all_lengths = small.reshape(nf, nc, -1)[:, 0, -seq_count:].reshape(seqs)

    inputs = own_part(tokens).astype(f32)
    normed_wide, norm_in_back = jax.vjp(layer_norm, inputs, pre_gain_full, pre_bias_full)
    normed = gather_rows(perm(normed_wide.astype(bf16)))
    positions = c * span + lax.iota(jnp.int32, span)
    own_ids = t * own_rows + lax.iota(jnp.int32, own_rows)
    own_valid = (c * span + own_ids % span < lengths[own_ids // span]).astype(f32)[:, None]
    error = own_valid * own_part(cotangent).astype(f32)
    error_all = gather_rows(perm(error.astype(bf16)))

    pre = product(normed, attn_w)
    valid = (positions.astype(f32)[None, :] < all_lengths[:, None]).astype(f32)[:, :, None]
    cosine, sine = turn_tables(positions, key_size // 2)
    key_scale = key_size ** (-0.5)
    query_pre = pre[:, :key_size].reshape(seqs, span, key_size)
    key_pre = pre[:, key_size : 2 * key_size].reshape(seqs, span, key_size)
    value_pre = pre[:, 2 * key_size : 2 * key_size + value_size]
    swish_pre = pre[:, 2 * key_size + value_size :]
    queries = rotate(query_pre, cosine, sine).astype(bf16)
    keys = (rotate(key_pre, cosine, sine) * key_scale * valid).astype(bf16)
    values = value_pre.astype(bf16).reshape(seqs, span, value_size)

    log_decay = jnp.log1p(-jnp.exp2(-5.0 - head.astype(f32)))
    offsets = jnp.arange(span)
    distance = (offsets[:, None] - offsets[None, :]).astype(f32)
    within_fade = jnp.where(distance >= 0, jnp.exp(jnp.maximum(distance, 0.0) * log_decay), 0.0)
    key_fade = jnp.exp((span - 1 - offsets).astype(f32) * log_decay)[:, None]
    query_fade = jnp.exp((offsets + 1).astype(f32) * log_decay)[:, None]
    block_fade = jnp.exp(span * log_decay)

    keys_faded = (keys.astype(f32) * key_fade).astype(bf16)
    queries_faded = (queries.astype(f32) * query_fade).astype(bf16)
    local_state = blocks("sjd,sje->sde", keys_faded, values)
    entering = pass_states(local_state, block_fade, 1)
    probs = (blocks("sid,sjd->sij", queries, keys) * within_fade).astype(bf16)
    mixed = blocks("sij,sje->sie", probs, values) + blocks("sid,sde->sie", queries_faded, entering)
    gated_wide, gate_back = jax.vjp(
        gate_mix, mixed.reshape(rows, value_size), swish_pre, group[0], group[1]
    )
    gated = gated_wide.astype(bf16)
    branch = scatter_rows(product_right(gated, out_t).astype(bf16))
    hidden = inputs + unperm(branch.astype(f32))

    mlp_wide, norm_mid_back = jax.vjp(layer_norm, hidden, mlp_gain_full, mlp_bias_full)
    mlp_in = gather_rows(perm(mlp_wide.astype(bf16)))
    pre_ff = product(mlp_in, gelu_up)
    inner_wide, mix_back = jax.vjp(mlp_mix, pre_ff[:, :hidden_size], pre_ff[:, hidden_size:])
    inner = inner_wide.astype(bf16)
    mlp_out = scatter_rows(product_right(inner, down_t).astype(bf16))
    block_own = (own_valid * (hidden + unperm(mlp_out.astype(f32)))).astype(bf16)
    block_out = lax.all_gather(block_own, "tp", axis=0, tiled=True).reshape(tokens.shape)

    def to_owners(grads):
        mine = lax.psum_scatter(grads.astype(bf16), "ctx", scatter_dimension=0, tiled=True)
        return lax.all_to_all(mine.reshape(nf, depth, -1), "fsdp", 0, 0, tiled=True).astype(f32)

    def along(grads):
        return grads.transpose(1, 0, 2).reshape(depth, -1)

    def across(grads):
        return grads.transpose(0, 2, 1).reshape(-1, depth)

    grad_down_t = product_left(error_all, inner)
    gelu_grad, up_grad = mix_back(product(error_all, down_t))
    ff_low = jnp.concatenate([gelu_grad.astype(bf16), up_grad.astype(bf16)], -1)
    grad_gelu_up = product_left(mlp_in, ff_low)
    ff_grads = to_owners(jnp.concatenate([grad_gelu_up, grad_down_t], -1))
    mlp_in_grad = unperm(scatter_rows(product_right(ff_low, gelu_up).astype(bf16)).astype(f32))
    hidden_norm_grad, grad_mlp_gain, grad_mlp_bias = norm_mid_back(mlp_in_grad)
    hidden_grad = error + hidden_norm_grad

    hidden_low = gather_rows(perm(hidden_grad.astype(bf16)))
    grad_out_t = product_left(hidden_low, gated)
    gated_grad = product(hidden_low, out_t)
    mixed_grad, swish_grad, grad_group_gain, grad_group_bias = gate_back(gated_grad)
    swish_low = swish_grad.astype(bf16)
    mixed_low = mixed_grad.astype(bf16).reshape(seqs, span, value_size)
    score_low = (blocks("sie,sje->sij", mixed_low, values) * within_fade).astype(bf16)
    pulled_state = blocks("sid,sie->sde", queries_faded, mixed_low)
    later = pass_states(pulled_state, block_fade, -1)
    query_grad = blocks("sij,sjd->sid", score_low, keys) + query_fade * blocks(
        "sie,sde->sid", mixed_low, entering
    )
    key_grad = blocks("sij,sid->sjd", score_low, queries) + key_fade * blocks(
        "sje,sde->sjd", values, later
    )
    value_grad = blocks("sij,sie->sje", probs, mixed_low) + blocks(
        "sjd,sde->sje", keys_faded, later
    )
    query_low = rotate_back(query_grad, cosine, sine).astype(bf16).reshape(rows, key_size)
    key_low = rotate_back(key_grad * key_scale * valid, cosine, sine).astype(bf16)
    low = jnp.concatenate(
        [
            query_low,
            key_low.reshape(rows, key_size),
            value_grad.astype(bf16).reshape(rows, value_size),
            swish_low,
        ],
        -1,
    )
    grad_attn = product_left(normed, low)
    attn_grads = to_owners(jnp.concatenate([grad_attn, grad_out_t], -1))
    normed_grad = unperm(scatter_rows(product_right(low, attn_w).astype(bf16)).astype(f32))
    input_norm_grad, grad_pre_gain, grad_pre_bias = norm_in_back(normed_grad)
    tokens_own = (hidden_grad + input_norm_grad).astype(bf16)
    grad_tokens = lax.all_gather(tokens_own, "tp", axis=0, tiled=True).reshape(tokens.shape)

    mine = (lax.iota(jnp.int32, nt * heads_local) == head).astype(f32)[:, None]
    sums = jnp.concatenate(
        [
            grad_pre_gain,
            grad_pre_bias,
            grad_mlp_gain,
            grad_mlp_bias,
            (mine * grad_group_gain[None]).reshape(-1),
            (mine * grad_group_bias[None]).reshape(-1),
        ]
    )
    sums = lax.psum(sums, ("fsdp", "ctx", "tp"))
    place = f * nc + c
    norm_sums = lax.dynamic_index_in_dim(
        sums[: 4 * width].reshape(4, nf * nc, depth), place, 1, False
    )
    group_sums = sums[4 * width :].reshape(2, nt, heads_local, nf * nc, -1)
    group_sums = lax.dynamic_index_in_dim(group_sums, t, 1, False)
    group_sums = lax.dynamic_index_in_dim(group_sums, place, 2, False)

    at = [0, key_size, 2 * key_size, 2 * key_size + value_size, 2 * key_size + 2 * value_size]
    return (
        block_out,
        grad_tokens,
        norm_sums[0],
        norm_sums[1],
        along(attn_grads[..., : at[1]]),
        along(attn_grads[..., at[1] : at[2]]),
        along(attn_grads[..., at[2] : at[3]]),
        along(attn_grads[..., at[3] : at[4]]),
        across(attn_grads[..., at[4] :]),
        group_sums[0],
        group_sums[1],
        norm_sums[2],
        norm_sums[3],
        along(ff_grads[..., :hidden_size]),
        along(ff_grads[..., hidden_size : 2 * hidden_size]),
        across(ff_grads[..., 2 * hidden_size :]),
    )


def solution(mesh):
    rows = P("fsdp", "ctx", None)
    vector = P(("fsdp", "ctx"))
    tall = P(("fsdp", "ctx"), "tp")
    wide = P("tp", ("fsdp", "ctx"))
    in_specs = (rows, P("fsdp"), rows, vector, vector, tall, tall, tall, tall, wide)
    in_specs += (wide, wide, vector, vector, tall, tall, wide)
    out_specs = (rows, rows, vector, vector, tall, tall, tall, tall, wide)
    out_specs += (wide, wide, vector, vector, tall, tall, wide)
    return jax.shard_map(shards, mesh=mesh, in_specs=in_specs, out_specs=out_specs, check_vma=False)
```

```python
import functools

import jax
import jax.numpy as jnp
from jax import lax
from jax.experimental import pallas as pl
from jax.experimental.pallas import tpu as pltpu
from jax.sharding import PartitionSpec as P

eps = 1e-05
group_floor = 1.0
f32 = jnp.float32
bf16 = jnp.bfloat16


def layer_norm(values, norm_gain, norm_shift):
    centred = values - jnp.mean(values, -1, keepdims=True)
    spread = jnp.mean(centred * centred, -1, keepdims=True)
    return centred * lax.rsqrt(spread + eps) * norm_gain + norm_shift


def turn_tables(positions, half_size):
    frequency = jnp.power(10000.0, -jnp.arange(half_size).astype(f32) / half_size)
    angles = positions.astype(f32)[:, None] * frequency[None, :]
    return jnp.cos(angles), jnp.sin(angles)


def rotate(values, cosine, sine):
    half_size = values.shape[-1] // 2
    first = values[..., :half_size]
    second = values[..., half_size:]
    return jnp.concatenate([first * cosine - second * sine, second * cosine + first * sine], -1)


def rotate_back(values, cosine, sine):
    return rotate(values, cosine, -sine)


def gate_mix(mixed, swish_pre, norm_gain, norm_shift):
    centred = mixed - jnp.mean(mixed, -1, keepdims=True)
    spread = jnp.mean(centred * centred, -1, keepdims=True)
    return jax.nn.silu(swish_pre) * (
        centred * lax.rsqrt(spread + group_floor) * norm_gain + norm_shift
    )


def mlp_mix(gelu_pre, up_pre):
    return jax.nn.gelu(gelu_pre) * up_pre


def product(left, right):
    return jnp.dot(left, right, preferred_element_type=f32)


def product_left(left, right):
    return lax.dot_general(left, right, (((0,), (0,)), ((), ())), preferred_element_type=f32)


def product_right(left, right):
    return lax.dot_general(left, right, (((1,), (1,)), ((), ())), preferred_element_type=f32)


def blocks(spec, left, right):
    return jnp.einsum(spec, left, right, preferred_element_type=f32)


MESH = pl.DeviceIdType.MESH


def beside(f):
    return f + 1 - 2 * (f % 2), (f + 2) % 4, 3 - f


def greet(devices):
    barrier = pltpu.get_barrier_semaphore()
    for device in devices:
        pl.semaphore_signal(barrier, inc=1, device_id=device, device_id_type=MESH)
    pl.semaphore_wait(barrier, len(devices))


def remote(src, dst, send, recv, device):
    return pltpu.make_async_remote_copy(
        src_ref=src, dst_ref=dst, send_sem=send, recv_sem=recv, device_id=device, device_id_type=MESH
    )


def gather_kernel(own, out, keep, send, recv):
    f, t = lax.axis_index("fsdp"), lax.axis_index("tp")
    fx, fy, fd = beside(f)
    x, y, core = {"fsdp": fx}, {"fsdp": fy}, {"tp": 1 - t}
    greet([x, y, core])
    half = own.shape[0] // 2

    def part(ref, h):
        return ref.at[pl.ds(h * half, half)]

    def slot(who, h):
        return part(out.at[2 * who + t], h)

    local = pltpu.make_async_copy(own, out.at[2 * f + t], keep)
    local.start()
    first = [
        remote(part(own, 0), slot(f, 0), send.at[0], recv.at[0], x),
        remote(part(own, 1), slot(f, 1), send.at[1], recv.at[3], y),
        remote(part(own, 1), slot(f, 1), send.at[2], recv.at[1], x),
        remote(part(own, 0), slot(f, 0), send.at[3], recv.at[2], y),
        remote(part(own, 0), slot(f, 0), send.at[4], recv.at[6], core),
        remote(part(own, 1), slot(f, 1), send.at[5], recv.at[7], core),
    ]
    for copy in first:
        copy.start()

    def pass_on(who, h, s, r, device):
        return remote(slot(who, h), slot(who, h), send.at[s], recv.at[r], device)

    sent = list(first)

    def go(copy):
        copy.start()
        sent.append(copy)

    first[0].wait_recv()
    go(pass_on(fx, 0, 6, 4, y))
    go(pass_on(fx, 0, 7, 8, core))
    first[1].wait_recv()
    go(pass_on(fy, 1, 8, 5, x))
    go(pass_on(fy, 1, 9, 11, core))
    first[2].wait_recv()
    go(pass_on(fx, 1, 10, 9, core))
    first[3].wait_recv()
    go(pass_on(fy, 0, 11, 10, core))
    remote(slot(fd, 0), slot(fd, 0), send.at[12], recv.at[4], y).wait_recv()
    go(pass_on(fd, 0, 12, 12, core))
    remote(slot(fd, 1), slot(fd, 1), send.at[13], recv.at[5], x).wait_recv()
    go(pass_on(fd, 1, 13, 13, core))
    for r in range(6, 14):
        remote(slot(f, 0), slot(f, 0), send.at[0], recv.at[r], core).wait_recv()
    for copy in sent:
        copy.wait_send()
    local.wait()


def gather_rows(own, collective_id):
    rows, width = own.shape
    out = pl.pallas_call(
        gather_kernel,
        out_shape=jax.ShapeDtypeStruct((8, rows, width), own.dtype),
        in_specs=[pl.BlockSpec(memory_space=pl.ANY)],
        out_specs=pl.BlockSpec(memory_space=pl.ANY),
        scratch_shapes=[
            pltpu.SemaphoreType.DMA,
            pltpu.SemaphoreType.DMA((14,)),
            pltpu.SemaphoreType.DMA((14,)),
        ],
        compiler_params=pltpu.CompilerParams(collective_id=collective_id, has_side_effects=True),
        cost_estimate=pl.CostEstimate(flops=0, bytes_accessed=160_000_000, transcendentals=0),
    )(own)
    return out.reshape(8 * rows, width)


def scatter_kernel(partial, out, mine, theirs, total, diag, last, keep, send, recv):
    f, t = lax.axis_index("fsdp"), lax.axis_index("tp")
    fx, fy, fd = beside(f)
    x, y, core = {"fsdp": fx}, {"fsdp": fy}, {"tp": 1 - t}
    greet([x, y, core])
    half = out.shape[0] // 2
    order = [fd, fy, fx, f]
    kept, crossing = [], []
    for i, who in enumerate(order):
        crossing.append(
            remote(partial.at[2 * who + 1 - t], theirs.at[i], send.at[i], recv.at[i], core)
        )
        kept.append(pltpu.make_async_copy(partial.at[2 * who + t], mine.at[i], keep.at[i]))
        crossing[i].start()
        kept[i].start()

    def part(ref, h):
        return ref.at[pl.ds(h * half, half)]

    def add(i):
        kept[i].wait()
        crossing[i].wait_recv()
        total[i] = (mine[i].astype(f32) + theirs[i].astype(f32)).astype(total.dtype)

    add(0)
    d0 = remote(part(total.at[0], 0), diag.at[0], send.at[4], recv.at[4], x)
    d1 = remote(part(total.at[0], 1), diag.at[1], send.at[5], recv.at[5], y)
    d0.start()
    d1.start()
    add(1)
    y1 = remote(part(total.at[1], 1), part(last.at[1], 1), send.at[6], recv.at[6], y)
    y1.start()
    add(2)
    x0 = remote(part(total.at[2], 0), part(last.at[0], 0), send.at[7], recv.at[7], x)
    x0.start()
    d0.wait_recv()
    total[1, :half] = (total[1, :half].astype(f32) + diag[0].astype(f32)).astype(total.dtype)
    y0 = remote(part(total.at[1], 0), part(last.at[1], 0), send.at[8], recv.at[8], y)
    y0.start()
    d1.wait_recv()
    total[2, half:] = (total[2, half:].astype(f32) + diag[1].astype(f32)).astype(total.dtype)
    x1 = remote(part(total.at[2], 1), part(last.at[0], 1), send.at[9], recv.at[9], x)
    x1.start()
    kept[3].wait()
    crossing[3].wait_recv()
    for copy in (y1, x0, y0, x1):
        copy.wait_recv()
    out[...] = (mine[3].astype(f32) + theirs[3].astype(f32)) + (
        last[0].astype(f32) + last[1].astype(f32)
    )
    for copy in (*crossing, d0, d1, y1, x0, y0, x1):
        copy.wait_send()


def scatter_rows(partial, collective_id):
    rows, width = partial.shape[0] // 8, partial.shape[1]
    dt = partial.dtype
    return pl.pallas_call(
        scatter_kernel,
        out_shape=jax.ShapeDtypeStruct((rows, width), f32),
        in_specs=[pl.BlockSpec(memory_space=pl.ANY)],
        out_specs=pl.BlockSpec(memory_space=pltpu.VMEM),
        scratch_shapes=[
            pltpu.VMEM((4, rows, width), dt),
            pltpu.VMEM((4, rows, width), dt),
            pltpu.VMEM((3, rows, width), dt),
            pltpu.VMEM((2, rows // 2, width), dt),
            pltpu.VMEM((2, rows, width), dt),
            pltpu.SemaphoreType.DMA((4,)),
            pltpu.SemaphoreType.DMA((10,)),
            pltpu.SemaphoreType.DMA((10,)),
        ],
        compiler_params=pltpu.CompilerParams(
            collective_id=collective_id, has_side_effects=True, vmem_limit_bytes=40 << 20
        ),
        cost_estimate=pl.CostEstimate(flops=0, bytes_accessed=160_000_000, transcendentals=0),
    )(partial.reshape(8, rows, width))


def pass_kernel(by, local, fade, out, held, send, recv):
    length = lax.axis_size("ctx")
    c = lax.axis_index("ctx")
    pieces = local.shape[0]
    first = c == (0 if by > 0 else length - 1)
    last = c == (length - 1 if by > 0 else 0)
    target = lax.rem(c + by + length, length)
    source = lax.rem(c - by + length, length)
    barrier = pltpu.get_barrier_semaphore()

    @pl.when(jnp.logical_not(first))
    def _():
        pl.semaphore_signal(barrier, inc=1, device_id={"ctx": source}, device_id_type=MESH)

    @pl.when(jnp.logical_not(last))
    def _():
        pl.semaphore_wait(barrier, 1)

    def copy(p):
        return remote(held.at[p], out.at[p], send.at[p], recv.at[p], {"ctx": target})

    def step(p, carry):
        @pl.when(first)
        def _():
            out[p] = jnp.zeros(out.shape[1:], out.dtype)

        @pl.when(jnp.logical_not(first))
        def _():
            copy(p).wait_recv()

        @pl.when(jnp.logical_not(last))
        def _():
            held[p] = (fade[...] * out[p].astype(f32) + local[p]).astype(held.dtype)
            copy(p).start()

        return carry

    lax.fori_loop(0, pieces, step, 0)

    @pl.when(jnp.logical_not(last))
    def _():
        def done(p, carry):
            copy(p).wait_send()
            return carry

        lax.fori_loop(0, pieces, done, 0)


def pass_states(local, fade, by, collective_id):
    pieces = local.shape[0]
    return pl.pallas_call(
        functools.partial(pass_kernel, by),
        out_shape=jax.ShapeDtypeStruct(local.shape, bf16),
        in_specs=[pl.BlockSpec(memory_space=pltpu.VMEM)] * 2,
        out_specs=pl.BlockSpec(memory_space=pltpu.VMEM),
        scratch_shapes=[
            pltpu.VMEM(local.shape, bf16),
            pltpu.SemaphoreType.DMA((pieces,)),
            pltpu.SemaphoreType.DMA((pieces,)),
        ],
        compiler_params=pltpu.CompilerParams(
            collective_id=collective_id, has_side_effects=True, vmem_limit_bytes=40 << 20
        ),
        cost_estimate=pl.CostEstimate(flops=0, bytes_accessed=200_000_000, transcendentals=0),
    )(local, jnp.full((1, local.shape[2]), fade, f32))

def peer_of(place, nc, nt):
    return {"fsdp": place // (nc * nt), "ctx": place // nt % nc, "tp": place % nt}


def spread_kernel(own, out, keep, send, recv):
    nc = lax.axis_size("ctx")
    count = out.shape[0]
    t = lax.axis_index("tp")
    place = lax.axis_index("fsdp") * nc + lax.axis_index("ctx")
    barrier = pltpu.get_barrier_semaphore()

    def peer(i):
        other = lax.rem(place + i, count)
        return {"fsdp": other // nc, "ctx": other % nc}

    def hello(i, carry):
        pl.semaphore_signal(barrier, inc=1, device_id=peer(i), device_id_type=MESH)
        return carry

    lax.fori_loop(1, count, hello, 0)
    pl.semaphore_wait(barrier, count - 1)

    def copy(i):
        return remote(own, out.at[place], send.at[i], recv.at[i], peer(i))

    def go(i, carry):
        copy(i).start()
        return carry

    lax.fori_loop(1, count, go, 0)
    local = pltpu.make_async_copy(own, out.at[place], keep)
    local.start()
    local.wait()

    def done(i, carry):
        copy(i).wait()
        return carry

    lax.fori_loop(1, count, done, 0)


def spread_small(own, collective_id):
    count = lax.axis_size("fsdp") * lax.axis_size("ctx")
    return pl.pallas_call(
        spread_kernel,
        out_shape=jax.ShapeDtypeStruct((count, *own.shape), own.dtype),
        in_specs=[pl.BlockSpec(memory_space=pltpu.VMEM)],
        out_specs=pl.BlockSpec(memory_space=pltpu.VMEM),
        scratch_shapes=[
            pltpu.SemaphoreType.DMA,
            pltpu.SemaphoreType.DMA((count,)),
            pltpu.SemaphoreType.DMA((count,)),
        ],
        compiler_params=pltpu.CompilerParams(collective_id=collective_id, has_side_effects=True),
        cost_estimate=pl.CostEstimate(flops=0, bytes_accessed=30_000_000, transcendentals=0),
    )(own)


def total_kernel(parts, out, slots, send, recv):
    nc, nt = lax.axis_size("ctx"), lax.axis_size("tp")
    count = parts.shape[0]
    place = (lax.axis_index("fsdp") * nc + lax.axis_index("ctx")) * nt + lax.axis_index("tp")
    barrier = pltpu.get_barrier_semaphore()

    def hello(i, carry):
        other = peer_of(lax.rem(place + i, count), nc, nt)
        pl.semaphore_signal(barrier, inc=1, device_id=other, device_id_type=MESH)
        return carry

    lax.fori_loop(1, count, hello, 0)
    pl.semaphore_wait(barrier, count - 1)

    def copy(i):
        other = lax.rem(place + i, count)
        return remote(
            parts.at[other], slots.at[i], send.at[i], recv.at[i], peer_of(other, nc, nt)
        )

    def go(i, carry):
        copy(i).start()
        return carry

    lax.fori_loop(1, count, go, 0)

    def add(i, carry):
        copy(i).wait()
        return carry + slots[i]

    out[...] = lax.fori_loop(1, count, add, parts[place])


def total_small(parts, collective_id):
    count = parts.shape[0]
    return pl.pallas_call(
        total_kernel,
        out_shape=jax.ShapeDtypeStruct(parts.shape[1:], parts.dtype),
        in_specs=[pl.BlockSpec(memory_space=pltpu.VMEM)],
        out_specs=pl.BlockSpec(memory_space=pltpu.VMEM),
        scratch_shapes=[
            pltpu.VMEM(parts.shape, parts.dtype),
            pltpu.SemaphoreType.DMA((count,)),
            pltpu.SemaphoreType.DMA((count,)),
        ],
        compiler_params=pltpu.CompilerParams(collective_id=collective_id, has_side_effects=True),
        cost_estimate=pl.CostEstimate(flops=0, bytes_accessed=30_000_000, transcendentals=0),
    )(parts)


def both_halves(own, t):
    other = lax.ppermute(own, "tp", [(0, 1), (1, 0)])
    return jnp.where(t == 0, jnp.concatenate([own, other]), jnp.concatenate([other, own]))


def shards(
    tokens,
    lengths,
    cotangent,
    pre_gain,
    pre_bias,
    query_weight,
    key_weight,
    value_weight,
    swish_weight,
    out_weight,
    group_gain,
    group_bias,
    mlp_gain,
    mlp_bias,
    gelu_weight,
    up_weight,
    down_weight,
):
    seq_count, span, width = tokens.shape
    nf, nc, nt = lax.axis_size("fsdp"), lax.axis_size("ctx"), lax.axis_size("tp")
    f, c, t = lax.axis_index("fsdp"), lax.axis_index("ctx"), lax.axis_index("tp")
    block_rows = seq_count * span
    own_rows = block_rows // nt
    depth = query_weight.shape[0]
    heads_local = group_gain.shape[0]
    assert heads_local == nf
    key_size = query_weight.shape[1] // heads_local
    value_size = value_weight.shape[1] // heads_local
    hidden_size = gelu_weight.shape[1] // nf
    seqs = nf * seq_count
    rows = seqs * span
    head = t * heads_local + f

    def pad_tile(v):
        return jnp.pad(v, [(0, 0)] * (v.ndim - 1) + [(0, -v.shape[-1] % 1024)]).reshape(
            *v.shape[:-1], 8, -1
        )

    def perm(v):
        return v.reshape(-1, nf, nc, depth).transpose(0, 2, 1, 3).reshape(-1, width)

    def unperm(v):
        return v.reshape(-1, nc, nf, depth).transpose(0, 2, 1, 3).reshape(-1, width)

    def own_part(v):
        return lax.dynamic_slice_in_dim(v.reshape(block_rows, width), t * own_rows, own_rows, 0)

    def spread(w):
        return w.reshape(depth, nf, -1).transpose(1, 0, 2)

    def full_weights(*ws):
        mine = jnp.concatenate([spread(w) for w in ws], -1)
        mine = lax.all_to_all(mine, "fsdp", 0, 0, tiled=True)
        return lax.all_gather(mine, "ctx", axis=0, tiled=True).reshape(width, -1)

    attn_w = full_weights(query_weight, key_weight, value_weight, swish_weight)
    rest_w = full_weights(out_weight.T, gelu_weight, up_weight, down_weight.T)
    out_t = rest_w[:, :value_size]
    gelu_up = rest_w[:, value_size : value_size + 2 * hidden_size]
    down_t = rest_w[:, value_size + 2 * hidden_size :]

    small = jnp.concatenate(
        [
            jnp.stack([pre_gain, pre_bias, mlp_gain, mlp_bias]).astype(f32).reshape(-1),
            group_gain.astype(f32).reshape(-1),
            group_bias.astype(f32).reshape(-1),
            lengths.astype(f32),
        ]
    )
    small_size = small.size
    small = spread_small(pad_tile(small), 4).reshape(nf * nc, -1)[:, :small_size]
    pre_gain_full, pre_bias_full, mlp_gain_full, mlp_bias_full = (
        small[:, i * depth : (i + 1) * depth].reshape(width) for i in range(4)
    )
    group = small[:, 4 * depth : 4 * depth + 2 * group_gain.size].reshape(
        nf * nc, 2, heads_local, -1
    )
    group = lax.dynamic_index_in_dim(group, f, 2, False).transpose(1, 0, 2).reshape(2, value_size)
    all_lengths = small.reshape(nf, nc, -1)[:, 0, -seq_count:].reshape(seqs)

    inputs = own_part(tokens).astype(f32)
    normed_wide, norm_in_back = jax.vjp(layer_norm, inputs, pre_gain_full, pre_bias_full)
    normed = gather_rows(perm(normed_wide.astype(bf16)), 0)
    positions = c * span + lax.iota(jnp.int32, span)
    own_ids = t * own_rows + lax.iota(jnp.int32, own_rows)
    own_valid = (c * span + own_ids % span < lengths[own_ids // span]).astype(f32)[:, None]
    error = own_valid * own_part(cotangent).astype(f32)
    error_all = gather_rows(perm(error.astype(bf16)), 0)

    pre = product(normed, attn_w)
    valid = (positions.astype(f32)[None, :] < all_lengths[:, None]).astype(f32)[:, :, None]
    cosine, sine = turn_tables(positions, key_size // 2)
    key_scale = key_size ** (-0.5)
    query_pre = pre[:, :key_size].reshape(seqs, span, key_size)
    key_pre = pre[:, key_size : 2 * key_size].reshape(seqs, span, key_size)
    value_pre = pre[:, 2 * key_size : 2 * key_size + value_size]
    swish_pre = pre[:, 2 * key_size + value_size :]
    queries = rotate(query_pre, cosine, sine).astype(bf16)
    keys = (rotate(key_pre, cosine, sine) * key_scale * valid).astype(bf16)
    values = value_pre.astype(bf16).reshape(seqs, span, value_size)

    log_decay = jnp.log1p(-jnp.exp2(-5.0 - head.astype(f32)))
    offsets = jnp.arange(span)
    distance = (offsets[:, None] - offsets[None, :]).astype(f32)
    within_fade = jnp.where(distance >= 0, jnp.exp(jnp.maximum(distance, 0.0) * log_decay), 0.0)
    key_fade = jnp.exp((span - 1 - offsets).astype(f32) * log_decay)[:, None]
    query_fade = jnp.exp((offsets + 1).astype(f32) * log_decay)[:, None]
    block_fade = jnp.exp(span * log_decay)

    keys_faded = (keys.astype(f32) * key_fade).astype(bf16)
    queries_faded = (queries.astype(f32) * query_fade).astype(bf16)
    local_state = blocks("sjd,sje->sde", keys_faded, values)
    entering = pass_states(local_state, block_fade, 1, 2)
    probs = (blocks("sid,sjd->sij", queries, keys) * within_fade).astype(bf16)
    mixed = blocks("sij,sje->sie", probs, values) + blocks("sid,sde->sie", queries_faded, entering)
    gated_wide, gate_back = jax.vjp(
        gate_mix, mixed.reshape(rows, value_size), swish_pre, group[0], group[1]
    )
    gated = gated_wide.astype(bf16)
    branch = scatter_rows(product_right(gated, out_t).astype(bf16), 1)
    hidden = inputs + unperm(branch)

    mlp_wide, norm_mid_back = jax.vjp(layer_norm, hidden, mlp_gain_full, mlp_bias_full)
    mlp_in = gather_rows(perm(mlp_wide.astype(bf16)), 0)
    pre_ff = product(mlp_in, gelu_up)
    inner_wide, mix_back = jax.vjp(mlp_mix, pre_ff[:, :hidden_size], pre_ff[:, hidden_size:])
    inner = inner_wide.astype(bf16)
    mlp_out = scatter_rows(product_right(inner, down_t).astype(bf16), 1)
    block_own = (own_valid * (hidden + unperm(mlp_out))).astype(bf16)
    block_out = both_halves(block_own, t).reshape(tokens.shape)

    def to_owners(grads):
        mine = lax.psum_scatter(grads.astype(bf16), "ctx", scatter_dimension=0, tiled=True)
        return lax.all_to_all(mine.reshape(nf, depth, -1), "fsdp", 0, 0, tiled=True).astype(f32)

    def along(grads):
        return grads.transpose(1, 0, 2).reshape(depth, -1)

    def across(grads):
        return grads.transpose(0, 2, 1).reshape(-1, depth)

    grad_down_t = product_left(error_all, inner)
    gelu_grad, up_grad = mix_back(product(error_all, down_t))
    ff_low = jnp.concatenate([gelu_grad.astype(bf16), up_grad.astype(bf16)], -1)
    grad_gelu_up = product_left(mlp_in, ff_low)
    ff_grads = to_owners(jnp.concatenate([grad_gelu_up, grad_down_t], -1))
    mlp_in_grad = unperm(scatter_rows(product_right(ff_low, gelu_up).astype(bf16), 1))
    hidden_norm_grad, grad_mlp_gain, grad_mlp_bias = norm_mid_back(mlp_in_grad)
    hidden_grad = error + hidden_norm_grad

    hidden_low = gather_rows(perm(hidden_grad.astype(bf16)), 0)
    grad_out_t = product_left(hidden_low, gated)
    gated_grad = product(hidden_low, out_t)
    mixed_grad, swish_grad, grad_group_gain, grad_group_bias = gate_back(gated_grad)
    swish_low = swish_grad.astype(bf16)
    mixed_low = mixed_grad.astype(bf16).reshape(seqs, span, value_size)
    score_low = (blocks("sie,sje->sij", mixed_low, values) * within_fade).astype(bf16)
    pulled_state = blocks("sid,sie->sde", queries_faded, mixed_low)
    later = pass_states(pulled_state, block_fade, -1, 3)
    query_grad = blocks("sij,sjd->sid", score_low, keys) + query_fade * blocks(
        "sie,sde->sid", mixed_low, entering
    )
    key_grad = blocks("sij,sid->sjd", score_low, queries) + key_fade * blocks(
        "sje,sde->sjd", values, later
    )
    value_grad = blocks("sij,sie->sje", probs, mixed_low) + blocks(
        "sjd,sde->sje", keys_faded, later
    )
    query_low = rotate_back(query_grad, cosine, sine).astype(bf16).reshape(rows, key_size)
    key_low = rotate_back(key_grad * key_scale * valid, cosine, sine).astype(bf16)
    low = jnp.concatenate(
        [
            query_low,
            key_low.reshape(rows, key_size),
            value_grad.astype(bf16).reshape(rows, value_size),
            swish_low,
        ],
        -1,
    )
    grad_attn = product_left(normed, low)
    attn_grads = to_owners(jnp.concatenate([grad_attn, grad_out_t], -1))
    normed_grad = unperm(scatter_rows(product_right(low, attn_w).astype(bf16), 1))
    input_norm_grad, grad_pre_gain, grad_pre_bias = norm_in_back(normed_grad)
    tokens_own = (hidden_grad + input_norm_grad).astype(bf16)
    grad_tokens = both_halves(tokens_own, t).reshape(tokens.shape)

    norm_parts = jnp.stack([grad_pre_gain, grad_pre_bias, grad_mlp_gain, grad_mlp_bias])
    norm_parts = norm_parts.reshape(4, nf * nc, 1, depth).transpose(1, 2, 0, 3)
    norm_parts = jnp.broadcast_to(norm_parts, (nf * nc, nt, 4, depth)).reshape(nf * nc, nt, -1)
    mine = lax.iota(jnp.int32, nt * heads_local) == head
    group_parts = jnp.stack([grad_group_gain, grad_group_bias]).reshape(1, 2, nf * nc, -1)
    group_parts = jnp.where(mine[:, None, None, None], group_parts, 0.0)
    group_parts = group_parts.reshape(nt, heads_local, 2, nf * nc, -1).transpose(3, 0, 2, 1, 4)
    parts = jnp.concatenate([norm_parts, group_parts.reshape(nf * nc, nt, -1)], -1)
    parts = parts.reshape(nf * nc * nt, -1)
    sums = total_small(pad_tile(parts), 5).reshape(-1)[: parts.shape[1]]
    norm_sums = sums[: 4 * depth].reshape(4, depth)
    group_sums = sums[4 * depth :].reshape(2, heads_local, -1)

    at = [0, key_size, 2 * key_size, 2 * key_size + value_size, 2 * key_size + 2 * value_size]
    return (
        block_out,
        grad_tokens,
        norm_sums[0],
        norm_sums[1],
        along(attn_grads[..., : at[1]]),
        along(attn_grads[..., at[1] : at[2]]),
        along(attn_grads[..., at[2] : at[3]]),
        along(attn_grads[..., at[3] : at[4]]),
        across(attn_grads[..., at[4] :]),
        group_sums[0],
        group_sums[1],
        norm_sums[2],
        norm_sums[3],
        along(ff_grads[..., :hidden_size]),
        along(ff_grads[..., hidden_size : 2 * hidden_size]),
        across(ff_grads[..., 2 * hidden_size :]),
    )


def solution(mesh):
    rows = P("fsdp", "ctx", None)
    vector = P(("fsdp", "ctx"))
    tall = P(("fsdp", "ctx"), "tp")
    wide = P("tp", ("fsdp", "ctx"))
    in_specs = (rows, P("fsdp"), rows, vector, vector, tall, tall, tall, tall, wide)
    in_specs += (wide, wide, vector, vector, tall, tall, wide)
    out_specs = (rows, rows, vector, vector, tall, tall, tall, tall, wide)
    out_specs += (wide, wide, vector, vector, tall, tall, wide)
    return jax.shard_map(shards, mesh=mesh, in_specs=in_specs, out_specs=out_specs, check_vma=False)
```

```python
import functools

import jax
import jax.numpy as jnp
from jax import lax
from jax.experimental import pallas as pl
from jax.experimental.layout import Layout, with_layout_constraint
from jax.experimental.pallas import tpu as pltpu
from jax.sharding import PartitionSpec as P

eps = 1e-05
group_floor = 1.0
f32 = jnp.float32
bf16 = jnp.bfloat16


def layer_norm(values, norm_gain, norm_shift):
    centred = values - jnp.mean(values, -1, keepdims=True)
    spread = jnp.mean(centred * centred, -1, keepdims=True)
    return centred * lax.rsqrt(spread + eps) * norm_gain + norm_shift


def turn_tables(positions, half_size):
    frequency = jnp.power(10000.0, -jnp.arange(half_size).astype(f32) / half_size)
    angles = positions.astype(f32)[:, None] * frequency[None, :]
    return jnp.cos(angles), jnp.sin(angles)


def rotate(values, cosine, sine):
    half_size = values.shape[-1] // 2
    first = values[..., :half_size]
    second = values[..., half_size:]
    return jnp.concatenate([first * cosine - second * sine, second * cosine + first * sine], -1)


def rotate_back(values, cosine, sine):
    return rotate(values, cosine, -sine)


def gate_mix(mixed, swish_pre, norm_gain, norm_shift):
    centred = mixed - jnp.mean(mixed, -1, keepdims=True)
    spread = jnp.mean(centred * centred, -1, keepdims=True)
    return jax.nn.silu(swish_pre) * (
        centred * lax.rsqrt(spread + group_floor) * norm_gain + norm_shift
    )


def mlp_mix(gelu_pre, up_pre):
    return jax.nn.gelu(gelu_pre) * up_pre


def product(left, right):
    return jnp.dot(left, right, preferred_element_type=f32)


def product_left(left, right):
    return lax.dot_general(left, right, (((0,), (0,)), ((), ())), preferred_element_type=f32)


def product_right(left, right):
    return lax.dot_general(left, right, (((1,), (1,)), ((), ())), preferred_element_type=f32)


def blocks(spec, left, right):
    return jnp.einsum(spec, left, right, preferred_element_type=f32)


MESH = pl.DeviceIdType.MESH


def beside(f):
    return f + 1 - 2 * (f % 2), (f + 2) % 4, 3 - f


def remote(src, dst, send, recv, device):
    return pltpu.make_async_remote_copy(
        src_ref=src, dst_ref=dst, send_sem=send, recv_sem=recv, device_id=device, device_id_type=MESH
    )


def gather_steps(own, out, keep, send, recv):
    f, t = lax.axis_index("fsdp"), lax.axis_index("tp")
    fx, fy, fd = beside(f)
    x, y, core = {"fsdp": fx}, {"fsdp": fy}, {"tp": 1 - t}
    half = own.shape[0] // 2

    def part(ref, h):
        return ref.at[pl.ds(h * half, half)]

    def slot(who, h):
        return part(out.at[2 * who + t], h)

    local = pltpu.make_async_copy(own, out.at[2 * f + t], keep)
    first = [
        remote(part(own, 0), slot(f, 0), send.at[0], recv.at[0], x),
        remote(part(own, 1), slot(f, 1), send.at[1], recv.at[3], y),
        remote(part(own, 1), slot(f, 1), send.at[2], recv.at[1], x),
        remote(part(own, 0), slot(f, 0), send.at[3], recv.at[2], y),
        remote(part(own, 0), slot(f, 0), send.at[4], recv.at[6], core),
        remote(part(own, 1), slot(f, 1), send.at[5], recv.at[7], core),
    ]
    sent = list(first)

    def pass_on(who, h, s, r, device):
        copy = remote(slot(who, h), slot(who, h), send.at[s], recv.at[r], device)
        copy.start()
        sent.append(copy)

    def begin():
        local.start()
        for copy in first:
            copy.start()

    def relay():
        first[0].wait_recv()
        pass_on(fx, 0, 6, 4, y)
        pass_on(fx, 0, 7, 8, core)
        first[1].wait_recv()
        pass_on(fy, 1, 8, 5, x)
        pass_on(fy, 1, 9, 11, core)

    def rest():
        first[2].wait_recv()
        pass_on(fx, 1, 10, 9, core)
        first[3].wait_recv()
        pass_on(fy, 0, 11, 10, core)

    def diagonal():
        remote(slot(fd, 0), slot(fd, 0), send.at[12], recv.at[4], y).wait_recv()
        pass_on(fd, 0, 12, 12, core)
        remote(slot(fd, 1), slot(fd, 1), send.at[13], recv.at[5], x).wait_recv()
        pass_on(fd, 1, 13, 13, core)

    def end():
        for r in range(6, 14):
            remote(slot(f, 0), slot(f, 0), send.at[0], recv.at[r], core).wait_recv()
        for copy in sent:
            copy.wait_send()
        local.wait()

    return begin, relay, rest, diagonal, end


def gather_scratch():
    return [
        pltpu.SemaphoreType.DMA,
        pltpu.SemaphoreType.DMA((14,)),
        pltpu.SemaphoreType.DMA((14,)),
    ]


def scatter_steps(partial, out, mine, theirs, total, diag, last, keep, send, recv):
    f, t = lax.axis_index("fsdp"), lax.axis_index("tp")
    fx, fy, fd = beside(f)
    x, y, core = {"fsdp": fx}, {"fsdp": fy}, {"tp": 1 - t}
    half = out.shape[0] // 2

    def part(ref, h):
        return ref.at[pl.ds(h * half, half)]

    crossing = [
        remote(partial.at[2 * who + 1 - t], theirs.at[i], send.at[i], recv.at[i], core)
        for i, who in enumerate([fd, fy, fx, f])
    ]
    kept = [
        pltpu.make_async_copy(partial.at[2 * who + t], mine.at[i], keep.at[i])
        for i, who in enumerate([fd, fy, fx, f])
    ]
    d0 = remote(part(total.at[0], 0), diag.at[0], send.at[4], recv.at[4], x)
    d1 = remote(part(total.at[0], 1), diag.at[1], send.at[5], recv.at[5], y)
    y1 = remote(part(total.at[1], 1), part(last.at[1], 1), send.at[6], recv.at[6], y)
    x0 = remote(part(total.at[2], 0), part(last.at[0], 0), send.at[7], recv.at[7], x)
    y0 = remote(part(total.at[1], 0), part(last.at[1], 0), send.at[8], recv.at[8], y)
    x1 = remote(part(total.at[2], 1), part(last.at[0], 1), send.at[9], recv.at[9], x)

    def begin():
        for a, b in zip(crossing, kept):
            a.start()
            b.start()

    def add(i):
        kept[i].wait()
        crossing[i].wait_recv()
        total[i] = (mine[i].astype(f32) + theirs[i].astype(f32)).astype(total.dtype)

    def diagonal():
        add(0)
        d0.start()
        d1.start()

    def straight():
        add(1)
        y1.start()
        add(2)
        x0.start()

    def relay():
        d0.wait_recv()
        total[1, :half] = (total[1, :half].astype(f32) + diag[0].astype(f32)).astype(total.dtype)
        y0.start()
        d1.wait_recv()
        total[2, half:] = (total[2, half:].astype(f32) + diag[1].astype(f32)).astype(total.dtype)
        x1.start()

    def end():
        kept[3].wait()
        crossing[3].wait_recv()
        for copy in (y1, x0, y0, x1):
            copy.wait_recv()
        out[...] = (mine[3].astype(f32) + theirs[3].astype(f32)) + (
            last[0].astype(f32) + last[1].astype(f32)
        )
        for copy in (*crossing, d0, d1, y1, x0, y0, x1):
            copy.wait_send()

    return begin, diagonal, straight, relay, end


def scatter_scratch(rows, width, kind):
    return [
        pltpu.VMEM((4, rows, width), kind),
        pltpu.VMEM((4, rows, width), kind),
        pltpu.VMEM((3, rows, width), kind),
        pltpu.VMEM((2, rows // 2, width), kind),
        pltpu.VMEM((2, rows, width), kind),
        pltpu.SemaphoreType.DMA((4,)),
        pltpu.SemaphoreType.DMA((10,)),
        pltpu.SemaphoreType.DMA((10,)),
    ]


def pass_steps(by, local, fade, out, held, send, recv):
    length = lax.axis_size("ctx")
    c = lax.axis_index("ctx")
    first = c == (0 if by > 0 else length - 1)
    last = c == (length - 1 if by > 0 else 0)
    target = lax.rem(c + by + length, length)

    def copy(p):
        return remote(held.at[p], out.at[p], send.at[p], recv.at[p], {"ctx": target})

    def step(p, carry):
        @pl.when(first)
        def _():
            out[p] = jnp.zeros(out.shape[1:], out.dtype)

        @pl.when(jnp.logical_not(first))
        def _():
            copy(p).wait_recv()

        @pl.when(jnp.logical_not(last))
        def _():
            held[p] = (fade[...] * out[p].astype(f32) + local[p]).astype(held.dtype)
            copy(p).start()

        return carry

    def end():
        @pl.when(jnp.logical_not(last))
        def _():
            def done(p, carry):
                copy(p).wait_send()
                return carry

            lax.fori_loop(0, local.shape[0], done, 0)

    return step, end


def greet_plane(by=0):
    f, c, t = lax.axis_index("fsdp"), lax.axis_index("ctx"), lax.axis_index("tp")
    length = lax.axis_size("ctx")
    fx, fy, _ = beside(f)
    barrier = pltpu.get_barrier_semaphore()
    for device in ({"fsdp": fx}, {"fsdp": fy}, {"tp": 1 - t}):
        pl.semaphore_signal(barrier, inc=1, device_id=device, device_id_type=MESH)
    if by != 0:
        first = c == (0 if by > 0 else length - 1)
        last = c == (length - 1 if by > 0 else 0)
        source = {"ctx": lax.rem(c - by + length, length)}

        @pl.when(jnp.logical_not(first))
        def _():
            pl.semaphore_signal(barrier, inc=1, device_id=source, device_id_type=MESH)

        @pl.when(jnp.logical_not(last))
        def _():
            pl.semaphore_wait(barrier, 4)

        @pl.when(last)
        def _():
            pl.semaphore_wait(barrier, 3)
    else:
        pl.semaphore_wait(barrier, 3)


def gather_kernel(*refs):
    steps = gather_steps(*refs)
    greet_plane()
    for step in steps:
        step()


def scatter_kernel(*refs):
    steps = scatter_steps(*refs)
    greet_plane()
    for step in steps:
        step()


def pass_gather_kernel(by, local, fade, own, out, full, held, send, recv, *scratch):
    begin, relay, rest, diagonal, end = gather_steps(own, full, *scratch)
    step, done = pass_steps(by, local, fade, out, held, send, recv)
    pieces = local.shape[0]
    greet_plane(by)
    begin()
    lax.fori_loop(0, pieces // 4, step, 0)
    relay()
    lax.fori_loop(pieces // 4, pieces // 2, step, 0)
    rest()
    lax.fori_loop(pieces // 2, pieces, step, 0)
    diagonal()
    end()
    done()


def pass_scatter_kernel(by, local, fade, partial, out, own, held, send, recv, *scratch):
    begin, diagonal, straight, relay, end = scatter_steps(partial, own, *scratch)
    step, done = pass_steps(by, local, fade, out, held, send, recv)
    pieces = local.shape[0]
    greet_plane(by)
    begin()
    lax.fori_loop(0, pieces // 4, step, 0)
    diagonal()
    straight()
    lax.fori_loop(pieces // 4, 3 * pieces // 4, step, 0)
    relay()
    lax.fori_loop(3 * pieces // 4, pieces, step, 0)
    end()
    done()


def call(kernel, collective_id, outs, ins, scratch, *args):
    shapes, spaces = zip(*outs)
    return pl.pallas_call(
        kernel,
        out_shape=shapes,
        in_specs=[pl.BlockSpec(memory_space=space) for space in ins],
        out_specs=tuple(pl.BlockSpec(memory_space=space) for space in spaces),
        scratch_shapes=scratch,
        compiler_params=pltpu.CompilerParams(
            collective_id=collective_id, has_side_effects=True, vmem_limit_bytes=44 << 20
        ),
        cost_estimate=pl.CostEstimate(flops=0, bytes_accessed=2_000_000, transcendentals=0),
    )(*args)


def gathered(own):
    rows, width = own.shape
    return jax.ShapeDtypeStruct((8, rows, width), own.dtype), pl.ANY


def scattered(partial):
    rows, width = partial.shape
    return jax.ShapeDtypeStruct((rows // 8, width), f32), pltpu.VMEM


def passed(local):
    return jax.ShapeDtypeStruct(local.shape, bf16), pltpu.VMEM


def pass_scratch(local):
    pieces = local.shape[0]
    return [
        pltpu.VMEM(local.shape, bf16),
        pltpu.SemaphoreType.DMA((pieces,)),
        pltpu.SemaphoreType.DMA((pieces,)),
    ]


def in_eights(partial):
    return partial.reshape(8, -1, partial.shape[1])


def gather_rows(own, collective_id):
    (out,) = call(gather_kernel, collective_id, [gathered(own)], [pl.ANY], gather_scratch(), own)
    return out.reshape(-1, own.shape[1])


def scatter_rows(partial, collective_id):
    scratch = scatter_scratch(partial.shape[0] // 8, partial.shape[1], partial.dtype)
    (out,) = call(
        scatter_kernel,
        collective_id,
        [scattered(partial)],
        [pl.ANY],
        scratch,
        in_eights(partial),
    )
    return out


def pass_and_gather(local, fade, own, by, collective_id):
    out, full = call(
        functools.partial(pass_gather_kernel, by),
        collective_id,
        [passed(local), gathered(own)],
        [pltpu.VMEM, pltpu.VMEM, pl.ANY],
        pass_scratch(local) + gather_scratch(),
        local,
        jnp.full((1, local.shape[2]), fade, f32),
        own,
    )
    return out, full.reshape(-1, own.shape[1])


def pass_and_scatter(local, fade, partial, by, collective_id):
    rows, width = partial.shape
    return call(
        functools.partial(pass_scatter_kernel, by),
        collective_id,
        [passed(local), scattered(partial)],
        [pltpu.VMEM, pltpu.VMEM, pl.ANY],
        pass_scratch(local) + scatter_scratch(rows // 8, width, partial.dtype),
        local,
        jnp.full((1, local.shape[2]), fade, f32),
        in_eights(partial),
    )


def peer_of(place, nc, nt):
    return {"fsdp": place // (nc * nt), "ctx": place // nt % nc, "tp": place % nt}


def spread_kernel(own, out, keep, send, recv):
    nc = lax.axis_size("ctx")
    count = out.shape[0]
    t = lax.axis_index("tp")
    place = lax.axis_index("fsdp") * nc + lax.axis_index("ctx")
    barrier = pltpu.get_barrier_semaphore()

    def peer(i):
        other = lax.rem(place + i, count)
        return {"fsdp": other // nc, "ctx": other % nc}

    def hello(i, carry):
        pl.semaphore_signal(barrier, inc=1, device_id=peer(i), device_id_type=MESH)
        return carry

    lax.fori_loop(1, count, hello, 0)
    pl.semaphore_wait(barrier, count - 1)

    def copy(i):
        return remote(own, out.at[place], send.at[i], recv.at[i], peer(i))

    def go(i, carry):
        copy(i).start()
        return carry

    lax.fori_loop(1, count, go, 0)
    local = pltpu.make_async_copy(own, out.at[place], keep)
    local.start()
    local.wait()

    def done(i, carry):
        copy(i).wait()
        return carry

    lax.fori_loop(1, count, done, 0)


def spread_small(own, collective_id):
    count = lax.axis_size("fsdp") * lax.axis_size("ctx")
    return pl.pallas_call(
        spread_kernel,
        out_shape=jax.ShapeDtypeStruct((count, *own.shape), own.dtype),
        in_specs=[pl.BlockSpec(memory_space=pltpu.VMEM)],
        out_specs=pl.BlockSpec(memory_space=pltpu.VMEM),
        scratch_shapes=[
            pltpu.SemaphoreType.DMA,
            pltpu.SemaphoreType.DMA((count,)),
            pltpu.SemaphoreType.DMA((count,)),
        ],
        compiler_params=pltpu.CompilerParams(collective_id=collective_id, has_side_effects=True),
        cost_estimate=pl.CostEstimate(flops=0, bytes_accessed=1_000_000, transcendentals=0),
    )(own)


def total_kernel(parts, out, slots, send, recv):
    nc, nt = lax.axis_size("ctx"), lax.axis_size("tp")
    count = parts.shape[0]
    place = (lax.axis_index("fsdp") * nc + lax.axis_index("ctx")) * nt + lax.axis_index("tp")
    barrier = pltpu.get_barrier_semaphore()

    def hello(i, carry):
        other = peer_of(lax.rem(place + i, count), nc, nt)
        pl.semaphore_signal(barrier, inc=1, device_id=other, device_id_type=MESH)
        return carry

    lax.fori_loop(1, count, hello, 0)
    pl.semaphore_wait(barrier, count - 1)

    def copy(i):
        other = lax.rem(place + i, count)
        return remote(
            parts.at[other], slots.at[i], send.at[i], recv.at[i], peer_of(other, nc, nt)
        )

    def go(i, carry):
        copy(i).start()
        return carry

    lax.fori_loop(1, count, go, 0)

    def add(i, carry):
        copy(i).wait()
        return carry + slots[i]

    out[...] = lax.fori_loop(1, count, add, parts[place])


def total_small(parts, collective_id):
    count = parts.shape[0]
    return pl.pallas_call(
        total_kernel,
        out_shape=jax.ShapeDtypeStruct(parts.shape[1:], parts.dtype),
        in_specs=[pl.BlockSpec(memory_space=pltpu.VMEM)],
        out_specs=pl.BlockSpec(memory_space=pltpu.VMEM),
        scratch_shapes=[
            pltpu.VMEM(parts.shape, parts.dtype),
            pltpu.SemaphoreType.DMA((count,)),
            pltpu.SemaphoreType.DMA((count,)),
        ],
        compiler_params=pltpu.CompilerParams(collective_id=collective_id, has_side_effects=True),
        cost_estimate=pl.CostEstimate(flops=0, bytes_accessed=1_000_000, transcendentals=0),
    )(parts)


def both_halves(own, t):
    other = lax.ppermute(own, "tp", [(0, 1), (1, 0)])
    return jnp.where(t == 0, jnp.concatenate([own, other]), jnp.concatenate([other, own]))


def shards(
    tokens,
    lengths,
    cotangent,
    pre_gain,
    pre_bias,
    query_weight,
    key_weight,
    value_weight,
    swish_weight,
    out_weight,
    group_gain,
    group_bias,
    mlp_gain,
    mlp_bias,
    gelu_weight,
    up_weight,
    down_weight,
):
    seq_count, span, width = tokens.shape
    nf, nc, nt = lax.axis_size("fsdp"), lax.axis_size("ctx"), lax.axis_size("tp")
    f, c, t = lax.axis_index("fsdp"), lax.axis_index("ctx"), lax.axis_index("tp")
    block_rows = seq_count * span
    own_rows = block_rows // nt
    depth = query_weight.shape[0]
    heads_local = group_gain.shape[0]
    assert heads_local == nf
    key_size = query_weight.shape[1] // heads_local
    value_size = value_weight.shape[1] // heads_local
    hidden_size = gelu_weight.shape[1] // nf
    seqs = nf * seq_count
    rows = seqs * span
    head = t * heads_local + f

    def pad_tile(v):
        return jnp.pad(v, [(0, 0)] * (v.ndim - 1) + [(0, -v.shape[-1] % 1024)]).reshape(
            *v.shape[:-1], 8, -1
        )

    def perm(v):
        return v.reshape(-1, nf, nc, depth).transpose(0, 2, 1, 3).reshape(-1, width)

    def unperm(v):
        return v.reshape(-1, nc, nf, depth).transpose(0, 2, 1, 3).reshape(-1, width)

    def own_part(v):
        return lax.dynamic_slice_in_dim(v.reshape(block_rows, width), t * own_rows, own_rows, 0)

    def spread(w):
        return w.reshape(depth, nf, -1).transpose(1, 0, 2)

    def head_columns(*ws):
        mine = jnp.concatenate([spread(w) for w in ws], -1)
        return lax.all_to_all(mine, "fsdp", 0, 0, tiled=True)

    def all_depths(mine):
        return lax.all_gather(mine, "ctx", axis=0, tiled=True).reshape(width, -1)

    attn_w = all_depths(head_columns(query_weight, key_weight, value_weight, swish_weight))
    rest = head_columns(out_weight.T, gelu_weight, up_weight, down_weight.T)
    out_t = all_depths(rest[..., :value_size])

    small = jnp.concatenate(
        [
            jnp.stack([pre_gain, pre_bias, mlp_gain, mlp_bias]).astype(f32).reshape(-1),
            group_gain.astype(f32).reshape(-1),
            group_bias.astype(f32).reshape(-1),
            lengths.astype(f32),
        ]
    )
    small_size = small.size
    small = spread_small(pad_tile(small), 4).reshape(nf * nc, -1)[:, :small_size]
    pre_gain_full, pre_bias_full, mlp_gain_full, mlp_bias_full = (
        small[:, i * depth : (i + 1) * depth].reshape(width) for i in range(4)
    )
    group = small[:, 4 * depth : 4 * depth + 2 * group_gain.size].reshape(
        nf * nc, 2, heads_local, -1
    )
    group = lax.dynamic_index_in_dim(group, f, 2, False).transpose(1, 0, 2).reshape(2, value_size)
    all_lengths = small.reshape(nf, nc, -1)[:, 0, -seq_count:].reshape(seqs)

    inputs = own_part(tokens).astype(f32)
    normed_wide, norm_in_back = jax.vjp(layer_norm, inputs, pre_gain_full, pre_bias_full)
    normed = gather_rows(perm(normed_wide.astype(bf16)), 0)
    positions = c * span + lax.iota(jnp.int32, span)
    own_ids = t * own_rows + lax.iota(jnp.int32, own_rows)
    own_valid = (c * span + own_ids % span < lengths[own_ids // span]).astype(f32)[:, None]
    error = own_valid * own_part(cotangent).astype(f32)

    pre = product(normed, attn_w)
    valid = (positions.astype(f32)[None, :] < all_lengths[:, None]).astype(f32)[:, :, None]
    cosine, sine = turn_tables(positions, key_size // 2)
    key_scale = key_size ** (-0.5)
    query_pre = pre[:, :key_size].reshape(seqs, span, key_size)
    key_pre = pre[:, key_size : 2 * key_size].reshape(seqs, span, key_size)
    value_pre = pre[:, 2 * key_size : 2 * key_size + value_size]
    swish_pre = pre[:, 2 * key_size + value_size :]
    queries = rotate(query_pre, cosine, sine).astype(bf16)
    keys = (rotate(key_pre, cosine, sine) * key_scale * valid).astype(bf16)
    values = value_pre.astype(bf16).reshape(seqs, span, value_size)

    log_decay = jnp.log1p(-jnp.exp2(-5.0 - head.astype(f32)))
    offsets = jnp.arange(span)
    distance = (offsets[:, None] - offsets[None, :]).astype(f32)
    within_fade = jnp.where(distance >= 0, jnp.exp(jnp.maximum(distance, 0.0) * log_decay), 0.0)
    key_fade = jnp.exp((span - 1 - offsets).astype(f32) * log_decay)[:, None]
    query_fade = jnp.exp((offsets + 1).astype(f32) * log_decay)[:, None]
    block_fade = jnp.exp(span * log_decay)

    keys_faded = (keys.astype(f32) * key_fade).astype(bf16)
    queries_faded = (queries.astype(f32) * query_fade).astype(bf16)
    local_state = blocks("sjd,sje->sde", keys_faded, values)
    error_low = perm(error.astype(bf16))
    entering, error_all = pass_and_gather(local_state, block_fade, error_low, 1, 2)
    rest, entering = lax.optimization_barrier((rest, entering))
    ff_w = all_depths(rest[..., value_size:])
    gelu_up = ff_w[:, : 2 * hidden_size]
    down_t = ff_w[:, 2 * hidden_size :]
    probs = (blocks("sid,sjd->sij", queries, keys) * within_fade).astype(bf16)
    mixed = blocks("sij,sje->sie", probs, values) + blocks("sid,sde->sie", queries_faded, entering)
    gated_wide, gate_back = jax.vjp(
        gate_mix, mixed.reshape(rows, value_size), swish_pre, group[0], group[1]
    )
    gated = gated_wide.astype(bf16)
    branch = scatter_rows(product_right(gated, out_t).astype(bf16), 1)
    hidden = inputs + unperm(branch)

    mlp_wide, norm_mid_back = jax.vjp(layer_norm, hidden, mlp_gain_full, mlp_bias_full)
    mlp_in = gather_rows(perm(mlp_wide.astype(bf16)), 0)
    pre_ff = product(mlp_in, gelu_up)
    inner_wide, mix_back = jax.vjp(mlp_mix, pre_ff[:, :hidden_size], pre_ff[:, hidden_size:])
    inner = inner_wide.astype(bf16)
    mlp_part = product_right(inner, down_t).astype(bf16)

    def sum_depths(grads):
        grads = with_layout_constraint(grads.astype(bf16), Layout((0, 1)))
        mine = lax.psum_scatter(grads, "ctx", scatter_dimension=0, tiled=True)
        return mine.reshape(nf, depth, -1)

    def all_heads(mine):
        return lax.all_to_all(mine, "fsdp", 0, 0, tiled=True).astype(f32)

    def along(grads):
        return grads.transpose(1, 0, 2).reshape(depth, -1)

    def across(grads):
        return grads.transpose(0, 2, 1).reshape(-1, depth)

    grad_down_t = product_left(error_all, inner)
    gelu_grad, up_grad = mix_back(product(error_all, down_t))
    ff_low = jnp.concatenate([gelu_grad.astype(bf16), up_grad.astype(bf16)], -1)
    grad_gelu_up = product_left(mlp_in, ff_low)
    ff_parts = jnp.concatenate([grad_gelu_up, grad_down_t], -1).astype(bf16)
    ff_parts, ff_low = lax.optimization_barrier((ff_parts, ff_low))
    ff_sum = sum_depths(ff_parts)
    mlp_in_grad = unperm(scatter_rows(product_right(ff_low, gelu_up).astype(bf16), 1))
    hidden_norm_grad, grad_mlp_gain, grad_mlp_bias = norm_mid_back(mlp_in_grad)
    hidden_grad = error + hidden_norm_grad

    hidden_low = gather_rows(perm(hidden_grad.astype(bf16)), 0)
    grad_out_t = product_left(hidden_low, gated)
    gated_grad = product(hidden_low, out_t)
    mixed_grad, swish_grad, grad_group_gain, grad_group_bias = gate_back(gated_grad)
    swish_low = swish_grad.astype(bf16)
    mixed_low = mixed_grad.astype(bf16).reshape(seqs, span, value_size)
    score_low = (blocks("sie,sje->sij", mixed_low, values) * within_fade).astype(bf16)
    pulled_state = blocks("sid,sie->sde", queries_faded, mixed_low)
    early = jnp.concatenate([product_left(normed, swish_low), grad_out_t], -1).astype(bf16)
    early, pulled_state, ff_sum = lax.optimization_barrier((early, pulled_state, ff_sum))
    later, mlp_out = pass_and_scatter(pulled_state, block_fade, mlp_part, -1, 3)
    early, later = lax.optimization_barrier((early, later))
    early_sum = sum_depths(early)
    block_own = (own_valid * (hidden + unperm(mlp_out))).astype(bf16)
    block_out = both_halves(block_own, t).reshape(tokens.shape)
    query_grad = blocks("sij,sjd->sid", score_low, keys) + query_fade * blocks(
        "sie,sde->sid", mixed_low, entering
    )
    key_grad = blocks("sij,sid->sjd", score_low, queries) + key_fade * blocks(
        "sje,sde->sjd", values, later
    )
    value_grad = blocks("sij,sie->sje", probs, mixed_low) + blocks(
        "sjd,sde->sje", keys_faded, later
    )
    query_low = rotate_back(query_grad, cosine, sine).astype(bf16).reshape(rows, key_size)
    key_low = rotate_back(key_grad * key_scale * valid, cosine, sine).astype(bf16)
    low = jnp.concatenate(
        [
            query_low,
            key_low.reshape(rows, key_size),
            value_grad.astype(bf16).reshape(rows, value_size),
        ],
        -1,
    )
    attn_part = product_left(normed, low).astype(bf16)
    attn_part, low = lax.optimization_barrier((attn_part, low))
    attn_sum = sum_depths(attn_part)
    low = jnp.concatenate([low, swish_low], -1)
    normed_grad = unperm(scatter_rows(product_right(low, attn_w).astype(bf16), 1))
    early_sum, normed_grad = lax.optimization_barrier((early_sum, normed_grad))
    input_norm_grad, grad_pre_gain, grad_pre_bias = norm_in_back(normed_grad)
    tokens_own = (hidden_grad + input_norm_grad).astype(bf16)
    grad_tokens = both_halves(tokens_own, t).reshape(tokens.shape)

    norm_parts = jnp.stack([grad_pre_gain, grad_pre_bias, grad_mlp_gain, grad_mlp_bias])
    norm_parts = norm_parts.reshape(4, nf * nc, 1, depth).transpose(1, 2, 0, 3)
    norm_parts = jnp.broadcast_to(norm_parts, (nf * nc, nt, 4, depth)).reshape(nf * nc, nt, -1)
    mine = lax.iota(jnp.int32, nt * heads_local) == head
    group_parts = jnp.stack([grad_group_gain, grad_group_bias]).reshape(1, 2, nf * nc, -1)
    group_parts = jnp.where(mine[:, None, None, None], group_parts, 0.0)
    group_parts = group_parts.reshape(nt, heads_local, 2, nf * nc, -1).transpose(3, 0, 2, 1, 4)
    parts = jnp.concatenate([norm_parts, group_parts.reshape(nf * nc, nt, -1)], -1)
    parts = parts.reshape(nf * nc * nt, -1)
    sums = total_small(pad_tile(parts), 5).reshape(-1)[: parts.shape[1]]
    sums, attn_sum = lax.optimization_barrier((sums, attn_sum))
    ff_grads, early_grads, attn_grads = (all_heads(v) for v in (ff_sum, early_sum, attn_sum))
    norm_sums = sums[: 4 * depth].reshape(4, depth)
    group_sums = sums[4 * depth :].reshape(2, heads_local, -1)

    at = [0, key_size, 2 * key_size]
    return (
        block_out,
        grad_tokens,
        norm_sums[0],
        norm_sums[1],
        along(attn_grads[..., : at[1]]),
        along(attn_grads[..., at[1] : at[2]]),
        along(attn_grads[..., at[2] :]),
        along(early_grads[..., :value_size]),
        across(early_grads[..., value_size:]),
        group_sums[0],
        group_sums[1],
        norm_sums[2],
        norm_sums[3],
        along(ff_grads[..., :hidden_size]),
        along(ff_grads[..., hidden_size : 2 * hidden_size]),
        across(ff_grads[..., 2 * hidden_size :]),
    )


def solution(mesh):
    rows = P("fsdp", "ctx", None)
    vector = P(("fsdp", "ctx"))
    tall = P(("fsdp", "ctx"), "tp")
    wide = P("tp", ("fsdp", "ctx"))
    in_specs = (rows, P("fsdp"), rows, vector, vector, tall, tall, tall, tall, wide)
    in_specs += (wide, wide, vector, vector, tall, tall, wide)
    out_specs = (rows, rows, vector, vector, tall, tall, tall, tall, wide)
    out_specs += (wide, wide, vector, vector, tall, tall, wide)
    return jax.shard_map(shards, mesh=mesh, in_specs=in_specs, out_specs=out_specs, check_vma=False)
```

```python
import functools

import jax
import jax.numpy as jnp
from jax import lax
from jax.experimental import pallas as pl
from jax.experimental.layout import Layout, with_layout_constraint
from jax.experimental.pallas import tpu as pltpu
from jax.sharding import PartitionSpec as P

eps = 1e-05
group_floor = 1.0
f32 = jnp.float32
bf16 = jnp.bfloat16


def layer_norm(values, norm_gain, norm_shift):
    centred = values - jnp.mean(values, -1, keepdims=True)
    spread = jnp.mean(centred * centred, -1, keepdims=True)
    return centred * lax.rsqrt(spread + eps) * norm_gain + norm_shift


def turn_tables(positions, half_size):
    frequency = jnp.power(10000.0, -jnp.arange(half_size).astype(f32) / half_size)
    angles = positions.astype(f32)[:, None] * frequency[None, :]
    return jnp.cos(angles), jnp.sin(angles)


def rotate(values, cosine, sine):
    half_size = values.shape[-1] // 2
    first = values[..., :half_size]
    second = values[..., half_size:]
    return jnp.concatenate([first * cosine - second * sine, second * cosine + first * sine], -1)


def rotate_back(values, cosine, sine):
    return rotate(values, cosine, -sine)


def gate_mix(mixed, swish_pre, norm_gain, norm_shift):
    centred = mixed - jnp.mean(mixed, -1, keepdims=True)
    spread = jnp.mean(centred * centred, -1, keepdims=True)
    return jax.nn.silu(swish_pre) * (
        centred * lax.rsqrt(spread + group_floor) * norm_gain + norm_shift
    )


def mlp_mix(gelu_pre, up_pre):
    return jax.nn.gelu(gelu_pre) * up_pre


def product(left, right):
    return jnp.dot(left, right, preferred_element_type=f32)


def product_left(left, right):
    return lax.dot_general(left, right, (((0,), (0,)), ((), ())), preferred_element_type=f32)


def product_right(left, right):
    return lax.dot_general(left, right, (((1,), (1,)), ((), ())), preferred_element_type=f32)


def blocks(spec, left, right):
    return jnp.einsum(spec, left, right, preferred_element_type=f32)


MESH = pl.DeviceIdType.MESH


def beside(f):
    return f + 1 - 2 * (f % 2), (f + 2) % 4, 3 - f


def remote(src, dst, send, recv, device):
    return pltpu.make_async_remote_copy(
        src_ref=src, dst_ref=dst, send_sem=send, recv_sem=recv, device_id=device, device_id_type=MESH
    )


def reorder(src, dst, kind, back):
    nf, nc = lax.axis_size("fsdp"), lax.axis_size("ctx")
    depth = src.shape[-1] // (nf * nc)
    for f in range(nf):
        for c in range(nc):
            plain, mixed = (f * nc + c) * depth, (c * nf + f) * depth
            if back:
                plain, mixed = mixed, plain
            dst[:, mixed : mixed + depth] = src[:, plain : plain + depth].astype(kind)


def gather_steps(plain, out, mixed, keep, send, recv):
    own = plain if mixed is None else mixed
    f, t = lax.axis_index("fsdp"), lax.axis_index("tp")
    fx, fy, fd = beside(f)
    x, y, core = {"fsdp": fx}, {"fsdp": fy}, {"tp": 1 - t}
    half = own.shape[0] // 2

    def part(ref, h):
        return ref.at[pl.ds(h * half, half)]

    def slot(who, h):
        return part(out.at[2 * who + t], h)

    local = pltpu.make_async_copy(own, out.at[2 * f + t], keep)
    first = [
        remote(part(own, 0), slot(f, 0), send.at[0], recv.at[0], x),
        remote(part(own, 1), slot(f, 1), send.at[1], recv.at[3], y),
        remote(part(own, 1), slot(f, 1), send.at[2], recv.at[1], x),
        remote(part(own, 0), slot(f, 0), send.at[3], recv.at[2], y),
        remote(part(own, 0), slot(f, 0), send.at[4], recv.at[6], core),
        remote(part(own, 1), slot(f, 1), send.at[5], recv.at[7], core),
    ]
    sent = list(first)

    def pass_on(who, h, s, r, device):
        copy = remote(slot(who, h), slot(who, h), send.at[s], recv.at[r], device)
        copy.start()
        sent.append(copy)

    def begin():
        if mixed is not None:
            reorder(plain, mixed, mixed.dtype, False)
        local.start()
        for copy in first:
            copy.start()

    def relay():
        first[0].wait_recv()
        pass_on(fx, 0, 6, 4, y)
        pass_on(fx, 0, 7, 8, core)
        first[1].wait_recv()
        pass_on(fy, 1, 8, 5, x)
        pass_on(fy, 1, 9, 11, core)

    def rest():
        first[2].wait_recv()
        pass_on(fx, 1, 10, 9, core)
        first[3].wait_recv()
        pass_on(fy, 0, 11, 10, core)

    def diagonal():
        remote(slot(fd, 0), slot(fd, 0), send.at[12], recv.at[4], y).wait_recv()
        pass_on(fd, 0, 12, 12, core)
        remote(slot(fd, 1), slot(fd, 1), send.at[13], recv.at[5], x).wait_recv()
        pass_on(fd, 1, 13, 13, core)

    def end():
        for r in range(6, 14):
            remote(slot(f, 0), slot(f, 0), send.at[0], recv.at[r], core).wait_recv()
        for copy in sent:
            copy.wait_send()
        local.wait()

    return begin, relay, rest, diagonal, end


def in_kernel(width):
    return width // (lax.axis_size("fsdp") * lax.axis_size("ctx")) % 128 == 0


def gather_scratch(own):
    return [
        pltpu.VMEM(own.shape if in_kernel(own.shape[1]) else (16, 128), own.dtype),
        pltpu.SemaphoreType.DMA,
        pltpu.SemaphoreType.DMA((14,)),
        pltpu.SemaphoreType.DMA((14,)),
    ]


def scatter_steps(start, left, right, out, mine, sent, theirs, total, diag, last, send, recv):
    f, t = lax.axis_index("fsdp"), lax.axis_index("tp")
    fx, fy, fd = beside(f)
    x, y, core = {"fsdp": fx}, {"fsdp": fy}, {"tp": 1 - t}
    half = out.shape[0] // 2
    order = [fd, fy, fx, f]
    tile, size = 512, left.shape[2]

    def part(ref, h):
        return ref.at[pl.ds(h * half, half)]

    crossing = [
        remote(sent.at[i], theirs.at[i], send.at[i], recv.at[i], core) for i in range(4)
    ]
    d0 = remote(part(total.at[0], 0), diag.at[0], send.at[4], recv.at[4], x)
    d1 = remote(part(total.at[0], 1), diag.at[1], send.at[5], recv.at[5], y)
    y1 = remote(part(total.at[1], 1), part(last.at[1], 1), send.at[6], recv.at[6], y)
    x0 = remote(part(total.at[2], 0), part(last.at[0], 0), send.at[7], recv.at[7], x)
    y0 = remote(part(total.at[1], 0), part(last.at[1], 0), send.at[8], recv.at[8], y)
    x1 = remote(part(total.at[2], 1), part(last.at[0], 1), send.at[9], recv.at[9], x)

    def make(block, put):
        def piece(j, carry):
            columns = pl.ds(pl.multiple_of(j * tile, tile), tile)
            put(columns, product_right(left[block], right[columns, start : start + size]))
            return carry

        lax.fori_loop(0, out.shape[1] // tile, piece, 0)

    def cross(i):
        def put(columns, value):
            sent[i, :, columns] = value.astype(sent.dtype)

        make(2 * order[i] + 1 - t, put)
        crossing[i].start()

    def keep(i):
        def put(columns, value):
            mine[:, columns] = value

        make(2 * order[i] + t, put)

    def add(i):
        keep(i)
        crossing[i].wait_recv()
        total[i] = (mine[...] + theirs[i].astype(f32)).astype(total.dtype)

    def diagonal():
        cross(0)
        cross(1)
        add(0)
        d0.start()
        d1.start()

    def straight():
        cross(2)
        add(1)
        y1.start()
        add(2)
        x0.start()
        cross(3)

    def relay():
        d0.wait_recv()
        total[1, :half] = (total[1, :half].astype(f32) + diag[0].astype(f32)).astype(total.dtype)
        y0.start()
        d1.wait_recv()
        total[2, half:] = (total[2, half:].astype(f32) + diag[1].astype(f32)).astype(total.dtype)
        x1.start()
        keep(3)
        crossing[3].wait_recv()
        mine[...] += theirs[3].astype(f32)

    def end():
        for copy in (y1, x0, y0, x1):
            copy.wait_recv()
        mine[...] += last[0].astype(f32) + last[1].astype(f32)
        if in_kernel(out.shape[1]):
            reorder(mine, out, out.dtype, True)
        else:
            out[...] = mine[...]
        for copy in (*crossing, d0, d1, y1, x0, y0, x1):
            copy.wait_send()

    return diagonal, straight, relay, end


def scatter_scratch(rows, width):
    return [
        pltpu.VMEM((rows, width), f32),
        pltpu.VMEM((4, rows, width), bf16),
        pltpu.VMEM((4, rows, width), bf16),
        pltpu.VMEM((3, rows, width), bf16),
        pltpu.VMEM((2, rows // 2, width), bf16),
        pltpu.VMEM((2, rows, width), bf16),
        pltpu.SemaphoreType.DMA((10,)),
        pltpu.SemaphoreType.DMA((10,)),
    ]


def pass_steps(by, local, fade, out, held, send, recv):
    length = lax.axis_size("ctx")
    c = lax.axis_index("ctx")
    first = c == (0 if by > 0 else length - 1)
    last = c == (length - 1 if by > 0 else 0)
    target = lax.rem(c + by + length, length)

    def copy(p):
        return remote(held.at[p], out.at[p], send.at[p], recv.at[p], {"ctx": target})

    def step(p, carry):
        @pl.when(first)
        def _():
            out[p] = jnp.zeros(out.shape[1:], out.dtype)

        @pl.when(jnp.logical_not(first))
        def _():
            copy(p).wait_recv()

        @pl.when(jnp.logical_not(last))
        def _():
            held[p] = (fade[...] * out[p].astype(f32) + local[p]).astype(held.dtype)
            copy(p).start()

        return carry

    def end():
        @pl.when(jnp.logical_not(last))
        def _():
            def done(p, carry):
                copy(p).wait_send()
                return carry

            lax.fori_loop(0, local.shape[0], done, 0)

    return step, end


def greet_plane(by=0):
    f, c, t = lax.axis_index("fsdp"), lax.axis_index("ctx"), lax.axis_index("tp")
    length = lax.axis_size("ctx")
    fx, fy, _ = beside(f)
    barrier = pltpu.get_barrier_semaphore()
    for device in ({"fsdp": fx}, {"fsdp": fy}, {"tp": 1 - t}):
        pl.semaphore_signal(barrier, inc=1, device_id=device, device_id_type=MESH)
    if by != 0:
        first = c == (0 if by > 0 else length - 1)
        last = c == (length - 1 if by > 0 else 0)
        source = {"ctx": lax.rem(c - by + length, length)}

        @pl.when(jnp.logical_not(first))
        def _():
            pl.semaphore_signal(barrier, inc=1, device_id=source, device_id_type=MESH)

        @pl.when(jnp.logical_not(last))
        def _():
            pl.semaphore_wait(barrier, 4)

        @pl.when(last)
        def _():
            pl.semaphore_wait(barrier, 3)
    else:
        pl.semaphore_wait(barrier, 3)


def gather_with(own, full, mixed, *scratch):
    return gather_steps(own, full, mixed if in_kernel(own.shape[1]) else None, *scratch)


def gather_kernel(*refs):
    steps = gather_with(*refs)
    greet_plane()
    for step in steps:
        step()


def scatter_kernel(start, *refs):
    steps = scatter_steps(start, *refs)
    greet_plane()
    for step in steps:
        step()


def pass_gather_kernel(by, local, fade, own, out, full, held, send, recv, *scratch):
    begin, relay, rest, diagonal, end = gather_with(own, full, *scratch)
    step, done = pass_steps(by, local, fade, out, held, send, recv)
    pieces = local.shape[0]
    greet_plane(by)
    begin()
    lax.fori_loop(0, pieces // 4, step, 0)
    relay()
    lax.fori_loop(pieces // 4, pieces // 2, step, 0)
    rest()
    lax.fori_loop(pieces // 2, pieces, step, 0)
    diagonal()
    end()
    done()


def pass_scatter_kernel(by, start, local, fade, left, right, out, own, held, send, recv, *scratch):
    diagonal, straight, relay, end = scatter_steps(start, left, right, own, *scratch)
    step, done = pass_steps(by, local, fade, out, held, send, recv)
    pieces = local.shape[0]
    greet_plane(by)
    lax.fori_loop(0, pieces // 4, step, 0)
    diagonal()
    lax.fori_loop(pieces // 4, pieces // 2, step, 0)
    straight()
    lax.fori_loop(pieces // 2, 3 * pieces // 4, step, 0)
    relay()
    lax.fori_loop(3 * pieces // 4, pieces, step, 0)
    end()
    done()


def call(kernel, collective_id, outs, ins, scratch, *args):
    shapes, spaces = zip(*outs)
    return pl.pallas_call(
        kernel,
        out_shape=shapes,
        in_specs=ins,
        out_specs=tuple(pl.BlockSpec(memory_space=space) for space in spaces),
        scratch_shapes=scratch,
        compiler_params=pltpu.CompilerParams(
            collective_id=collective_id, has_side_effects=True, vmem_limit_bytes=52 << 20
        ),
        cost_estimate=pl.CostEstimate(flops=0, bytes_accessed=2_000_000, transcendentals=0),
    )(*args)


def vmem():
    return pl.BlockSpec(memory_space=pltpu.VMEM)


def perm(v):
    nf, nc = lax.axis_size("fsdp"), lax.axis_size("ctx")
    return v.reshape(len(v), nf, nc, -1).transpose(0, 2, 1, 3).reshape(v.shape)


def unperm(v):
    nf, nc = lax.axis_size("fsdp"), lax.axis_size("ctx")
    return v.reshape(len(v), nc, nf, -1).transpose(0, 2, 1, 3).reshape(v.shape)


def gathered(own):
    rows, width = own.shape
    return jax.ShapeDtypeStruct((8, rows, width), own.dtype), pl.ANY


def scattered(left, right):
    return jax.ShapeDtypeStruct((left.shape[0] // 8, right.shape[0]), f32), pltpu.VMEM


def passed(local):
    return jax.ShapeDtypeStruct(local.shape, bf16), pltpu.VMEM


def pass_scratch(local):
    pieces = local.shape[0]
    return [
        pltpu.VMEM(local.shape, bf16),
        pltpu.SemaphoreType.DMA((pieces,)),
        pltpu.SemaphoreType.DMA((pieces,)),
    ]


def in_eights(left):
    return left.reshape(8, -1, left.shape[1])


def ready(own):
    return own if in_kernel(own.shape[1]) else perm(own)


def plain(own):
    return own if in_kernel(own.shape[1]) else unperm(own)


def gather_rows(own, collective_id):
    own = ready(own)
    (out,) = call(gather_kernel, collective_id, [gathered(own)], [vmem()], gather_scratch(own), own)
    return out.reshape(-1, own.shape[1])


def scatter_product(left, right, start, collective_id):
    (out,) = call(
        functools.partial(scatter_kernel, start),
        collective_id,
        [scattered(left, right)],
        [vmem(), vmem()],
        scatter_scratch(left.shape[0] // 8, right.shape[0]),
        in_eights(left),
        right,
    )
    return plain(out)


def pass_and_gather(local, fade, own, by, collective_id):
    own = ready(own)
    out, full = call(
        functools.partial(pass_gather_kernel, by),
        collective_id,
        [passed(local), gathered(own)],
        [vmem(), vmem(), vmem()],
        pass_scratch(local) + gather_scratch(own),
        local,
        jnp.full((1, local.shape[2]), fade, f32),
        own,
    )
    return out, full.reshape(-1, own.shape[1])


def pass_and_scatter(local, fade, left, right, start, by, collective_id):
    out, own = call(
        functools.partial(pass_scatter_kernel, by, start),
        collective_id,
        [passed(local), scattered(left, right)],
        [vmem(), vmem(), vmem(), vmem()],
        pass_scratch(local) + scatter_scratch(left.shape[0] // 8, right.shape[0]),
        local,
        jnp.full((1, local.shape[2]), fade, f32),
        in_eights(left),
        right,
    )
    return out, plain(own)


def peer_of(place, nc, nt):
    return {"fsdp": place // (nc * nt), "ctx": place // nt % nc, "tp": place % nt}


def line_steps(home, place, arrived, send, recv):
    nf, nc = lax.axis_size("fsdp"), lax.axis_size("ctx")
    f, c = lax.axis_index("fsdp"), lax.axis_index("ctx")
    order = [f, *beside(f)]
    above, below = c < nc - 1, c > 0

    def copy(src, place_of, who, up):
        chunk = place_of * nf + who
        return remote(
            src,
            place(place_of, who),
            send.at[chunk if up else nc * nf + chunk],
            recv.at[chunk],
            {"ctx": lax.rem(c + 1, nc) if up else lax.rem(c + nc - 1, nc)},
        )

    def first(i):
        who = order[i]
        arrived(i)

        @pl.when(above)
        def _():
            copy(home(who), c, who, True).start()

        @pl.when(below)
        def _():
            copy(home(who), c, who, False).start()

    def step(k, carry):
        for who in order:

            @pl.when(c - k >= 0)
            def _():
                copy(place(c - k, who), c - k, who, True).wait_recv()

                @pl.when(above)
                def _():
                    copy(place(c - k, who), c - k, who, True).start()

            @pl.when(c + k < nc)
            def _():
                copy(place(c + k, who), c + k, who, False).wait_recv()

                @pl.when(below)
                def _():
                    copy(place(c + k, who), c + k, who, False).start()

        return carry

    def end():
        def one(other, carry):
            for who in order:

                @pl.when(above & (other <= c))
                def _():
                    copy(place(other, who), other, who, True).wait_send()

                @pl.when(below & (other >= c))
                def _():
                    copy(place(other, who), other, who, False).wait_send()

            return carry

        lax.fori_loop(0, nc, one, 0)

    return first, step, end


def line_scratch():
    count = lax.axis_size("fsdp") * lax.axis_size("ctx")
    return [pltpu.SemaphoreType.DMA((2 * count,)), pltpu.SemaphoreType.DMA((count,))]


def start_kernel(sizes, split, turned, own, small, *refs):
    count = len(sizes)
    weights = list(refs[:count])
    attn, rest, full, everyone = refs[count : count + 4]
    (
        turns,
        gains,
        normed,
        mixed,
        gather_keep,
        gather_send,
        gather_recv,
        line_send,
        line_recv,
        keep,
        send,
        recv,
        small_send,
        small_recv,
    ) = refs[count + 4 :]
    nf, nc = lax.axis_size("fsdp"), lax.axis_size("ctx")
    f, c, t = lax.axis_index("fsdp"), lax.axis_index("ctx"), lax.axis_index("tp")
    here, places = f * nc + c, nf * nc
    depth = weights[0].shape[0]
    across = [weights[i] for i in turned]
    for n, i in enumerate(turned):
        weights[i] = turns.at[n]
    near = beside(f)
    starts = [sum(sizes[:i]) if i < split else sum(sizes[split:i]) for i in range(count)]

    def peer(i):
        other = lax.rem(here + i, places)
        return {"fsdp": other // nc, "ctx": other % nc}

    barrier = pltpu.get_barrier_semaphore()
    pl.semaphore_signal(barrier, inc=1, device_id={"tp": 1 - t}, device_id_type=MESH)

    def hello(i, carry):
        pl.semaphore_signal(barrier, inc=1, device_id=peer(i), device_id_type=MESH)
        return carry

    lax.fori_loop(1, places, hello, 0)
    pl.semaphore_wait(barrier, places)

    def chunk(place_of, who):
        rows = pl.multiple_of((place_of * nf + who) * depth, depth)
        return attn.at[pl.ds(rows, depth)]

    def columns(i, who):
        return weights[i].at[:, pl.ds(pl.multiple_of(who * sizes[i], sizes[i]), sizes[i])]

    def target(i):
        where = chunk(c, f) if i < split else rest.at[f]
        return where.at[:, pl.ds(starts[i], sizes[i])]

    def hand_out(i, n):
        return remote(
            columns(i, near[n]),
            target(i),
            send.at[3 * i + n],
            recv.at[n if i < split else 3 + n],
            {"fsdp": near[n]},
        )

    def hold(i):
        return pltpu.make_async_copy(columns(i, f), target(i), keep.at[0 if i < split else 1])

    for i in range(split):
        hold(i).start()
    for n in range(3):
        for i in range(split):
            hand_out(i, n).start()

    def arrived(i):
        if i == 0:
            pltpu.make_async_copy(chunk(c, f), chunk(c, f), keep.at[0]).wait()
        else:
            who = near[i - 1]
            remote(
                chunk(c, who), chunk(c, who), send.at[0], recv.at[i - 1], {"fsdp": who}
            ).wait_recv()

    first, step, end = line_steps(lambda who: chunk(c, who), chunk, arrived, line_send, line_recv)
    first(0)

    def tell(i):
        return remote(small, everyone.at[here], small_send.at[i], small_recv.at[i], peer(i))

    def go(i, carry):
        tell(i).start()
        return carry

    def told(i, carry):
        tell(i).wait()
        return carry

    lax.fori_loop(1, places, go, 0)
    everyone[here] = small[...]
    first(1)
    lax.fori_loop(1, places, told, 0)
    for i in range(places):
        for j in range(2):
            gains[j : j + 1, i * depth : (i + 1) * depth] = everyone[i, j : j + 1, :depth]
    rows = normed.shape[0]
    mine = own[pl.ds(pl.multiple_of(t * rows, rows), rows), :].astype(f32)
    normed[...] = layer_norm(mine, gains[0:1, :], gains[1:2, :]).astype(bf16)
    begin, relay, others, diagonal, finish = gather_steps(
        normed, full, mixed, gather_keep, gather_send, gather_recv
    )
    begin()
    first(2)
    first(3)
    step(1, 0)
    relay()
    for n in range(len(turned)):
        turns[n] = across[n][...].T
    for i in range(split, count):
        hold(i).start()
        for n in range(3):
            hand_out(i, n).start()
    lax.fori_loop(2, 3, step, 0)
    others()
    diagonal()
    lax.fori_loop(3, nc, step, 0)
    finish()
    pltpu.make_async_copy(rest.at[f], rest.at[f], keep.at[1]).wait()
    for n in range(3):
        where = rest.at[near[n]]
        remote(where, where, send.at[0], recv.at[3 + n], {"fsdp": near[n]}).wait_recv()
    for i in range(count):
        for n in range(3):
            hand_out(i, n).wait_send()
    end()


def start(tokens, small, weights, split, turned, collective_id):
    nf, nc = lax.axis_size("fsdp"), lax.axis_size("ctx")
    rows, width = tokens.shape
    rows //= lax.axis_size("tp")
    depth = weights[0].shape[0]
    sizes = [w.size // depth // nf for w in weights]
    anywhere = pl.BlockSpec(memory_space=pl.ANY)
    count = nf * nc
    return call(
        functools.partial(start_kernel, sizes, split, turned),
        collective_id,
        [
            (jax.ShapeDtypeStruct((width, sum(sizes[:split])), bf16), pl.ANY),
            (jax.ShapeDtypeStruct((nf, depth, sum(sizes[split:])), bf16), pl.ANY),
            (jax.ShapeDtypeStruct((8, rows, width), bf16), pl.ANY),
            (jax.ShapeDtypeStruct((count, *small.shape), f32), pltpu.VMEM),
        ],
        [vmem(), vmem()]
        + [vmem() if i in turned else anywhere for i in range(len(weights))],
        [
            pltpu.VMEM((len(turned), depth, sizes[turned[0]] * nf), bf16),
            pltpu.VMEM((8, width), f32),
            pltpu.VMEM((rows, width), bf16),
            pltpu.VMEM((rows, width), bf16),
            *gather_scratch(tokens)[1:],
            *line_scratch(),
            pltpu.SemaphoreType.DMA((2,)),
            pltpu.SemaphoreType.DMA((3 * len(weights),)),
            pltpu.SemaphoreType.DMA((6,)),
            pltpu.SemaphoreType.DMA((count,)),
            pltpu.SemaphoreType.DMA((count,)),
        ],
        tokens,
        small,
        *weights,
    )


def total_kernel(parts, out, slots, send, recv):
    nc, nt = lax.axis_size("ctx"), lax.axis_size("tp")
    count = parts.shape[0]
    place = (lax.axis_index("fsdp") * nc + lax.axis_index("ctx")) * nt + lax.axis_index("tp")
    barrier = pltpu.get_barrier_semaphore()

    def hello(i, carry):
        other = peer_of(lax.rem(place + i, count), nc, nt)
        pl.semaphore_signal(barrier, inc=1, device_id=other, device_id_type=MESH)
        return carry

    lax.fori_loop(1, count, hello, 0)
    pl.semaphore_wait(barrier, count - 1)

    def copy(i):
        other = lax.rem(place + i, count)
        return remote(
            parts.at[other], slots.at[i], send.at[i], recv.at[i], peer_of(other, nc, nt)
        )

    def go(i, carry):
        copy(i).start()
        return carry

    lax.fori_loop(1, count, go, 0)

    def add(i, carry):
        copy(i).wait()
        return carry + slots[i]

    out[...] = lax.fori_loop(1, count, add, parts[place])


def total_small(parts, collective_id):
    count = parts.shape[0]
    return pl.pallas_call(
        total_kernel,
        out_shape=jax.ShapeDtypeStruct(parts.shape[1:], parts.dtype),
        in_specs=[pl.BlockSpec(memory_space=pltpu.VMEM)],
        out_specs=pl.BlockSpec(memory_space=pltpu.VMEM),
        scratch_shapes=[
            pltpu.VMEM(parts.shape, parts.dtype),
            pltpu.SemaphoreType.DMA((count,)),
            pltpu.SemaphoreType.DMA((count,)),
        ],
        compiler_params=pltpu.CompilerParams(collective_id=collective_id, has_side_effects=True),
        cost_estimate=pl.CostEstimate(flops=0, bytes_accessed=1_000_000, transcendentals=0),
    )(parts)


def both_halves(own, t):
    other = lax.ppermute(own, "tp", [(0, 1), (1, 0)])
    return jnp.where(t == 0, jnp.concatenate([own, other]), jnp.concatenate([other, own]))


def shards(
    tokens,
    lengths,
    cotangent,
    pre_gain,
    pre_bias,
    query_weight,
    key_weight,
    value_weight,
    swish_weight,
    out_weight,
    group_gain,
    group_bias,
    mlp_gain,
    mlp_bias,
    gelu_weight,
    up_weight,
    down_weight,
):
    seq_count, span, width = tokens.shape
    nf, nc, nt = lax.axis_size("fsdp"), lax.axis_size("ctx"), lax.axis_size("tp")
    f, c, t = lax.axis_index("fsdp"), lax.axis_index("ctx"), lax.axis_index("tp")
    block_rows = seq_count * span
    own_rows = block_rows // nt
    depth = query_weight.shape[0]
    heads_local = group_gain.shape[0]
    assert heads_local == nf
    key_size = query_weight.shape[1] // heads_local
    value_size = value_weight.shape[1] // heads_local
    hidden_size = gelu_weight.shape[1] // nf
    seqs = nf * seq_count
    rows = seqs * span
    head = t * heads_local + f

    def pad_tile(v):
        return jnp.pad(v, [(0, 0)] * (v.ndim - 1) + [(0, -v.shape[-1] % 1024)]).reshape(
            *v.shape[:-1], 8, -1
        )

    def own_part(v):
        return lax.dynamic_slice_in_dim(v.reshape(block_rows, width), t * own_rows, own_rows, 0)

    def all_depths(mine):
        return lax.all_gather(mine, "ctx", axis=0, tiled=True).reshape(width, -1)

    def padded(v):
        return jnp.pad(v.astype(f32).reshape(-1), (0, 128 - v.size))

    kinds = [pre_gain, pre_bias, mlp_gain, mlp_bias, group_gain, group_bias, lengths]
    small = jnp.stack([padded(v) for v in kinds] + [jnp.zeros(128, f32)])
    weights = [query_weight, key_weight, value_weight, swish_weight]
    weights += [out_weight, gelu_weight, up_weight, down_weight]
    attn_w, rest, normed, small = start(
        tokens.reshape(block_rows, width), small, weights, 4, (4, 7), 0
    )
    small, tokens, cotangent = lax.optimization_barrier((small, tokens, cotangent))
    normed = normed.reshape(rows, width)
    out_t = all_depths(rest[..., :value_size])
    pre_gain_full, pre_bias_full, mlp_gain_full, mlp_bias_full = (
        small[:, i, :depth].reshape(width) for i in range(4)
    )
    group = small[:, 4:6, : group_gain.size].reshape(nf * nc, 2, heads_local, -1)
    group = lax.dynamic_index_in_dim(group, f, 2, False).transpose(1, 0, 2).reshape(2, value_size)
    all_lengths = small.reshape(nf, nc, 8, 128)[:, 0, 6, :seq_count].reshape(seqs)

    inputs = own_part(tokens).astype(f32)
    _, norm_in_back = jax.vjp(layer_norm, inputs, pre_gain_full, pre_bias_full)
    positions = c * span + lax.iota(jnp.int32, span)
    own_ids = t * own_rows + lax.iota(jnp.int32, own_rows)
    own_valid = (c * span + own_ids % span < lengths[own_ids // span]).astype(f32)[:, None]
    error = own_valid * own_part(cotangent).astype(f32)

    pre = product(normed, attn_w)
    valid = (positions.astype(f32)[None, :] < all_lengths[:, None]).astype(f32)[:, :, None]
    cosine, sine = turn_tables(positions, key_size // 2)
    key_scale = key_size ** (-0.5)
    query_pre = pre[:, :key_size].reshape(seqs, span, key_size)
    key_pre = pre[:, key_size : 2 * key_size].reshape(seqs, span, key_size)
    value_pre = pre[:, 2 * key_size : 2 * key_size + value_size]
    swish_pre = pre[:, 2 * key_size + value_size :]
    queries = rotate(query_pre, cosine, sine).astype(bf16)
    keys = (rotate(key_pre, cosine, sine) * key_scale * valid).astype(bf16)
    values = value_pre.astype(bf16).reshape(seqs, span, value_size)

    log_decay = jnp.log1p(-jnp.exp2(-5.0 - head.astype(f32)))
    offsets = jnp.arange(span)
    distance = (offsets[:, None] - offsets[None, :]).astype(f32)
    within_fade = jnp.where(distance >= 0, jnp.exp(jnp.maximum(distance, 0.0) * log_decay), 0.0)
    key_fade = jnp.exp((span - 1 - offsets).astype(f32) * log_decay)[:, None]
    query_fade = jnp.exp((offsets + 1).astype(f32) * log_decay)[:, None]
    block_fade = jnp.exp(span * log_decay)

    keys_faded = (keys.astype(f32) * key_fade).astype(bf16)
    queries_faded = (queries.astype(f32) * query_fade).astype(bf16)
    local_state = blocks("sjd,sje->sde", keys_faded, values)
    error_low = error.astype(bf16)
    entering, error_all = pass_and_gather(local_state, block_fade, error_low, 1, 2)
    rest, entering = lax.optimization_barrier((rest, entering))
    ff_w = all_depths(rest[..., value_size:])
    gelu_up = ff_w[:, : 2 * hidden_size]
    down_t = ff_w[:, 2 * hidden_size :]
    probs = (blocks("sid,sjd->sij", queries, keys) * within_fade).astype(bf16)
    mixed = blocks("sij,sje->sie", probs, values) + blocks("sid,sde->sie", queries_faded, entering)
    gated_wide, gate_back = jax.vjp(
        gate_mix, mixed.reshape(rows, value_size), swish_pre, group[0], group[1]
    )
    gated = gated_wide.astype(bf16)
    branch = scatter_product(gated, out_t, 0, 1)
    hidden = inputs + branch

    mlp_wide, norm_mid_back = jax.vjp(layer_norm, hidden, mlp_gain_full, mlp_bias_full)
    mlp_in = gather_rows(mlp_wide.astype(bf16), 4)
    pre_ff = product(mlp_in, gelu_up)
    inner_wide, mix_back = jax.vjp(mlp_mix, pre_ff[:, :hidden_size], pre_ff[:, hidden_size:])
    inner = inner_wide.astype(bf16)

    def sum_depths(grads):
        grads = with_layout_constraint(grads.astype(bf16), Layout((0, 1)))
        mine = lax.psum_scatter(grads, "ctx", scatter_dimension=0, tiled=True)
        return mine.reshape(nf, depth, -1)

    def all_heads(mine):
        return lax.all_to_all(mine, "fsdp", 0, 0, tiled=True).astype(f32)

    def along(grads):
        return grads.transpose(1, 0, 2).reshape(depth, -1)

    def across(grads):
        return grads.transpose(0, 2, 1).reshape(-1, depth)

    down_part = product_left(error_all, inner).astype(bf16)
    down_part, down_t = lax.optimization_barrier((down_part, down_t))
    down_sum = sum_depths(down_part)
    gelu_grad, up_grad = mix_back(product(error_all, down_t))
    ff_low = jnp.concatenate([gelu_grad.astype(bf16), up_grad.astype(bf16)], -1)
    grad_gelu_up = product_left(mlp_in, ff_low)
    ff_parts = grad_gelu_up.astype(bf16)
    ff_parts, ff_low = lax.optimization_barrier((ff_parts, ff_low))
    ff_sum = sum_depths(ff_parts)
    mlp_in_grad = scatter_product(ff_low, ff_w, 0, 6)
    hidden_norm_grad, grad_mlp_gain, grad_mlp_bias = norm_mid_back(mlp_in_grad)
    hidden_grad = error + hidden_norm_grad

    hidden_low = gather_rows(hidden_grad.astype(bf16), 4)
    grad_out_t = product_left(hidden_low, gated)
    gated_grad = product(hidden_low, out_t)
    mixed_grad, swish_grad, grad_group_gain, grad_group_bias = gate_back(gated_grad)
    swish_low = swish_grad.astype(bf16)
    mixed_low = mixed_grad.astype(bf16).reshape(seqs, span, value_size)
    score_low = (blocks("sie,sje->sij", mixed_low, values) * within_fade).astype(bf16)
    pulled_state = blocks("sid,sie->sde", queries_faded, mixed_low)
    out_sum = sum_depths(grad_out_t)
    swish_part = product_left(normed, swish_low).astype(bf16)
    swish_part, pulled_state, ff_sum, down_sum = lax.optimization_barrier(
        (swish_part, pulled_state, ff_sum, down_sum)
    )
    later, mlp_out = pass_and_scatter(
        pulled_state, block_fade, inner, ff_w, 2 * hidden_size, -1, 3
    )
    swish_part, later, out_sum = lax.optimization_barrier((swish_part, later, out_sum))
    swish_sum = sum_depths(swish_part)
    block_own = (own_valid * (hidden + mlp_out)).astype(bf16)
    block_out = both_halves(block_own, t).reshape(tokens.shape)
    query_grad = blocks("sij,sjd->sid", score_low, keys) + query_fade * blocks(
        "sie,sde->sid", mixed_low, entering
    )
    key_grad = blocks("sij,sid->sjd", score_low, queries) + key_fade * blocks(
        "sje,sde->sjd", values, later
    )
    value_grad = blocks("sij,sie->sje", probs, mixed_low) + blocks(
        "sjd,sde->sje", keys_faded, later
    )
    query_low = rotate_back(query_grad, cosine, sine).astype(bf16).reshape(rows, key_size)
    key_low = rotate_back(key_grad * key_scale * valid, cosine, sine).astype(bf16)
    low = jnp.concatenate(
        [
            query_low,
            key_low.reshape(rows, key_size),
            value_grad.astype(bf16).reshape(rows, value_size),
        ],
        -1,
    )
    attn_part = product_left(normed, low).astype(bf16)
    attn_part, low = lax.optimization_barrier((attn_part, low))
    attn_sum = sum_depths(attn_part)
    low = jnp.concatenate([low, swish_low], -1)
    normed_grad = scatter_product(low, attn_w, 0, 7)
    swish_sum, normed_grad = lax.optimization_barrier((swish_sum, normed_grad))
    input_norm_grad, grad_pre_gain, grad_pre_bias = norm_in_back(normed_grad)
    tokens_own = (hidden_grad + input_norm_grad).astype(bf16)
    grad_tokens = both_halves(tokens_own, t).reshape(tokens.shape)

    norm_parts = jnp.stack([grad_pre_gain, grad_pre_bias, grad_mlp_gain, grad_mlp_bias])
    norm_parts = norm_parts.reshape(4, nf * nc, 1, depth).transpose(1, 2, 0, 3)
    norm_parts = jnp.broadcast_to(norm_parts, (nf * nc, nt, 4, depth)).reshape(nf * nc, nt, -1)
    mine = lax.iota(jnp.int32, nt * heads_local) == head
    group_parts = jnp.stack([grad_group_gain, grad_group_bias]).reshape(1, 2, nf * nc, -1)
    group_parts = jnp.where(mine[:, None, None, None], group_parts, 0.0)
    group_parts = group_parts.reshape(nt, heads_local, 2, nf * nc, -1).transpose(3, 0, 2, 1, 4)
    parts = jnp.concatenate([norm_parts, group_parts.reshape(nf * nc, nt, -1)], -1)
    parts = parts.reshape(nf * nc * nt, -1)
    sums = total_small(pad_tile(parts), 5).reshape(-1)[: parts.shape[1]]
    sums, attn_sum = lax.optimization_barrier((sums, attn_sum))
    ready_sums = jnp.concatenate([ff_sum, down_sum, out_sum], -1)
    ff_grads = all_heads(ready_sums)
    attn_grads = all_heads(jnp.concatenate([swish_sum, attn_sum], -1))
    norm_sums = sums[: 4 * depth].reshape(4, depth)
    group_sums = sums[4 * depth :].reshape(2, heads_local, -1)

    at = [value_size, value_size + key_size, value_size + 2 * key_size]
    return (
        block_out,
        grad_tokens,
        norm_sums[0],
        norm_sums[1],
        along(attn_grads[..., at[0] : at[1]]),
        along(attn_grads[..., at[1] : at[2]]),
        along(attn_grads[..., at[2] :]),
        along(attn_grads[..., : at[0]]),
        across(ff_grads[..., 3 * hidden_size :]),
        group_sums[0],
        group_sums[1],
        norm_sums[2],
        norm_sums[3],
        along(ff_grads[..., :hidden_size]),
        along(ff_grads[..., hidden_size : 2 * hidden_size]),
        across(ff_grads[..., 2 * hidden_size : 3 * hidden_size]),
    )


def solution(mesh):
    rows = P("fsdp", "ctx", None)
    vector = P(("fsdp", "ctx"))
    tall = P(("fsdp", "ctx"), "tp")
    wide = P("tp", ("fsdp", "ctx"))
    in_specs = (rows, P("fsdp"), rows, vector, vector, tall, tall, tall, tall, wide)
    in_specs += (wide, wide, vector, vector, tall, tall, wide)
    out_specs = (rows, rows, vector, vector, tall, tall, tall, tall, wide)
    out_specs += (wide, wide, vector, vector, tall, tall, wide)
    return jax.shard_map(shards, mesh=mesh, in_specs=in_specs, out_specs=out_specs, check_vma=False)
```

```python
import functools

import jax
import jax.numpy as jnp
from jax import lax
from jax.experimental import pallas as pl
from jax.experimental.layout import Layout, with_layout_constraint
from jax.experimental.pallas import tpu as pltpu
from jax.sharding import PartitionSpec as P

eps = 1e-05
group_floor = 1.0
f32 = jnp.float32
bf16 = jnp.bfloat16


def layer_norm(values, norm_gain, norm_shift):
    centred = values - jnp.mean(values, -1, keepdims=True)
    spread = jnp.mean(centred * centred, -1, keepdims=True)
    return centred * lax.rsqrt(spread + eps) * norm_gain + norm_shift


def turn_tables(positions, half_size):
    frequency = jnp.power(10000.0, -jnp.arange(half_size).astype(f32) / half_size)
    angles = positions.astype(f32)[:, None] * frequency[None, :]
    return jnp.cos(angles), jnp.sin(angles)


def rotate(values, cosine, sine):
    half_size = values.shape[-1] // 2
    first = values[..., :half_size]
    second = values[..., half_size:]
    return jnp.concatenate([first * cosine - second * sine, second * cosine + first * sine], -1)


def rotate_back(values, cosine, sine):
    return rotate(values, cosine, -sine)


def gate_mix(mixed, swish_pre, norm_gain, norm_shift):
    centred = mixed - jnp.mean(mixed, -1, keepdims=True)
    spread = jnp.mean(centred * centred, -1, keepdims=True)
    return jax.nn.silu(swish_pre) * (
        centred * lax.rsqrt(spread + group_floor) * norm_gain + norm_shift
    )


def mlp_mix(gelu_pre, up_pre):
    return jax.nn.gelu(gelu_pre) * up_pre


def product(left, right):
    return jnp.dot(left, right, preferred_element_type=f32)


def product_left(left, right):
    return lax.dot_general(left, right, (((0,), (0,)), ((), ())), preferred_element_type=f32)


def product_right(left, right):
    return lax.dot_general(left, right, (((1,), (1,)), ((), ())), preferred_element_type=f32)


def blocks(spec, left, right):
    return jnp.einsum(spec, left, right, preferred_element_type=f32)


MESH = pl.DeviceIdType.MESH


def beside(f):
    return f + 1 - 2 * (f % 2), (f + 2) % 4, 3 - f


def remote(src, dst, send, recv, device):
    return pltpu.make_async_remote_copy(
        src_ref=src, dst_ref=dst, send_sem=send, recv_sem=recv, device_id=device, device_id_type=MESH
    )


def reorder(src, dst, kind, back):
    nf, nc = lax.axis_size("fsdp"), lax.axis_size("ctx")
    depth = src.shape[-1] // (nf * nc)
    for f in range(nf):
        for c in range(nc):
            plain, mixed = (f * nc + c) * depth, (c * nf + f) * depth
            if back:
                plain, mixed = mixed, plain
            dst[:, mixed : mixed + depth] = src[:, plain : plain + depth].astype(kind)


def gather_steps(plain, out, mixed, keep, send, recv):
    own = plain if mixed is None else mixed
    f, t = lax.axis_index("fsdp"), lax.axis_index("tp")
    fx, fy, fd = beside(f)
    x, y, core = {"fsdp": fx}, {"fsdp": fy}, {"tp": 1 - t}
    half = own.shape[0] // 2

    def part(ref, h):
        return ref.at[pl.ds(h * half, half)]

    def slot(who, h):
        return part(out.at[2 * who + t], h)

    local = pltpu.make_async_copy(own, out.at[2 * f + t], keep)
    first = [
        remote(part(own, 0), slot(f, 0), send.at[0], recv.at[0], x),
        remote(part(own, 1), slot(f, 1), send.at[1], recv.at[3], y),
        remote(part(own, 1), slot(f, 1), send.at[2], recv.at[1], x),
        remote(part(own, 0), slot(f, 0), send.at[3], recv.at[2], y),
        remote(part(own, 0), slot(f, 0), send.at[4], recv.at[6], core),
        remote(part(own, 1), slot(f, 1), send.at[5], recv.at[7], core),
    ]
    sent = list(first)

    def pass_on(who, h, s, r, device):
        copy = remote(slot(who, h), slot(who, h), send.at[s], recv.at[r], device)
        copy.start()
        sent.append(copy)

    def begin():
        if mixed is not None:
            reorder(plain, mixed, mixed.dtype, False)
        local.start()
        for copy in first:
            copy.start()

    def relay():
        first[0].wait_recv()
        pass_on(fx, 0, 6, 4, y)
        pass_on(fx, 0, 7, 8, core)
        first[1].wait_recv()
        pass_on(fy, 1, 8, 5, x)
        pass_on(fy, 1, 9, 11, core)

    def rest():
        first[2].wait_recv()
        pass_on(fx, 1, 10, 9, core)
        first[3].wait_recv()
        pass_on(fy, 0, 11, 10, core)

    def diagonal():
        remote(slot(fd, 0), slot(fd, 0), send.at[12], recv.at[4], y).wait_recv()
        pass_on(fd, 0, 12, 12, core)
        remote(slot(fd, 1), slot(fd, 1), send.at[13], recv.at[5], x).wait_recv()
        pass_on(fd, 1, 13, 13, core)

    def end(crossed=False):
        if not crossed:
            for r in range(6, 14):
                remote(slot(f, 0), slot(f, 0), send.at[0], recv.at[r], core).wait_recv()
            local.wait()
        for copy in sent:
            copy.wait_send()

    return begin, relay, rest, diagonal, end


def in_kernel(width):
    return width // (lax.axis_size("fsdp") * lax.axis_size("ctx")) % 128 == 0


def gather_scratch(own):
    return [
        pltpu.VMEM(own.shape if in_kernel(own.shape[1]) else (16, 128), own.dtype),
        pltpu.SemaphoreType.DMA,
        pltpu.SemaphoreType.DMA((14,)),
        pltpu.SemaphoreType.DMA((14,)),
    ]


def scatter_steps(start, lefts, right, out, mine, sent, theirs, total, diag, last, send, recv):
    f, t = lax.axis_index("fsdp"), lax.axis_index("tp")
    fx, fy, fd = beside(f)
    x, y, core = {"fsdp": fx}, {"fsdp": fy}, {"tp": 1 - t}
    half = out.shape[0] // 2
    order = [fd, fy, fx, f]
    tile = 512

    def part(ref, h):
        return ref.at[pl.ds(h * half, half)]

    crossing = [
        remote(sent.at[i], theirs.at[i], send.at[i], recv.at[i], core) for i in range(4)
    ]
    d0 = remote(part(total.at[0], 0), diag.at[0], send.at[4], recv.at[4], x)
    d1 = remote(part(total.at[0], 1), diag.at[1], send.at[5], recv.at[5], y)
    y1 = remote(part(total.at[1], 1), part(last.at[1], 1), send.at[6], recv.at[6], y)
    x0 = remote(part(total.at[2], 0), part(last.at[0], 0), send.at[7], recv.at[7], x)
    y0 = remote(part(total.at[1], 0), part(last.at[1], 0), send.at[8], recv.at[8], y)
    x1 = remote(part(total.at[2], 1), part(last.at[0], 1), send.at[9], recv.at[9], x)

    def make(block, put):
        def piece(j, carry):
            columns = pl.ds(pl.multiple_of(j * tile, tile), tile)
            at, value = start, 0.0
            for left in lefts:
                size = left.shape[2]
                value += product_right(left[block], right[columns, at : at + size])
                at += size
            put(columns, value)
            return carry

        lax.fori_loop(0, out.shape[1] // tile, piece, 0)

    def cross(i):
        def put(columns, value):
            sent[i, :, columns] = value.astype(sent.dtype)

        make(2 * order[i] + 1 - t, put)
        crossing[i].start()

    def keep(i):
        def put(columns, value):
            mine[:, columns] = value

        make(2 * order[i] + t, put)

    def add(i):
        keep(i)
        crossing[i].wait_recv()
        total[i] = (mine[...] + theirs[i].astype(f32)).astype(total.dtype)

    def diagonal():
        cross(0)
        cross(1)
        add(0)
        d0.start()
        d1.start()

    def straight():
        cross(2)
        add(1)
        y1.start()
        add(2)
        x0.start()
        cross(3)

    def relay():
        d0.wait_recv()
        total[1, :half] = (total[1, :half].astype(f32) + diag[0].astype(f32)).astype(total.dtype)
        y0.start()
        d1.wait_recv()
        total[2, half:] = (total[2, half:].astype(f32) + diag[1].astype(f32)).astype(total.dtype)
        x1.start()
        keep(3)
        crossing[3].wait_recv()
        mine[...] += theirs[3].astype(f32)

    def end():
        for copy in (y1, x0, y0, x1):
            copy.wait_recv()
        mine[...] += last[0].astype(f32) + last[1].astype(f32)
        if in_kernel(out.shape[1]):
            reorder(mine, out, out.dtype, True)
        else:
            out[...] = mine[...]
        for copy in (*crossing, d0, d1, y1, x0, y0, x1):
            copy.wait_send()

    return diagonal, straight, relay, end


def scatter_scratch(rows, width):
    return [
        pltpu.VMEM((rows, width), f32),
        pltpu.VMEM((4, rows, width), bf16),
        pltpu.VMEM((4, rows, width), bf16),
        pltpu.VMEM((3, rows, width), bf16),
        pltpu.VMEM((2, rows // 2, width), bf16),
        pltpu.VMEM((2, rows, width), bf16),
        pltpu.SemaphoreType.DMA((10,)),
        pltpu.SemaphoreType.DMA((10,)),
    ]


def pass_steps(by, local, fade, out, held, send, recv):
    length = lax.axis_size("ctx")
    c = lax.axis_index("ctx")
    first = c == (0 if by > 0 else length - 1)
    last = c == (length - 1 if by > 0 else 0)
    target = lax.rem(c + by + length, length)

    def copy(p):
        return remote(held.at[p], out.at[p], send.at[p], recv.at[p], {"ctx": target})

    def step(p, carry):
        @pl.when(first)
        def _():
            out[p] = jnp.zeros(out.shape[1:], out.dtype)

        @pl.when(jnp.logical_not(first))
        def _():
            copy(p).wait_recv()

        @pl.when(jnp.logical_not(last))
        def _():
            held[p] = (fade[...] * out[p].astype(f32) + local[p]).astype(held.dtype)
            copy(p).start()

        return carry

    def run(quarter):
        count = local.shape[0]
        low = 0 if quarter == 0 else jnp.where(first, count, quarter * count // 4)
        lax.fori_loop(low, jnp.where(first, count, (quarter + 1) * count // 4), step, 0)

    def end():
        @pl.when(jnp.logical_not(last))
        def _():
            def done(p, carry):
                copy(p).wait_send()
                return carry

            lax.fori_loop(0, local.shape[0], done, 0)

    return run, end


def greet_plane(by=0, diagonal=False):
    f, c, t = lax.axis_index("fsdp"), lax.axis_index("ctx"), lax.axis_index("tp")
    length = lax.axis_size("ctx")
    fx, fy, fd = beside(f)
    barrier = pltpu.get_barrier_semaphore()
    peers = [{"fsdp": fx}, {"fsdp": fy}, {"tp": 1 - t}] + [{"fsdp": fd}] * diagonal
    for device in peers:
        pl.semaphore_signal(barrier, inc=1, device_id=device, device_id_type=MESH)
    if by != 0:
        first = c == (0 if by > 0 else length - 1)
        last = c == (length - 1 if by > 0 else 0)
        source = {"ctx": lax.rem(c - by + length, length)}

        @pl.when(jnp.logical_not(first))
        def _():
            pl.semaphore_signal(barrier, inc=1, device_id=source, device_id_type=MESH)

        @pl.when(jnp.logical_not(last))
        def _():
            pl.semaphore_wait(barrier, len(peers) + 1)

        @pl.when(last)
        def _():
            pl.semaphore_wait(barrier, len(peers))
    else:
        pl.semaphore_wait(barrier, len(peers))


def gather_with(own, full, mixed, *scratch):
    return gather_steps(own, full, mixed if in_kernel(own.shape[1]) else None, *scratch)


def gather_kernel(*refs):
    steps = gather_with(*refs)
    greet_plane()
    for step in steps:
        step()


def scatter_kernel(count, start, *refs):
    steps = scatter_steps(start, refs[:count], *refs[count:])
    greet_plane()
    for step in steps:
        step()


def gather_products_kernel(own, left, right, grad, back, full, total, mixed, *scratch):
    f, t = lax.axis_index("fsdp"), lax.axis_index("tp")
    fx, fy, fd = beside(f)
    recv = scratch[2]
    begin, relay, rest, diagonal, end = gather_with(own, full, mixed, *scratch)
    tile = 512

    def use(block, fresh=False):
        back[block] = product(full[block], right[...])

        def piece(j, carry):
            columns = pl.ds(pl.multiple_of(j * tile, tile), tile)
            value = product_left(full[block, :, columns], left[block])
            total[columns, :] = value if fresh else total[columns, :] + value
            return carry

        lax.fori_loop(0, total.shape[0] // tile, piece, 0)

    def crossed(who, r):
        block = full.at[2 * who + 1 - t]
        half = block.shape[0] // 2
        for h in range(2):
            where = block.at[pl.ds(h * half, half)]
            remote(where, where, scratch[1].at[0], recv.at[r + h], {"tp": 1 - t}).wait_recv()

    greet_plane()
    begin()
    pltpu.make_async_copy(full.at[2 * f + t], full.at[2 * f + t], scratch[0]).wait()
    use(2 * f + t, True)
    relay()
    crossed(f, 6)
    use(2 * f + 1 - t)
    rest()
    use(2 * fx + t)
    use(2 * fy + t)
    crossed(fx, 8)
    use(2 * fx + 1 - t)
    crossed(fy, 10)
    use(2 * fy + 1 - t)
    diagonal()
    use(2 * fd + t)
    crossed(fd, 12)
    use(2 * fd + 1 - t)
    end(True)
    grad[...] = total[...].astype(grad.dtype)


def gather_products(own, left, right, collective_id):
    own = ready(own)
    rows, width = own.shape
    size = left.shape[1]
    grad, back = call(
        gather_products_kernel,
        collective_id,
        [
            (jax.ShapeDtypeStruct((width, size), bf16), pltpu.VMEM),
            (jax.ShapeDtypeStruct((8, rows, size), f32), pltpu.VMEM),
        ],
        [vmem()] * 3,
        [
            pltpu.VMEM((8, rows, width), bf16),
            pltpu.VMEM((width, size), f32),
            *gather_scratch(own),
        ],
        own,
        in_eights(left),
        right,
    )
    return grad, back.reshape(8 * rows, size)


def pass_gather_kernel(by, local, fade, own, out, full, held, send, recv, *scratch):
    begin, relay, rest, diagonal, end = gather_with(own, full, *scratch)
    run, done = pass_steps(by, local, fade, out, held, send, recv)
    greet_plane(by)
    begin()
    run(0)
    relay()
    run(1)
    rest()
    run(2)
    run(3)
    diagonal()
    end()
    done()


def pass_scatter_kernel(by, start, local, fade, left, right, ff, down, out, own, *refs):
    gelu_grad, up_grad, down_grad, held, send, recv = refs[:6]
    scratch, hand = refs[6:-3], refs[-3:]
    targets = [[(gelu_grad, False), (up_grad, False)], [(down_grad, True)]]
    hand_over, take = hand_steps([ff, down], targets, *hand)
    diagonal, straight, relay, end = scatter_steps(start, [left], right, own, *scratch)
    run, done = pass_steps(by, local, fade, out, held, send, recv)
    greet_plane(by, True)
    run(0)
    diagonal()
    run(1)
    straight()
    run(2)
    relay()
    hand_over()
    run(3)
    end()
    take()
    done()


def call(kernel, collective_id, outs, ins, scratch, *args):
    shapes, spaces = zip(*outs)
    return pl.pallas_call(
        kernel,
        out_shape=shapes,
        in_specs=ins,
        out_specs=tuple(pl.BlockSpec(memory_space=space) for space in spaces),
        scratch_shapes=scratch,
        compiler_params=pltpu.CompilerParams(
            collective_id=collective_id, has_side_effects=True, vmem_limit_bytes=52 << 20
        ),
        cost_estimate=pl.CostEstimate(flops=0, bytes_accessed=2_000_000, transcendentals=0),
    )(*args)


def vmem():
    return pl.BlockSpec(memory_space=pltpu.VMEM)


def perm(v):
    nf, nc = lax.axis_size("fsdp"), lax.axis_size("ctx")
    return v.reshape(len(v), nf, nc, -1).transpose(0, 2, 1, 3).reshape(v.shape)


def unperm(v):
    nf, nc = lax.axis_size("fsdp"), lax.axis_size("ctx")
    return v.reshape(len(v), nc, nf, -1).transpose(0, 2, 1, 3).reshape(v.shape)


def gathered(own):
    rows, width = own.shape
    return jax.ShapeDtypeStruct((8, rows, width), own.dtype), pl.ANY


def scattered(left, right):
    return jax.ShapeDtypeStruct((left.shape[0] // 8, right.shape[0]), f32), pltpu.VMEM


def passed(local):
    return jax.ShapeDtypeStruct(local.shape, bf16), pltpu.VMEM


def pass_scratch(local):
    pieces = local.shape[0]
    return [
        pltpu.VMEM(local.shape, bf16),
        pltpu.SemaphoreType.DMA((pieces,)),
        pltpu.SemaphoreType.DMA((pieces,)),
    ]


def in_eights(left):
    return left.reshape(8, -1, left.shape[1])


def ready(own):
    return own if in_kernel(own.shape[1]) else perm(own)


def plain(own):
    return own if in_kernel(own.shape[1]) else unperm(own)


def gather_rows(own, collective_id):
    own = ready(own)
    (out,) = call(gather_kernel, collective_id, [gathered(own)], [vmem()], gather_scratch(own), own)
    return out.reshape(-1, own.shape[1])


def scatter_product(lefts, right, start, collective_id):
    rows, width = lefts[0].shape[0] // 8, right.shape[0]
    (out,) = call(
        functools.partial(scatter_kernel, len(lefts), start),
        collective_id,
        [(jax.ShapeDtypeStruct((rows, width), f32), pltpu.VMEM)],
        [vmem()] * (len(lefts) + 1),
        scatter_scratch(rows, width),
        *(in_eights(left) for left in lefts),
        right,
    )
    return plain(out)


def pass_and_gather(local, fade, own, by, collective_id):
    shape = local.shape
    local = local.reshape(2 * shape[0], -1, shape[2])
    own = ready(own)
    out, full = call(
        functools.partial(pass_gather_kernel, by),
        collective_id,
        [passed(local), gathered(own)],
        [vmem(), vmem(), vmem()],
        pass_scratch(local) + gather_scratch(own),
        local,
        jnp.full((1, local.shape[2]), fade, f32),
        own,
    )
    return out.reshape(shape), full.reshape(-1, own.shape[1])


def pass_and_scatter(local, fade, left, right, start, ff, down, by, collective_id):
    shape = local.shape
    local = local.reshape(2 * shape[0], -1, shape[2])
    out, own, *grads = call(
        functools.partial(pass_scatter_kernel, by, start),
        collective_id,
        [
            passed(local),
            scattered(left, right),
            *handed(ff, [down.shape[2]] * 2),
            *handed(down, [down.shape[2]], True),
        ],
        [vmem()] * 6,
        pass_scratch(local)
        + scatter_scratch(left.shape[0] // 8, right.shape[0])
        + hand_scratch([ff, down]),
        local,
        jnp.full((1, local.shape[2]), fade, f32),
        in_eights(left),
        right,
        ff,
        down,
    )
    return out.reshape(shape), plain(own), *(grad.astype(f32) for grad in grads)


def peer_of(place, nc, nt):
    return {"fsdp": place // (nc * nt), "ctx": place // nt % nc, "tp": place % nt}


def line_steps(home, place, arrived, send, recv):
    nf, nc = lax.axis_size("fsdp"), lax.axis_size("ctx")
    f, c = lax.axis_index("fsdp"), lax.axis_index("ctx")
    order = [f, *beside(f)]
    above, below = c < nc - 1, c > 0

    def copy(src, place_of, who, up):
        chunk = place_of * nf + who
        return remote(
            src,
            place(place_of, who),
            send.at[chunk if up else nc * nf + chunk],
            recv.at[chunk],
            {"ctx": lax.rem(c + 1, nc) if up else lax.rem(c + nc - 1, nc)},
        )

    def first(i):
        who = order[i]
        arrived(i)

        @pl.when(above)
        def _():
            copy(home(who), c, who, True).start()

        @pl.when(below)
        def _():
            copy(home(who), c, who, False).start()

    def step(k, carry):
        for who in order:

            @pl.when(c - k >= 0)
            def _():
                copy(place(c - k, who), c - k, who, True).wait_recv()

                @pl.when(above)
                def _():
                    copy(place(c - k, who), c - k, who, True).start()

            @pl.when(c + k < nc)
            def _():
                copy(place(c + k, who), c + k, who, False).wait_recv()

                @pl.when(below)
                def _():
                    copy(place(c + k, who), c + k, who, False).start()

        return carry

    def end():
        def one(other, carry):
            for who in order:

                @pl.when(above & (other <= c))
                def _():
                    copy(place(other, who), other, who, True).wait_send()

                @pl.when(below & (other >= c))
                def _():
                    copy(place(other, who), other, who, False).wait_send()

            return carry

        lax.fori_loop(0, nc, one, 0)

    return first, step, end


def line_scratch():
    count = lax.axis_size("fsdp") * lax.axis_size("ctx")
    return [pltpu.SemaphoreType.DMA((2 * count,)), pltpu.SemaphoreType.DMA((count,))]


def start_kernel(sizes, split, turned, own, small, *refs):
    count = len(sizes)
    weights = list(refs[:count])
    attn, rest, full, everyone = refs[count : count + 4]
    (
        turns,
        gains,
        normed,
        mixed,
        gather_keep,
        gather_send,
        gather_recv,
        line_send,
        line_recv,
        keep,
        send,
        recv,
        small_send,
        small_recv,
    ) = refs[count + 4 :]
    nf, nc = lax.axis_size("fsdp"), lax.axis_size("ctx")
    f, c, t = lax.axis_index("fsdp"), lax.axis_index("ctx"), lax.axis_index("tp")
    here, places = f * nc + c, nf * nc
    depth = weights[0].shape[0]
    across = [weights[i] for i in turned]
    for n, i in enumerate(turned):
        weights[i] = turns.at[n]
    near = beside(f)
    starts = [sum(sizes[:i]) if i < split else sum(sizes[split:i]) for i in range(count)]

    def peer(i):
        other = lax.rem(here + i, places)
        return {"fsdp": other // nc, "ctx": other % nc}

    barrier = pltpu.get_barrier_semaphore()
    pl.semaphore_signal(barrier, inc=1, device_id={"tp": 1 - t}, device_id_type=MESH)

    def hello(i, carry):
        pl.semaphore_signal(barrier, inc=1, device_id=peer(i), device_id_type=MESH)
        return carry

    lax.fori_loop(1, places, hello, 0)
    pl.semaphore_wait(barrier, places)

    def chunk(place_of, who):
        rows = pl.multiple_of((place_of * nf + who) * depth, depth)
        return attn.at[pl.ds(rows, depth)]

    def columns(i, who):
        return weights[i].at[:, pl.ds(pl.multiple_of(who * sizes[i], sizes[i]), sizes[i])]

    def target(i):
        where = chunk(c, f) if i < split else rest.at[f]
        return where.at[:, pl.ds(starts[i], sizes[i])]

    def hand_out(i, n):
        return remote(
            columns(i, near[n]),
            target(i),
            send.at[3 * i + n],
            recv.at[n if i < split else 3 + n],
            {"fsdp": near[n]},
        )

    def hold(i):
        return pltpu.make_async_copy(columns(i, f), target(i), keep.at[0 if i < split else 1])

    for i in range(split):
        hold(i).start()
    for n in range(3):
        for i in range(split):
            hand_out(i, n).start()

    def arrived(i):
        if i == 0:
            pltpu.make_async_copy(chunk(c, f), chunk(c, f), keep.at[0]).wait()
        else:
            who = near[i - 1]
            remote(
                chunk(c, who), chunk(c, who), send.at[0], recv.at[i - 1], {"fsdp": who}
            ).wait_recv()

    first, step, end = line_steps(lambda who: chunk(c, who), chunk, arrived, line_send, line_recv)
    first(0)

    def tell(i):
        return remote(small, everyone.at[here], small_send.at[i], small_recv.at[i], peer(i))

    def go(i, carry):
        tell(i).start()
        return carry

    def told(i, carry):
        tell(i).wait()
        return carry

    lax.fori_loop(1, places, go, 0)
    everyone[here] = small[...]
    first(1)
    lax.fori_loop(1, places, told, 0)
    for i in range(places):
        for j in range(2):
            gains[j : j + 1, i * depth : (i + 1) * depth] = everyone[i, j : j + 1, :depth]
    rows = normed.shape[0]
    mine = own[pl.ds(pl.multiple_of(t * rows, rows), rows), :].astype(f32)
    normed[...] = layer_norm(mine, gains[0:1, :], gains[1:2, :]).astype(bf16)
    begin, relay, others, diagonal, finish = gather_steps(
        normed, full, mixed, gather_keep, gather_send, gather_recv
    )
    begin()
    first(2)
    first(3)
    step(1, 0)
    relay()
    for n in range(len(turned)):
        turns[n] = across[n][...].T
    for i in range(split, count):
        hold(i).start()
        for n in range(3):
            hand_out(i, n).start()
    lax.fori_loop(2, 3, step, 0)
    others()
    diagonal()
    lax.fori_loop(3, nc, step, 0)
    finish()
    pltpu.make_async_copy(rest.at[f], rest.at[f], keep.at[1]).wait()
    for n in range(3):
        where = rest.at[near[n]]
        remote(where, where, send.at[0], recv.at[3 + n], {"fsdp": near[n]}).wait_recv()
    for i in range(count):
        for n in range(3):
            hand_out(i, n).wait_send()
    end()


def start(tokens, small, weights, split, turned, collective_id):
    nf, nc = lax.axis_size("fsdp"), lax.axis_size("ctx")
    rows, width = tokens.shape
    rows //= lax.axis_size("tp")
    depth = weights[0].shape[0]
    sizes = [w.size // depth // nf for w in weights]
    anywhere = pl.BlockSpec(memory_space=pl.ANY)
    count = nf * nc
    return call(
        functools.partial(start_kernel, sizes, split, turned),
        collective_id,
        [
            (jax.ShapeDtypeStruct((width, sum(sizes[:split])), bf16), pl.ANY),
            (jax.ShapeDtypeStruct((nf, depth, sum(sizes[split:])), bf16), pl.ANY),
            (jax.ShapeDtypeStruct((8, rows, width), bf16), pl.ANY),
            (jax.ShapeDtypeStruct((count, *small.shape), f32), pltpu.VMEM),
        ],
        [vmem(), vmem()]
        + [vmem() if i in turned else anywhere for i in range(len(weights))],
        [
            pltpu.VMEM((len(turned), depth, sizes[turned[0]] * nf), bf16),
            pltpu.VMEM((8, width), f32),
            pltpu.VMEM((rows, width), bf16),
            pltpu.VMEM((rows, width), bf16),
            *gather_scratch(tokens)[1:],
            *line_scratch(),
            pltpu.SemaphoreType.DMA((2,)),
            pltpu.SemaphoreType.DMA((3 * len(weights),)),
            pltpu.SemaphoreType.DMA((6,)),
            pltpu.SemaphoreType.DMA((count,)),
            pltpu.SemaphoreType.DMA((count,)),
        ],
        tokens,
        small,
        *weights,
    )


def hand_steps(parts, outs, slots, send, recv):
    f = lax.axis_index("fsdp")
    near = beside(f)
    starts = [sum(part.shape[2] for part in parts[:i]) for i in range(len(parts))]

    def copies(n):
        return [
            remote(
                part.at[near[n]],
                slots.at[n, :, pl.ds(at, part.shape[2])],
                send.at[len(parts) * n + i],
                recv.at[len(parts) * n + i],
                {"fsdp": near[n]},
            )
            for i, (part, at) in enumerate(zip(parts, starts))
        ]

    def begin():
        for n in range(3):
            for copy in copies(n):
                copy.start()

    def put(who, blocks):
        for block, targets in zip(blocks, outs):
            at = 0
            for out, turned in targets:
                size = out.shape[0 if turned else 1] // lax.axis_size("fsdp")
                where = pl.ds(pl.multiple_of(who * size, size), size)
                if turned:
                    out[where, :] = block[:, at : at + size].T
                else:
                    out[:, where] = block[:, at : at + size]
                at += size

    def end():
        put(f, [part[f] for part in parts])
        for n in range(3):
            for copy in copies(n):
                copy.wait()
            put(
                near[n],
                [slots[n, :, at : at + part.shape[2]] for part, at in zip(parts, starts)],
            )

    return begin, end


def hand_scratch(parts):
    size = sum(part.shape[2] for part in parts)
    return [
        pltpu.VMEM((3, parts[0].shape[1], size), bf16),
        pltpu.SemaphoreType.DMA((3 * len(parts),)),
        pltpu.SemaphoreType.DMA((3 * len(parts),)),
    ]


def handed(part, sizes, turned=False):
    nf, depth = part.shape[:2]
    shapes = [(nf * n, depth) if turned else (depth, nf * n) for n in sizes]
    return [(jax.ShapeDtypeStruct(shape, bf16), pltpu.VMEM) for shape in shapes]


def finish_kernel(turned, counts, *refs):
    parts, outs, scratch = refs[: len(turned)], list(refs[len(turned) : -3]), refs[-3:]
    targets = [[(outs.pop(0), turn) for _ in range(n)] for turn, n in zip(turned, counts)]
    begin, end = hand_steps(parts, targets, *scratch)
    greet_fsdp()
    begin()
    end()


def greet_fsdp():
    near = beside(lax.axis_index("fsdp"))
    barrier = pltpu.get_barrier_semaphore()
    for who in near:
        pl.semaphore_signal(barrier, inc=1, device_id={"fsdp": who}, device_id_type=MESH)
    pl.semaphore_wait(barrier, 3)


def finish(parts, sizes, turned, collective_id):
    outs = [one for n in zip(parts, sizes, turned) for one in handed(*n)]
    outs = call(
        functools.partial(finish_kernel, turned, [len(size) for size in sizes]),
        collective_id,
        outs,
        [vmem()] * len(parts),
        hand_scratch(parts),
        *parts,
    )
    return [out.astype(f32) for out in outs]


def halves_kernel(own, out, keep, send, recv):
    t = lax.axis_index("tp")
    core = {"tp": 1 - t}
    barrier = pltpu.get_barrier_semaphore()
    pl.semaphore_signal(barrier, inc=1, device_id=core, device_id_type=MESH)
    pl.semaphore_wait(barrier, 1)
    copy = remote(own, out.at[t], send, recv, core)
    copy.start()
    local = pltpu.make_async_copy(own, out.at[t], keep)
    local.start()
    local.wait()
    copy.wait()


def both_halves(own, collective_id):
    (out,) = call(
        halves_kernel,
        collective_id,
        [(jax.ShapeDtypeStruct((2, *own.shape), own.dtype), pl.ANY)],
        [pl.BlockSpec(memory_space=pl.ANY)],
        [pltpu.SemaphoreType.DMA] * 3,
        own,
    )
    return out


def total_kernel(parts, out, slots, send, recv):
    nc, nt = lax.axis_size("ctx"), lax.axis_size("tp")
    count = parts.shape[0]
    place = (lax.axis_index("fsdp") * nc + lax.axis_index("ctx")) * nt + lax.axis_index("tp")
    barrier = pltpu.get_barrier_semaphore()

    def hello(i, carry):
        other = peer_of(lax.rem(place + i, count), nc, nt)
        pl.semaphore_signal(barrier, inc=1, device_id=other, device_id_type=MESH)
        return carry

    lax.fori_loop(1, count, hello, 0)
    pl.semaphore_wait(barrier, count - 1)

    def copy(i):
        other = lax.rem(place + i, count)
        return remote(
            parts.at[other], slots.at[i], send.at[i], recv.at[i], peer_of(other, nc, nt)
        )

    def go(i, carry):
        copy(i).start()
        return carry

    lax.fori_loop(1, count, go, 0)

    def add(i, carry):
        copy(i).wait()
        return carry + slots[i]

    out[...] = lax.fori_loop(1, count, add, parts[place])


def total_small(parts, collective_id):
    count = parts.shape[0]
    return pl.pallas_call(
        total_kernel,
        out_shape=jax.ShapeDtypeStruct(parts.shape[1:], parts.dtype),
        in_specs=[pl.BlockSpec(memory_space=pltpu.VMEM)],
        out_specs=pl.BlockSpec(memory_space=pltpu.VMEM),
        scratch_shapes=[
            pltpu.VMEM(parts.shape, parts.dtype),
            pltpu.SemaphoreType.DMA((count,)),
            pltpu.SemaphoreType.DMA((count,)),
        ],
        compiler_params=pltpu.CompilerParams(collective_id=collective_id, has_side_effects=True),
        cost_estimate=pl.CostEstimate(flops=0, bytes_accessed=1_000_000, transcendentals=0),
    )(parts)


def shards(
    tokens,
    lengths,
    cotangent,
    pre_gain,
    pre_bias,
    query_weight,
    key_weight,
    value_weight,
    swish_weight,
    out_weight,
    group_gain,
    group_bias,
    mlp_gain,
    mlp_bias,
    gelu_weight,
    up_weight,
    down_weight,
):
    seq_count, span, width = tokens.shape
    nf, nc, nt = lax.axis_size("fsdp"), lax.axis_size("ctx"), lax.axis_size("tp")
    f, c, t = lax.axis_index("fsdp"), lax.axis_index("ctx"), lax.axis_index("tp")
    block_rows = seq_count * span
    own_rows = block_rows // nt
    depth = query_weight.shape[0]
    heads_local = group_gain.shape[0]
    assert heads_local == nf
    key_size = query_weight.shape[1] // heads_local
    value_size = value_weight.shape[1] // heads_local
    hidden_size = gelu_weight.shape[1] // nf
    seqs = nf * seq_count
    rows = seqs * span
    head = t * heads_local + f

    def pad_tile(v):
        return jnp.pad(v, [(0, 0)] * (v.ndim - 1) + [(0, -v.shape[-1] % 1024)]).reshape(
            *v.shape[:-1], 8, -1
        )

    def own_part(v):
        return lax.dynamic_slice_in_dim(v.reshape(block_rows, width), t * own_rows, own_rows, 0)

    def all_depths(mine):
        return lax.all_gather(mine, "ctx", axis=0, tiled=True).reshape(width, -1)

    def padded(v):
        return jnp.pad(v.astype(f32).reshape(-1), (0, 128 - v.size))

    kinds = [pre_gain, pre_bias, mlp_gain, mlp_bias, group_gain, group_bias, lengths]
    small = jnp.stack([padded(v) for v in kinds] + [jnp.zeros(128, f32)])
    weights = [query_weight, key_weight, value_weight, swish_weight]
    weights += [out_weight, gelu_weight, up_weight, down_weight]
    attn_w, rest, normed, small = start(
        tokens.reshape(block_rows, width), small, weights, 4, (4, 7), 0
    )
    small, tokens, cotangent = lax.optimization_barrier((small, tokens, cotangent))
    normed = normed.reshape(rows, width)
    out_t = all_depths(rest[..., :value_size])
    pre_gain_full, pre_bias_full, mlp_gain_full, mlp_bias_full = (
        small[:, i, :depth].reshape(width) for i in range(4)
    )
    group = small[:, 4:6, : group_gain.size].reshape(nf * nc, 2, heads_local, -1)
    group = lax.dynamic_index_in_dim(group, f, 2, False).transpose(1, 0, 2).reshape(2, value_size)
    all_lengths = small.reshape(nf, nc, 8, 128)[:, 0, 6, :seq_count].reshape(seqs)

    inputs = own_part(tokens).astype(f32)
    _, norm_in_back = jax.vjp(layer_norm, inputs, pre_gain_full, pre_bias_full)
    positions = c * span + lax.iota(jnp.int32, span)
    own_ids = t * own_rows + lax.iota(jnp.int32, own_rows)
    own_valid = (c * span + own_ids % span < lengths[own_ids // span]).astype(f32)[:, None]
    error = own_valid * own_part(cotangent).astype(f32)

    pre = product(normed, attn_w)
    valid = (positions.astype(f32)[None, :] < all_lengths[:, None]).astype(f32)[:, :, None]
    cosine, sine = turn_tables(positions, key_size // 2)
    key_scale = key_size ** (-0.5)
    query_pre = pre[:, :key_size].reshape(seqs, span, key_size)
    key_pre = pre[:, key_size : 2 * key_size].reshape(seqs, span, key_size)
    value_pre = pre[:, 2 * key_size : 2 * key_size + value_size]
    swish_pre = pre[:, 2 * key_size + value_size :]
    queries = rotate(query_pre, cosine, sine).astype(bf16)
    keys = (rotate(key_pre, cosine, sine) * key_scale * valid).astype(bf16)
    values = value_pre.astype(bf16).reshape(seqs, span, value_size)

    log_decay = jnp.log1p(-jnp.exp2(-5.0 - head.astype(f32)))
    offsets = jnp.arange(span)
    distance = (offsets[:, None] - offsets[None, :]).astype(f32)
    within_fade = jnp.where(distance >= 0, jnp.exp(jnp.maximum(distance, 0.0) * log_decay), 0.0)
    key_fade = jnp.exp((span - 1 - offsets).astype(f32) * log_decay)[:, None]
    query_fade = jnp.exp((offsets + 1).astype(f32) * log_decay)[:, None]
    block_fade = jnp.exp(span * log_decay)

    keys_faded = (keys.astype(f32) * key_fade).astype(bf16)
    queries_faded = (queries.astype(f32) * query_fade).astype(bf16)
    local_state = blocks("sjd,sje->sde", keys_faded, values)
    error_low = error.astype(bf16)
    entering, error_all = pass_and_gather(local_state, block_fade, error_low, 1, 2)
    rest, entering = lax.optimization_barrier((rest, entering))
    ff_w = all_depths(rest[..., value_size:])
    gelu_up = ff_w[:, : 2 * hidden_size]
    down_t = ff_w[:, 2 * hidden_size :]
    probs = (blocks("sid,sjd->sij", queries, keys) * within_fade).astype(bf16)
    mixed = blocks("sij,sje->sie", probs, values) + blocks("sid,sde->sie", queries_faded, entering)
    gated_wide, gate_back = jax.vjp(
        gate_mix, mixed.reshape(rows, value_size), swish_pre, group[0], group[1]
    )
    gated = gated_wide.astype(bf16)
    branch = scatter_product([gated], out_t, 0, 1)
    hidden = inputs + branch

    mlp_wide, norm_mid_back = jax.vjp(layer_norm, hidden, mlp_gain_full, mlp_bias_full)
    mlp_in = gather_rows(mlp_wide.astype(bf16), 4)
    pre_ff = product(mlp_in, gelu_up)
    inner_wide, mix_back = jax.vjp(mlp_mix, pre_ff[:, :hidden_size], pre_ff[:, hidden_size:])
    inner = inner_wide.astype(bf16)

    def sum_depths(grads):
        grads = with_layout_constraint(grads.astype(bf16), Layout((0, 1)))
        mine = lax.psum_scatter(grads, "ctx", scatter_dimension=0, tiled=True)
        return mine.reshape(nf, depth, -1)

    down_part = product_left(error_all, inner).astype(bf16)
    down_part, down_t = lax.optimization_barrier((down_part, down_t))
    down_sum = sum_depths(down_part)
    gelu_grad, up_grad = mix_back(product(error_all, down_t))
    ff_low = jnp.concatenate([gelu_grad.astype(bf16), up_grad.astype(bf16)], -1)
    grad_gelu_up = product_left(mlp_in, ff_low)
    ff_parts = grad_gelu_up.astype(bf16)
    ff_parts, ff_low = lax.optimization_barrier((ff_parts, ff_low))
    ff_sum = sum_depths(ff_parts)
    mlp_in_grad = scatter_product([ff_low], ff_w, 0, 6)
    hidden_norm_grad, grad_mlp_gain, grad_mlp_bias = norm_mid_back(mlp_in_grad)
    hidden_grad = error + hidden_norm_grad

    out_part, gated_grad = gather_products(hidden_grad.astype(bf16), gated, out_t, 10)
    out_sum = sum_depths(out_part)
    mixed_grad, swish_grad, grad_group_gain, grad_group_bias = gate_back(gated_grad)
    swish_low = swish_grad.astype(bf16)
    mixed_low = mixed_grad.astype(bf16).reshape(seqs, span, value_size)
    score_low = (blocks("sie,sje->sij", mixed_low, values) * within_fade).astype(bf16)
    pulled_state = blocks("sid,sie->sde", queries_faded, mixed_low)
    swish_part = product_left(normed, swish_low).astype(bf16)
    swish_part, pulled_state, ff_sum, down_sum = lax.optimization_barrier(
        (swish_part, pulled_state, ff_sum, down_sum)
    )
    later, mlp_out, grad_gelu, grad_up, grad_down = pass_and_scatter(
        pulled_state, block_fade, inner, ff_w, 2 * hidden_size, ff_sum, down_sum, -1, 3
    )
    out_sum, swish_part, later = lax.optimization_barrier((out_sum, swish_part, later))
    swish_sum = sum_depths(swish_part)
    block_own = (own_valid * (hidden + mlp_out)).astype(bf16)
    block_out = both_halves(block_own, 8).reshape(tokens.shape)
    query_grad = blocks("sij,sjd->sid", score_low, keys) + query_fade * blocks(
        "sie,sde->sid", mixed_low, entering
    )
    key_grad = blocks("sij,sid->sjd", score_low, queries) + key_fade * blocks(
        "sje,sde->sjd", values, later
    )
    value_grad = blocks("sij,sie->sje", probs, mixed_low) + blocks(
        "sjd,sde->sje", keys_faded, later
    )
    query_low = rotate_back(query_grad, cosine, sine).astype(bf16).reshape(rows, key_size)
    key_low = rotate_back(key_grad * key_scale * valid, cosine, sine).astype(bf16)
    low = jnp.concatenate(
        [
            query_low,
            key_low.reshape(rows, key_size),
            value_grad.astype(bf16).reshape(rows, value_size),
        ],
        -1,
    )
    attn_part = product_left(normed, low).astype(bf16)
    attn_part, low = lax.optimization_barrier((attn_part, low))
    attn_sum = sum_depths(attn_part)
    normed_grad = scatter_product([low, swish_low], attn_w, 0, 7)
    swish_sum, normed_grad = lax.optimization_barrier((swish_sum, normed_grad))
    input_norm_grad, grad_pre_gain, grad_pre_bias = norm_in_back(normed_grad)
    tokens_own = (hidden_grad + input_norm_grad).astype(bf16)
    grad_tokens = both_halves(tokens_own, 8).reshape(tokens.shape)

    early_grads = finish(
        [out_sum, swish_sum],
        [[value_size], [value_size]],
        [True, False],
        9,
    )
    norm_parts = jnp.stack([grad_pre_gain, grad_pre_bias, grad_mlp_gain, grad_mlp_bias])
    norm_parts = norm_parts.reshape(4, nf * nc, 1, depth).transpose(1, 2, 0, 3)
    norm_parts = jnp.broadcast_to(norm_parts, (nf * nc, nt, 4, depth)).reshape(nf * nc, nt, -1)
    mine = lax.iota(jnp.int32, nt * heads_local) == head
    group_parts = jnp.stack([grad_group_gain, grad_group_bias]).reshape(1, 2, nf * nc, -1)
    group_parts = jnp.where(mine[:, None, None, None], group_parts, 0.0)
    group_parts = group_parts.reshape(nt, heads_local, 2, nf * nc, -1).transpose(3, 0, 2, 1, 4)
    parts = jnp.concatenate([norm_parts, group_parts.reshape(nf * nc, nt, -1)], -1)
    parts = parts.reshape(nf * nc * nt, -1)
    sums = total_small(pad_tile(parts), 5).reshape(-1)[: parts.shape[1]]
    sums, attn_sum, block_out, grad_tokens, early_grads = lax.optimization_barrier(
        (sums, attn_sum, block_out, grad_tokens, early_grads)
    )
    grad_out, grad_swish = early_grads
    grad_query, grad_key, grad_value = finish(
        [attn_sum], [[key_size, key_size, value_size]], [False], 11
    )
    norm_sums = sums[: 4 * depth].reshape(4, depth)
    group_sums = sums[4 * depth :].reshape(2, heads_local, -1)

    return (
        block_out,
        grad_tokens,
        norm_sums[0],
        norm_sums[1],
        grad_query,
        grad_key,
        grad_value,
        grad_swish,
        grad_out,
        group_sums[0],
        group_sums[1],
        norm_sums[2],
        norm_sums[3],
        grad_gelu,
        grad_up,
        grad_down,
    )


def solution(mesh):
    rows = P("fsdp", "ctx", None)
    vector = P(("fsdp", "ctx"))
    tall = P(("fsdp", "ctx"), "tp")
    wide = P("tp", ("fsdp", "ctx"))
    in_specs = (rows, P("fsdp"), rows, vector, vector, tall, tall, tall, tall, wide)
    in_specs += (wide, wide, vector, vector, tall, tall, wide)
    out_specs = (rows, rows, vector, vector, tall, tall, tall, tall, wide)
    out_specs += (wide, wide, vector, vector, tall, tall, wide)
    return jax.shard_map(shards, mesh=mesh, in_specs=in_specs, out_specs=out_specs, check_vma=False)
```

```python
import functools

import jax
import jax.numpy as jnp
from jax import lax
from jax.experimental import pallas as pl
from jax.experimental.layout import Layout, with_layout_constraint
from jax.experimental.pallas import tpu as pltpu
from jax.sharding import PartitionSpec as P

eps = 1e-05
group_floor = 1.0
f32 = jnp.float32
bf16 = jnp.bfloat16


def layer_norm(values, norm_gain, norm_shift):
    centred = values - jnp.mean(values, -1, keepdims=True)
    spread = jnp.mean(centred * centred, -1, keepdims=True)
    return centred * lax.rsqrt(spread + eps) * norm_gain + norm_shift


def turn_tables(positions, half_size):
    frequency = jnp.power(10000.0, -jnp.arange(half_size).astype(f32) / half_size)
    angles = positions.astype(f32)[:, None] * frequency[None, :]
    return jnp.cos(angles), jnp.sin(angles)


def rotate(values, cosine, sine):
    half_size = values.shape[-1] // 2
    first = values[..., :half_size]
    second = values[..., half_size:]
    return jnp.concatenate([first * cosine - second * sine, second * cosine + first * sine], -1)


def rotate_back(values, cosine, sine):
    return rotate(values, cosine, -sine)


def gate_mix(mixed, swish_pre, norm_gain, norm_shift):
    centred = mixed - jnp.mean(mixed, -1, keepdims=True)
    spread = jnp.mean(centred * centred, -1, keepdims=True)
    return jax.nn.silu(swish_pre) * (
        centred * lax.rsqrt(spread + group_floor) * norm_gain + norm_shift
    )


def mlp_mix(gelu_pre, up_pre):
    return jax.nn.gelu(gelu_pre) * up_pre


def product(left, right):
    return jnp.dot(left, right, preferred_element_type=f32)


def product_left(left, right):
    return lax.dot_general(left, right, (((0,), (0,)), ((), ())), preferred_element_type=f32)


def product_right(left, right):
    return lax.dot_general(left, right, (((1,), (1,)), ((), ())), preferred_element_type=f32)


def blocks(spec, left, right):
    return jnp.einsum(spec, left, right, preferred_element_type=f32)


MESH = pl.DeviceIdType.MESH


def beside(f):
    return f + 1 - 2 * (f % 2), (f + 2) % 4, 3 - f


def remote(src, dst, send, recv, device):
    return pltpu.make_async_remote_copy(
        src_ref=src, dst_ref=dst, send_sem=send, recv_sem=recv, device_id=device, device_id_type=MESH
    )


def reorder(src, dst, kind, back):
    nf, nc = lax.axis_size("fsdp"), lax.axis_size("ctx")
    depth = src.shape[-1] // (nf * nc)
    for f in range(nf):
        for c in range(nc):
            plain, mixed = (f * nc + c) * depth, (c * nf + f) * depth
            if back:
                plain, mixed = mixed, plain
            dst[:, mixed : mixed + depth] = src[:, plain : plain + depth].astype(kind)


def gather_steps(plain, out, mixed, keep, send, recv):
    own = plain if mixed is None else mixed
    f, t = lax.axis_index("fsdp"), lax.axis_index("tp")
    fx, fy, fd = beside(f)
    x, y, core = {"fsdp": fx}, {"fsdp": fy}, {"tp": 1 - t}
    half = own.shape[0] // 2

    def part(ref, h):
        return ref.at[pl.ds(h * half, half)]

    def slot(who, h):
        return part(out.at[2 * who + t], h)

    local = pltpu.make_async_copy(own, out.at[2 * f + t], keep)
    first = [
        remote(part(own, 0), slot(f, 0), send.at[0], recv.at[0], x),
        remote(part(own, 1), slot(f, 1), send.at[1], recv.at[3], y),
        remote(part(own, 1), slot(f, 1), send.at[2], recv.at[1], x),
        remote(part(own, 0), slot(f, 0), send.at[3], recv.at[2], y),
        remote(part(own, 0), slot(f, 0), send.at[4], recv.at[6], core),
        remote(part(own, 1), slot(f, 1), send.at[5], recv.at[7], core),
    ]
    sent = list(first)

    def pass_on(who, h, s, r, device):
        copy = remote(slot(who, h), slot(who, h), send.at[s], recv.at[r], device)
        copy.start()
        sent.append(copy)

    def begin():
        if mixed is not None:
            reorder(plain, mixed, mixed.dtype, False)
        local.start()
        for copy in first:
            copy.start()

    def relay():
        first[0].wait_recv()
        pass_on(fx, 0, 6, 4, y)
        pass_on(fx, 0, 7, 8, core)
        first[1].wait_recv()
        pass_on(fy, 1, 8, 5, x)
        pass_on(fy, 1, 9, 11, core)

    def rest():
        first[2].wait_recv()
        pass_on(fx, 1, 10, 9, core)
        first[3].wait_recv()
        pass_on(fy, 0, 11, 10, core)

    def diagonal():
        remote(slot(fd, 0), slot(fd, 0), send.at[12], recv.at[4], y).wait_recv()
        pass_on(fd, 0, 12, 12, core)
        remote(slot(fd, 1), slot(fd, 1), send.at[13], recv.at[5], x).wait_recv()
        pass_on(fd, 1, 13, 13, core)

    def end(crossed=False):
        if not crossed:
            for r in range(6, 14):
                remote(slot(f, 0), slot(f, 0), send.at[0], recv.at[r], core).wait_recv()
            local.wait()
        for copy in sent:
            copy.wait_send()

    return begin, relay, rest, diagonal, end


def in_kernel(width):
    return width // (lax.axis_size("fsdp") * lax.axis_size("ctx")) % 128 == 0


def gather_scratch(own):
    return [
        pltpu.VMEM(own.shape if in_kernel(own.shape[1]) else (16, 128), own.dtype),
        pltpu.SemaphoreType.DMA,
        pltpu.SemaphoreType.DMA((14,)),
        pltpu.SemaphoreType.DMA((14,)),
    ]


def scatter_steps(start, lefts, right, out, mine, sent, theirs, total, diag, last, send, recv):
    f, t = lax.axis_index("fsdp"), lax.axis_index("tp")
    fx, fy, fd = beside(f)
    x, y, core = {"fsdp": fx}, {"fsdp": fy}, {"tp": 1 - t}
    half = out.shape[0] // 2
    order = [fd, fy, fx, f]
    tile = 512

    def part(ref, h):
        return ref.at[pl.ds(h * half, half)]

    crossing = [
        remote(sent.at[i], theirs.at[i], send.at[i], recv.at[i], core) for i in range(4)
    ]
    d0 = remote(part(total.at[0], 0), diag.at[0], send.at[4], recv.at[4], x)
    d1 = remote(part(total.at[0], 1), diag.at[1], send.at[5], recv.at[5], y)
    y1 = remote(part(total.at[1], 1), part(last.at[1], 1), send.at[6], recv.at[6], y)
    x0 = remote(part(total.at[2], 0), part(last.at[0], 0), send.at[7], recv.at[7], x)
    y0 = remote(part(total.at[1], 0), part(last.at[1], 0), send.at[8], recv.at[8], y)
    x1 = remote(part(total.at[2], 1), part(last.at[0], 1), send.at[9], recv.at[9], x)

    def make(block, put):
        def piece(j, carry):
            columns = pl.ds(pl.multiple_of(j * tile, tile), tile)
            at, value = start, 0.0
            for left in lefts:
                size = left.shape[2]
                value += product_right(left[block], right[columns, at : at + size])
                at += size
            put(columns, value)
            return carry

        lax.fori_loop(0, out.shape[1] // tile, piece, 0)

    def cross(i):
        def put(columns, value):
            sent[i, :, columns] = value.astype(sent.dtype)

        make(2 * order[i] + 1 - t, put)
        crossing[i].start()

    def keep(i):
        def put(columns, value):
            mine[:, columns] = value

        make(2 * order[i] + t, put)

    def add(i):
        keep(i)
        crossing[i].wait_recv()
        total[i] = (mine[...] + theirs[i].astype(f32)).astype(total.dtype)

    def diagonal():
        cross(0)
        cross(1)
        add(0)
        d0.start()
        d1.start()

    def straight():
        cross(2)
        add(1)
        y1.start()
        add(2)
        x0.start()
        cross(3)

    def relay():
        d0.wait_recv()
        total[1, :half] = (total[1, :half].astype(f32) + diag[0].astype(f32)).astype(total.dtype)
        y0.start()
        d1.wait_recv()
        total[2, half:] = (total[2, half:].astype(f32) + diag[1].astype(f32)).astype(total.dtype)
        x1.start()
        keep(3)
        crossing[3].wait_recv()
        mine[...] += theirs[3].astype(f32)

    def end():
        for copy in (y1, x0, y0, x1):
            copy.wait_recv()
        mine[...] += last[0].astype(f32) + last[1].astype(f32)
        if in_kernel(out.shape[1]):
            reorder(mine, out, out.dtype, True)
        else:
            out[...] = mine[...]
        for copy in (*crossing, d0, d1, y1, x0, y0, x1):
            copy.wait_send()

    return diagonal, straight, relay, end


def scatter_scratch(rows, width):
    return [
        pltpu.VMEM((rows, width), f32),
        pltpu.VMEM((4, rows, width), bf16),
        pltpu.VMEM((4, rows, width), bf16),
        pltpu.VMEM((3, rows, width), bf16),
        pltpu.VMEM((2, rows // 2, width), bf16),
        pltpu.VMEM((2, rows, width), bf16),
        pltpu.SemaphoreType.DMA((10,)),
        pltpu.SemaphoreType.DMA((10,)),
    ]


def pass_steps(by, local, fade, out, held, send, recv):
    length = lax.axis_size("ctx")
    c = lax.axis_index("ctx")
    first = c == (0 if by > 0 else length - 1)
    last = c == (length - 1 if by > 0 else 0)
    target = lax.rem(c + by + length, length)

    def copy(p):
        return remote(held.at[p], out.at[p], send.at[p], recv.at[p], {"ctx": target})

    def step(p, carry):
        @pl.when(first)
        def _():
            out[p] = jnp.zeros(out.shape[1:], out.dtype)

        @pl.when(jnp.logical_not(first))
        def _():
            copy(p).wait_recv()

        @pl.when(jnp.logical_not(last))
        def _():
            held[p] = (fade[...] * out[p].astype(f32) + local[p]).astype(held.dtype)
            copy(p).start()

        return carry

    def run(quarter):
        count = local.shape[0]
        if quarter < 0:
            lax.fori_loop(0, jnp.where(first, count, 0), step, 0)
        else:
            low, high = quarter * count // 4, (quarter + 1) * count // 4
            lax.fori_loop(jnp.where(first, count, low), jnp.where(first, count, high), step, 0)

    def end():
        @pl.when(jnp.logical_not(last))
        def _():
            def done(p, carry):
                copy(p).wait_send()
                return carry

            lax.fori_loop(0, local.shape[0], done, 0)

    return run, end


def greet_plane(by=0, diagonal=False):
    f, c, t = lax.axis_index("fsdp"), lax.axis_index("ctx"), lax.axis_index("tp")
    length = lax.axis_size("ctx")
    fx, fy, fd = beside(f)
    barrier = pltpu.get_barrier_semaphore()
    peers = [{"fsdp": fx}, {"fsdp": fy}, {"tp": 1 - t}] + [{"fsdp": fd}] * diagonal
    for device in peers:
        pl.semaphore_signal(barrier, inc=1, device_id=device, device_id_type=MESH)
    if by != 0:
        first = c == (0 if by > 0 else length - 1)
        last = c == (length - 1 if by > 0 else 0)
        source = {"ctx": lax.rem(c - by + length, length)}

        @pl.when(jnp.logical_not(first))
        def _():
            pl.semaphore_signal(barrier, inc=1, device_id=source, device_id_type=MESH)

        @pl.when(jnp.logical_not(last))
        def _():
            pl.semaphore_wait(barrier, len(peers) + 1)

        @pl.when(last)
        def _():
            pl.semaphore_wait(barrier, len(peers))
    else:
        pl.semaphore_wait(barrier, len(peers))


def gather_with(own, full, mixed, *scratch):
    return gather_steps(own, full, mixed if in_kernel(own.shape[1]) else None, *scratch)


def gather_kernel(*refs):
    steps = gather_with(*refs)
    greet_plane()
    for step in steps:
        step()


def scatter_kernel(count, start, *refs):
    steps = scatter_steps(start, refs[:count], *refs[count:])
    greet_plane()
    for step in steps:
        step()


def gather_products_kernel(own, left, right, grad, back, full, total, mixed, *scratch):
    f, t = lax.axis_index("fsdp"), lax.axis_index("tp")
    fx, fy, fd = beside(f)
    recv = scratch[2]
    begin, relay, rest, diagonal, end = gather_with(own, full, mixed, *scratch)
    tile = 512

    def use(block, fresh=False):
        back[block] = product(full[block], right[...])

        def piece(j, carry):
            columns = pl.ds(pl.multiple_of(j * tile, tile), tile)
            value = product_left(full[block, :, columns], left[block])
            total[columns, :] = value if fresh else total[columns, :] + value
            return carry

        lax.fori_loop(0, total.shape[0] // tile, piece, 0)

    def crossed(who, r):
        block = full.at[2 * who + 1 - t]
        half = block.shape[0] // 2
        for h in range(2):
            where = block.at[pl.ds(h * half, half)]
            remote(where, where, scratch[1].at[0], recv.at[r + h], {"tp": 1 - t}).wait_recv()

    greet_plane()
    begin()
    pltpu.make_async_copy(full.at[2 * f + t], full.at[2 * f + t], scratch[0]).wait()
    use(2 * f + t, True)
    relay()
    crossed(f, 6)
    use(2 * f + 1 - t)
    rest()
    use(2 * fx + t)
    use(2 * fy + t)
    crossed(fx, 8)
    use(2 * fx + 1 - t)
    crossed(fy, 10)
    use(2 * fy + 1 - t)
    diagonal()
    use(2 * fd + t)
    crossed(fd, 12)
    use(2 * fd + 1 - t)
    end(True)
    grad[...] = total[...].astype(grad.dtype)


def gather_products(own, left, right, collective_id):
    own = ready(own)
    rows, width = own.shape
    size = left.shape[1]
    grad, back = call(
        gather_products_kernel,
        collective_id,
        [
            (jax.ShapeDtypeStruct((width, size), bf16), pltpu.VMEM),
            (jax.ShapeDtypeStruct((8, rows, size), f32), pltpu.VMEM),
        ],
        [vmem()] * 3,
        [
            pltpu.VMEM((8, rows, width), bf16),
            pltpu.VMEM((width, size), f32),
            *gather_scratch(own),
        ],
        own,
        in_eights(left),
        right,
    )
    return grad, back.reshape(8 * rows, size)


def pass_gather_kernel(by, local, fade, own, out, full, held, send, recv, *scratch):
    begin, relay, rest, diagonal, end = gather_with(own, full, *scratch)
    run, done = pass_steps(by, local, fade, out, held, send, recv)
    greet_plane(by)
    begin()
    run(-1)
    run(0)
    relay()
    run(1)
    rest()
    run(2)
    run(3)
    diagonal()
    end()
    done()


def pass_scatter_kernel(by, start, local, fade, left, right, ff, out, own, *refs):
    gelu_grad, up_grad, down_grad, held, send, recv = refs[:6]
    scratch, hand = refs[6:-3], refs[-3:]
    targets = [[(gelu_grad, False), (up_grad, False), (down_grad, True)]]
    hand_over, take = hand_steps([ff], targets, *hand)
    diagonal, straight, relay, end = scatter_steps(start, [left], right, own, *scratch)
    run, done = pass_steps(by, local, fade, out, held, send, recv)
    greet_plane(by, True)
    run(-1)
    diagonal()
    straight()
    run(0)
    run(1)
    relay()
    hand_over()
    run(2)
    run(3)
    end()
    take()
    done()


def call(kernel, collective_id, outs, ins, scratch, *args):
    shapes, spaces = zip(*outs)
    return pl.pallas_call(
        kernel,
        out_shape=shapes,
        in_specs=ins,
        out_specs=tuple(pl.BlockSpec(memory_space=space) for space in spaces),
        scratch_shapes=scratch,
        compiler_params=pltpu.CompilerParams(
            collective_id=collective_id, has_side_effects=True, vmem_limit_bytes=52 << 20
        ),
        cost_estimate=pl.CostEstimate(flops=0, bytes_accessed=2_000_000, transcendentals=0),
    )(*args)


def vmem():
    return pl.BlockSpec(memory_space=pltpu.VMEM)


def perm(v):
    nf, nc = lax.axis_size("fsdp"), lax.axis_size("ctx")
    return v.reshape(len(v), nf, nc, -1).transpose(0, 2, 1, 3).reshape(v.shape)


def unperm(v):
    nf, nc = lax.axis_size("fsdp"), lax.axis_size("ctx")
    return v.reshape(len(v), nc, nf, -1).transpose(0, 2, 1, 3).reshape(v.shape)


def gathered(own):
    rows, width = own.shape
    return jax.ShapeDtypeStruct((8, rows, width), own.dtype), pl.ANY


def scattered(left, right):
    return jax.ShapeDtypeStruct((left.shape[0] // 8, right.shape[0]), f32), pltpu.VMEM


def passed(local):
    return jax.ShapeDtypeStruct(local.shape, bf16), pltpu.VMEM


def pass_scratch(local):
    pieces = local.shape[0]
    return [
        pltpu.VMEM(local.shape, bf16),
        pltpu.SemaphoreType.DMA((pieces,)),
        pltpu.SemaphoreType.DMA((pieces,)),
    ]


def in_eights(left):
    return left.reshape(8, -1, left.shape[1])


def ready(own):
    return own if in_kernel(own.shape[1]) else perm(own)


def plain(own):
    return own if in_kernel(own.shape[1]) else unperm(own)


def gather_rows(own, collective_id):
    own = ready(own)
    (out,) = call(gather_kernel, collective_id, [gathered(own)], [vmem()], gather_scratch(own), own)
    return out.reshape(-1, own.shape[1])


def scatter_product(lefts, right, start, collective_id):
    rows, width = lefts[0].shape[0] // 8, right.shape[0]
    (out,) = call(
        functools.partial(scatter_kernel, len(lefts), start),
        collective_id,
        [(jax.ShapeDtypeStruct((rows, width), f32), pltpu.VMEM)],
        [vmem()] * (len(lefts) + 1),
        scatter_scratch(rows, width),
        *(in_eights(left) for left in lefts),
        right,
    )
    return plain(out)


def pass_and_gather(local, fade, own, by, collective_id):
    shape = local.shape
    local = local.reshape(2 * shape[0], -1, shape[2])
    own = ready(own)
    out, full = call(
        functools.partial(pass_gather_kernel, by),
        collective_id,
        [passed(local), gathered(own)],
        [vmem(), vmem(), vmem()],
        pass_scratch(local) + gather_scratch(own),
        local,
        jnp.full((1, local.shape[2]), fade, f32),
        own,
    )
    return out.reshape(shape), full.reshape(-1, own.shape[1])


def feed_forward_kernel(rows, error, weight, inner, low, grads, total):
    step = pl.program_id(0)
    size, tile, deep = inner.shape[1], 512, 1024
    root = (2.0 / jnp.pi) ** 0.5

    def units(j, carry):
        at = pl.multiple_of(j * tile, tile)
        gelu_pre = product(rows[...], weight[:, pl.ds(at, tile)])
        up_pre = product(rows[...], weight[:, pl.ds(at + size, tile)])
        square = gelu_pre * gelu_pre
        bend = jnp.tanh(root * gelu_pre * (1.0 + 0.044715 * square))
        half = 0.5 * (1.0 + bend)
        gelu = gelu_pre * half
        slope = half + 0.5 * gelu_pre * (1.0 - bend * bend) * root * (1.0 + 0.134145 * square)
        inner[:, pl.ds(at, tile)] = (gelu * up_pre).astype(bf16)
        inner_grad = product(error[...], weight[:, pl.ds(at + 2 * size, tile)])
        low[:, pl.ds(at, tile)] = (inner_grad * up_pre * slope).astype(bf16)
        low[:, pl.ds(at + size, tile)] = (inner_grad * gelu).astype(bf16)
        return carry

    lax.fori_loop(0, size // tile, units, 0)

    def depths(first, last):
        def piece(j, carry):
            at = pl.ds(pl.multiple_of(j * deep, deep), deep)
            into = grads if last else total
            for left, right, columns in (
                (rows, low, slice(0, 2 * size)),
                (error, inner, slice(2 * size, 3 * size)),
            ):
                value = product_left(left[:, at], right[...])
                if not first:
                    value += total[at, columns]
                into[at, columns] = value.astype(into.dtype)
            return carry

        lax.fori_loop(0, total.shape[0] // deep, piece, 0)

    steps = pl.num_programs(0)
    pl.when(step == 0)(lambda: depths(True, False))
    pl.when((step > 0) & (step < steps - 1))(lambda: depths(False, False))
    pl.when(step == steps - 1)(lambda: depths(False, True))


def feed_forward(rows, error, weight):
    count, width = rows.shape
    size, block = weight.shape[1] // 3, 512
    whole = pl.BlockSpec(weight.shape, lambda i: (0, 0))

    def some(columns):
        return pl.BlockSpec((block, columns), lambda i: (i, 0))

    return pl.pallas_call(
        feed_forward_kernel,
        grid=(count // block,),
        out_shape=(
            jax.ShapeDtypeStruct((count, size), bf16),
            jax.ShapeDtypeStruct((count, 2 * size), bf16),
            jax.ShapeDtypeStruct(weight.shape, bf16),
        ),
        in_specs=[some(width), some(width), whole],
        out_specs=(some(size), some(2 * size), whole),
        scratch_shapes=[pltpu.VMEM(weight.shape, f32)],
        compiler_params=pltpu.CompilerParams(vmem_limit_bytes=56 << 20),
        cost_estimate=pl.CostEstimate(
            flops=14 * count * width * size, bytes_accessed=40_000_000, transcendentals=count * size
        ),
    )(rows, error, weight)


def pass_and_scatter(local, fade, left, right, start, ff, by, collective_id):
    shape = local.shape
    local = local.reshape(2 * shape[0], -1, shape[2])
    out, own, *grads = call(
        functools.partial(pass_scatter_kernel, by, start),
        collective_id,
        [
            passed(local),
            scattered(left, right),
            *handed(ff, [left.shape[1]] * 2),
            *handed(ff, [left.shape[1]], True),
        ],
        [vmem()] * 5,
        pass_scratch(local)
        + scatter_scratch(left.shape[0] // 8, right.shape[0])
        + hand_scratch([ff]),
        local,
        jnp.full((1, local.shape[2]), fade, f32),
        in_eights(left),
        right,
        ff,
    )
    return out.reshape(shape), plain(own), *(grad.astype(f32) for grad in grads)


def peer_of(place, nc, nt):
    return {"fsdp": place // (nc * nt), "ctx": place // nt % nc, "tp": place % nt}


def line_steps(home, place, arrived, send, recv):
    nf, nc = lax.axis_size("fsdp"), lax.axis_size("ctx")
    f, c = lax.axis_index("fsdp"), lax.axis_index("ctx")
    order = [f, *beside(f)]
    above, below = c < nc - 1, c > 0

    def copy(src, place_of, who, up):
        chunk = place_of * nf + who
        return remote(
            src,
            place(place_of, who),
            send.at[chunk if up else nc * nf + chunk],
            recv.at[chunk],
            {"ctx": lax.rem(c + 1, nc) if up else lax.rem(c + nc - 1, nc)},
        )

    def first(i):
        who = order[i]
        arrived(i)

        @pl.when(above)
        def _():
            copy(home(who), c, who, True).start()

        @pl.when(below)
        def _():
            copy(home(who), c, who, False).start()

    def step(k, carry):
        for who in order:

            @pl.when(c - k >= 0)
            def _():
                copy(place(c - k, who), c - k, who, True).wait_recv()

                @pl.when(above)
                def _():
                    copy(place(c - k, who), c - k, who, True).start()

            @pl.when(c + k < nc)
            def _():
                copy(place(c + k, who), c + k, who, False).wait_recv()

                @pl.when(below)
                def _():
                    copy(place(c + k, who), c + k, who, False).start()

        return carry

    def end():
        def one(other, carry):
            for who in order:

                @pl.when(above & (other <= c))
                def _():
                    copy(place(other, who), other, who, True).wait_send()

                @pl.when(below & (other >= c))
                def _():
                    copy(place(other, who), other, who, False).wait_send()

            return carry

        lax.fori_loop(0, nc, one, 0)

    return first, step, end


def line_scratch():
    count = lax.axis_size("fsdp") * lax.axis_size("ctx")
    return [pltpu.SemaphoreType.DMA((2 * count,)), pltpu.SemaphoreType.DMA((count,))]


def start_kernel(sizes, split, turned, own, small, *refs):
    count = len(sizes)
    weights = list(refs[:count])
    attn, rest, full, everyone = refs[count : count + 4]
    (
        turns,
        gains,
        normed,
        mixed,
        gather_keep,
        gather_send,
        gather_recv,
        line_send,
        line_recv,
        keep,
        send,
        recv,
        small_send,
        small_recv,
    ) = refs[count + 4 :]
    nf, nc = lax.axis_size("fsdp"), lax.axis_size("ctx")
    f, c, t = lax.axis_index("fsdp"), lax.axis_index("ctx"), lax.axis_index("tp")
    here, places = f * nc + c, nf * nc
    depth = weights[0].shape[0]
    across = [weights[i] for i in turned]
    for n, i in enumerate(turned):
        weights[i] = turns.at[n]
    near = beside(f)
    starts = [sum(sizes[:i]) if i < split else sum(sizes[split:i]) for i in range(count)]

    def peer(i):
        other = lax.rem(here + i, places)
        return {"fsdp": other // nc, "ctx": other % nc}

    barrier = pltpu.get_barrier_semaphore()
    pl.semaphore_signal(barrier, inc=1, device_id={"tp": 1 - t}, device_id_type=MESH)

    def hello(i, carry):
        pl.semaphore_signal(barrier, inc=1, device_id=peer(i), device_id_type=MESH)
        return carry

    lax.fori_loop(1, places, hello, 0)
    pl.semaphore_wait(barrier, places)

    def chunk(place_of, who):
        rows = pl.multiple_of((place_of * nf + who) * depth, depth)
        return attn.at[pl.ds(rows, depth)]

    def columns(i, who):
        return weights[i].at[:, pl.ds(pl.multiple_of(who * sizes[i], sizes[i]), sizes[i])]

    def target(i):
        where = chunk(c, f) if i < split else rest.at[f]
        return where.at[:, pl.ds(starts[i], sizes[i])]

    def hand_out(i, n):
        return remote(
            columns(i, near[n]),
            target(i),
            send.at[3 * i + n],
            recv.at[n if i < split else 3 + n],
            {"fsdp": near[n]},
        )

    def hold(i):
        return pltpu.make_async_copy(columns(i, f), target(i), keep.at[0 if i < split else 1])

    for i in range(split):
        hold(i).start()
    for n in range(3):
        for i in range(split):
            hand_out(i, n).start()

    def arrived(i):
        if i == 0:
            pltpu.make_async_copy(chunk(c, f), chunk(c, f), keep.at[0]).wait()
        else:
            who = near[i - 1]
            remote(
                chunk(c, who), chunk(c, who), send.at[0], recv.at[i - 1], {"fsdp": who}
            ).wait_recv()

    first, step, end = line_steps(lambda who: chunk(c, who), chunk, arrived, line_send, line_recv)
    first(0)

    def tell(i):
        return remote(small, everyone.at[here], small_send.at[i], small_recv.at[i], peer(i))

    def go(i, carry):
        tell(i).start()
        return carry

    def told(i, carry):
        tell(i).wait()
        return carry

    lax.fori_loop(1, places, go, 0)
    everyone[here] = small[...]
    first(1)
    lax.fori_loop(1, places, told, 0)
    for i in range(places):
        for j in range(2):
            gains[j : j + 1, i * depth : (i + 1) * depth] = everyone[i, j : j + 1, :depth]
    rows = normed.shape[0]
    mine = own[pl.ds(pl.multiple_of(t * rows, rows), rows), :].astype(f32)
    normed[...] = layer_norm(mine, gains[0:1, :], gains[1:2, :]).astype(bf16)
    begin, relay, others, diagonal, finish = gather_steps(
        normed, full, mixed, gather_keep, gather_send, gather_recv
    )
    begin()
    first(2)
    first(3)
    step(1, 0)
    relay()
    for n in range(len(turned)):
        turns[n] = across[n][...].T
    for i in range(split, count):
        hold(i).start()
        for n in range(3):
            hand_out(i, n).start()
    lax.fori_loop(2, 3, step, 0)
    others()
    diagonal()
    lax.fori_loop(3, nc, step, 0)
    finish()
    pltpu.make_async_copy(rest.at[f], rest.at[f], keep.at[1]).wait()
    for n in range(3):
        where = rest.at[near[n]]
        remote(where, where, send.at[0], recv.at[3 + n], {"fsdp": near[n]}).wait_recv()
    for i in range(count):
        for n in range(3):
            hand_out(i, n).wait_send()
    end()


def start(tokens, small, weights, split, turned, collective_id):
    nf, nc = lax.axis_size("fsdp"), lax.axis_size("ctx")
    rows, width = tokens.shape
    rows //= lax.axis_size("tp")
    depth = weights[0].shape[0]
    sizes = [w.size // depth // nf for w in weights]
    anywhere = pl.BlockSpec(memory_space=pl.ANY)
    count = nf * nc
    return call(
        functools.partial(start_kernel, sizes, split, turned),
        collective_id,
        [
            (jax.ShapeDtypeStruct((width, sum(sizes[:split])), bf16), pl.ANY),
            (jax.ShapeDtypeStruct((nf, depth, sum(sizes[split:])), bf16), pl.ANY),
            (jax.ShapeDtypeStruct((8, rows, width), bf16), pl.ANY),
            (jax.ShapeDtypeStruct((count, *small.shape), f32), pltpu.VMEM),
        ],
        [vmem(), vmem()]
        + [vmem() if i in turned else anywhere for i in range(len(weights))],
        [
            pltpu.VMEM((len(turned), depth, sizes[turned[0]] * nf), bf16),
            pltpu.VMEM((8, width), f32),
            pltpu.VMEM((rows, width), bf16),
            pltpu.VMEM((rows, width), bf16),
            *gather_scratch(tokens)[1:],
            *line_scratch(),
            pltpu.SemaphoreType.DMA((2,)),
            pltpu.SemaphoreType.DMA((3 * len(weights),)),
            pltpu.SemaphoreType.DMA((6,)),
            pltpu.SemaphoreType.DMA((count,)),
            pltpu.SemaphoreType.DMA((count,)),
        ],
        tokens,
        small,
        *weights,
    )


def hand_steps(parts, outs, slots, send, recv):
    f = lax.axis_index("fsdp")
    near = beside(f)
    starts = [sum(part.shape[2] for part in parts[:i]) for i in range(len(parts))]

    def copies(n):
        return [
            remote(
                part.at[near[n]],
                slots.at[n, :, pl.ds(at, part.shape[2])],
                send.at[len(parts) * n + i],
                recv.at[len(parts) * n + i],
                {"fsdp": near[n]},
            )
            for i, (part, at) in enumerate(zip(parts, starts))
        ]

    def begin():
        for n in range(3):
            for copy in copies(n):
                copy.start()

    def put(who, blocks):
        for block, targets in zip(blocks, outs):
            at = 0
            for out, turned in targets:
                size = out.shape[0 if turned else 1] // lax.axis_size("fsdp")
                where = pl.ds(pl.multiple_of(who * size, size), size)
                if turned:
                    out[where, :] = block[:, at : at + size].T
                else:
                    out[:, where] = block[:, at : at + size]
                at += size

    def end():
        put(f, [part[f] for part in parts])
        for n in range(3):
            for copy in copies(n):
                copy.wait()
            put(
                near[n],
                [slots[n, :, at : at + part.shape[2]] for part, at in zip(parts, starts)],
            )

    return begin, end


def hand_scratch(parts):
    size = sum(part.shape[2] for part in parts)
    return [
        pltpu.VMEM((3, parts[0].shape[1], size), bf16),
        pltpu.SemaphoreType.DMA((3 * len(parts),)),
        pltpu.SemaphoreType.DMA((3 * len(parts),)),
    ]


def handed(part, sizes, turned=False):
    nf, depth = part.shape[:2]
    shapes = [(nf * n, depth) if turned else (depth, nf * n) for n in sizes]
    return [(jax.ShapeDtypeStruct(shape, bf16), pltpu.VMEM) for shape in shapes]


def finish_kernel(turned, counts, *refs):
    parts, outs, scratch = refs[: len(turned)], list(refs[len(turned) : -3]), refs[-3:]
    targets = [[(outs.pop(0), turn) for _ in range(n)] for turn, n in zip(turned, counts)]
    begin, end = hand_steps(parts, targets, *scratch)
    greet_fsdp()
    begin()
    end()


def greet_fsdp():
    near = beside(lax.axis_index("fsdp"))
    barrier = pltpu.get_barrier_semaphore()
    for who in near:
        pl.semaphore_signal(barrier, inc=1, device_id={"fsdp": who}, device_id_type=MESH)
    pl.semaphore_wait(barrier, 3)


def finish(parts, sizes, turned, collective_id):
    outs = [one for n in zip(parts, sizes, turned) for one in handed(*n)]
    outs = call(
        functools.partial(finish_kernel, turned, [len(size) for size in sizes]),
        collective_id,
        outs,
        [vmem()] * len(parts),
        hand_scratch(parts),
        *parts,
    )
    return [out.astype(f32) for out in outs]


def halves_kernel(own, out, keep, send, recv):
    t = lax.axis_index("tp")
    core = {"tp": 1 - t}
    barrier = pltpu.get_barrier_semaphore()
    pl.semaphore_signal(barrier, inc=1, device_id=core, device_id_type=MESH)
    pl.semaphore_wait(barrier, 1)
    copy = remote(own, out.at[t], send, recv, core)
    copy.start()
    local = pltpu.make_async_copy(own, out.at[t], keep)
    local.start()
    local.wait()
    copy.wait()


def both_halves(own, collective_id):
    (out,) = call(
        halves_kernel,
        collective_id,
        [(jax.ShapeDtypeStruct((2, *own.shape), own.dtype), pl.ANY)],
        [pl.BlockSpec(memory_space=pl.ANY)],
        [pltpu.SemaphoreType.DMA] * 3,
        own,
    )
    return out


def total_kernel(parts, out, slots, send, recv):
    nc, nt = lax.axis_size("ctx"), lax.axis_size("tp")
    count = parts.shape[0]
    place = (lax.axis_index("fsdp") * nc + lax.axis_index("ctx")) * nt + lax.axis_index("tp")
    barrier = pltpu.get_barrier_semaphore()

    def hello(i, carry):
        other = peer_of(lax.rem(place + i, count), nc, nt)
        pl.semaphore_signal(barrier, inc=1, device_id=other, device_id_type=MESH)
        return carry

    lax.fori_loop(1, count, hello, 0)
    pl.semaphore_wait(barrier, count - 1)

    def copy(i):
        other = lax.rem(place + i, count)
        return remote(
            parts.at[other], slots.at[i], send.at[i], recv.at[i], peer_of(other, nc, nt)
        )

    def go(i, carry):
        copy(i).start()
        return carry

    lax.fori_loop(1, count, go, 0)

    def add(i, carry):
        copy(i).wait()
        return carry + slots[i]

    out[...] = lax.fori_loop(1, count, add, parts[place])


def total_small(parts, collective_id):
    count = parts.shape[0]
    return pl.pallas_call(
        total_kernel,
        out_shape=jax.ShapeDtypeStruct(parts.shape[1:], parts.dtype),
        in_specs=[pl.BlockSpec(memory_space=pltpu.VMEM)],
        out_specs=pl.BlockSpec(memory_space=pltpu.VMEM),
        scratch_shapes=[
            pltpu.VMEM(parts.shape, parts.dtype),
            pltpu.SemaphoreType.DMA((count,)),
            pltpu.SemaphoreType.DMA((count,)),
        ],
        compiler_params=pltpu.CompilerParams(collective_id=collective_id, has_side_effects=True),
        cost_estimate=pl.CostEstimate(flops=0, bytes_accessed=1_000_000, transcendentals=0),
    )(parts)


def shards(
    tokens,
    lengths,
    cotangent,
    pre_gain,
    pre_bias,
    query_weight,
    key_weight,
    value_weight,
    swish_weight,
    out_weight,
    group_gain,
    group_bias,
    mlp_gain,
    mlp_bias,
    gelu_weight,
    up_weight,
    down_weight,
):
    seq_count, span, width = tokens.shape
    nf, nc, nt = lax.axis_size("fsdp"), lax.axis_size("ctx"), lax.axis_size("tp")
    f, c, t = lax.axis_index("fsdp"), lax.axis_index("ctx"), lax.axis_index("tp")
    block_rows = seq_count * span
    own_rows = block_rows // nt
    depth = query_weight.shape[0]
    heads_local = group_gain.shape[0]
    assert heads_local == nf
    key_size = query_weight.shape[1] // heads_local
    value_size = value_weight.shape[1] // heads_local
    hidden_size = gelu_weight.shape[1] // nf
    seqs = nf * seq_count
    rows = seqs * span
    head = t * heads_local + f

    def pad_tile(v):
        return jnp.pad(v, [(0, 0)] * (v.ndim - 1) + [(0, -v.shape[-1] % 1024)]).reshape(
            *v.shape[:-1], 8, -1
        )

    def own_part(v):
        return lax.dynamic_slice_in_dim(v.reshape(block_rows, width), t * own_rows, own_rows, 0)

    def all_depths(mine):
        return lax.all_gather(mine, "ctx", axis=0, tiled=True).reshape(width, -1)

    def padded(v):
        return jnp.pad(v.astype(f32).reshape(-1), (0, 128 - v.size))

    kinds = [pre_gain, pre_bias, mlp_gain, mlp_bias, group_gain, group_bias, lengths]
    small = jnp.stack([padded(v) for v in kinds] + [jnp.zeros(128, f32)])
    weights = [query_weight, key_weight, value_weight, swish_weight]
    weights += [out_weight, gelu_weight, up_weight, down_weight]
    attn_w, rest, normed, small = start(
        tokens.reshape(block_rows, width), small, weights, 4, (4, 7), 0
    )
    small, tokens, cotangent = lax.optimization_barrier((small, tokens, cotangent))
    normed = normed.reshape(rows, width)
    out_t = all_depths(rest[..., :value_size])
    pre_gain_full, pre_bias_full, mlp_gain_full, mlp_bias_full = (
        small[:, i, :depth].reshape(width) for i in range(4)
    )
    group = small[:, 4:6, : group_gain.size].reshape(nf * nc, 2, heads_local, -1)
    group = lax.dynamic_index_in_dim(group, f, 2, False).transpose(1, 0, 2).reshape(2, value_size)
    all_lengths = small.reshape(nf, nc, 8, 128)[:, 0, 6, :seq_count].reshape(seqs)

    inputs = own_part(tokens).astype(f32)
    _, norm_in_back = jax.vjp(layer_norm, inputs, pre_gain_full, pre_bias_full)
    positions = c * span + lax.iota(jnp.int32, span)
    own_ids = t * own_rows + lax.iota(jnp.int32, own_rows)
    own_valid = (c * span + own_ids % span < lengths[own_ids // span]).astype(f32)[:, None]
    error = own_valid * own_part(cotangent).astype(f32)

    pre = product(normed, attn_w)
    valid = (positions.astype(f32)[None, :] < all_lengths[:, None]).astype(f32)[:, :, None]
    cosine, sine = turn_tables(positions, key_size // 2)
    key_scale = key_size ** (-0.5)
    query_pre = pre[:, :key_size].reshape(seqs, span, key_size)
    key_pre = pre[:, key_size : 2 * key_size].reshape(seqs, span, key_size)
    value_pre = pre[:, 2 * key_size : 2 * key_size + value_size]
    swish_pre = pre[:, 2 * key_size + value_size :]
    queries = rotate(query_pre, cosine, sine).astype(bf16)
    keys = (rotate(key_pre, cosine, sine) * key_scale * valid).astype(bf16)
    values = value_pre.astype(bf16).reshape(seqs, span, value_size)

    log_decay = jnp.log1p(-jnp.exp2(-5.0 - head.astype(f32)))
    offsets = jnp.arange(span)
    distance = (offsets[:, None] - offsets[None, :]).astype(f32)
    within_fade = jnp.where(distance >= 0, jnp.exp(jnp.maximum(distance, 0.0) * log_decay), 0.0)
    key_fade = jnp.exp((span - 1 - offsets).astype(f32) * log_decay)[:, None]
    query_fade = jnp.exp((offsets + 1).astype(f32) * log_decay)[:, None]
    block_fade = jnp.exp(span * log_decay)

    keys_faded = (keys.astype(f32) * key_fade).astype(bf16)
    queries_faded = (queries.astype(f32) * query_fade).astype(bf16)
    local_state = blocks("sjd,sje->sde", keys_faded, values)
    error_low = error.astype(bf16)
    entering, error_all = pass_and_gather(local_state, block_fade, error_low, 1, 2)
    rest, entering = lax.optimization_barrier((rest, entering))
    ff_w = all_depths(rest[..., value_size:])
    probs = (blocks("sid,sjd->sij", queries, keys) * within_fade).astype(bf16)
    mixed = blocks("sij,sje->sie", probs, values) + blocks("sid,sde->sie", queries_faded, entering)
    gated_wide, gate_back = jax.vjp(
        gate_mix, mixed.reshape(rows, value_size), swish_pre, group[0], group[1]
    )
    gated = gated_wide.astype(bf16)
    branch = scatter_product([gated], out_t, 0, 1)
    hidden = inputs + branch

    mlp_wide, norm_mid_back = jax.vjp(layer_norm, hidden, mlp_gain_full, mlp_bias_full)
    mlp_in = gather_rows(mlp_wide.astype(bf16), 4)
    inner, ff_low, ff_part = feed_forward(mlp_in, error_all, ff_w)

    def sum_depths(grads):
        grads = with_layout_constraint(grads.astype(bf16), Layout((0, 1)))
        mine = lax.psum_scatter(grads, "ctx", scatter_dimension=0, tiled=True)
        return mine.reshape(nf, depth, -1)

    ff_sum = sum_depths(ff_part)
    mlp_in_grad = scatter_product([ff_low], ff_w, 0, 6)
    hidden_norm_grad, grad_mlp_gain, grad_mlp_bias = norm_mid_back(mlp_in_grad)
    hidden_grad = error + hidden_norm_grad

    out_part, gated_grad = gather_products(hidden_grad.astype(bf16), gated, out_t, 10)
    out_sum = sum_depths(out_part)
    mixed_grad, swish_grad, grad_group_gain, grad_group_bias = gate_back(gated_grad)
    swish_low = swish_grad.astype(bf16)
    mixed_low = mixed_grad.astype(bf16).reshape(seqs, span, value_size)
    score_low = (blocks("sie,sje->sij", mixed_low, values) * within_fade).astype(bf16)
    pulled_state = blocks("sid,sie->sde", queries_faded, mixed_low)
    swish_part = product_left(normed, swish_low).astype(bf16)
    swish_part, pulled_state, ff_sum = lax.optimization_barrier(
        (swish_part, pulled_state, ff_sum)
    )
    later, mlp_out, grad_gelu, grad_up, grad_down = pass_and_scatter(
        pulled_state, block_fade, inner, ff_w, 2 * hidden_size, ff_sum, -1, 3
    )
    out_sum, swish_part, later = lax.optimization_barrier((out_sum, swish_part, later))
    swish_sum = sum_depths(swish_part)
    block_own = (own_valid * (hidden + mlp_out)).astype(bf16)
    block_out = both_halves(block_own, 8).reshape(tokens.shape)
    query_grad = blocks("sij,sjd->sid", score_low, keys) + query_fade * blocks(
        "sie,sde->sid", mixed_low, entering
    )
    key_grad = blocks("sij,sid->sjd", score_low, queries) + key_fade * blocks(
        "sje,sde->sjd", values, later
    )
    value_grad = blocks("sij,sie->sje", probs, mixed_low) + blocks(
        "sjd,sde->sje", keys_faded, later
    )
    query_low = rotate_back(query_grad, cosine, sine).astype(bf16).reshape(rows, key_size)
    key_low = rotate_back(key_grad * key_scale * valid, cosine, sine).astype(bf16)
    low = jnp.concatenate(
        [
            query_low,
            key_low.reshape(rows, key_size),
            value_grad.astype(bf16).reshape(rows, value_size),
        ],
        -1,
    )
    attn_part = product_left(normed, low).astype(bf16)
    attn_part, low = lax.optimization_barrier((attn_part, low))
    attn_sum = sum_depths(attn_part)
    normed_grad = scatter_product([low, swish_low], attn_w, 0, 7)
    swish_sum, normed_grad = lax.optimization_barrier((swish_sum, normed_grad))
    input_norm_grad, grad_pre_gain, grad_pre_bias = norm_in_back(normed_grad)
    tokens_own = (hidden_grad + input_norm_grad).astype(bf16)
    grad_tokens = both_halves(tokens_own, 8).reshape(tokens.shape)

    early_grads = finish(
        [out_sum, swish_sum],
        [[value_size], [value_size]],
        [True, False],
        9,
    )
    norm_parts = jnp.stack([grad_pre_gain, grad_pre_bias, grad_mlp_gain, grad_mlp_bias])
    norm_parts = norm_parts.reshape(4, nf * nc, 1, depth).transpose(1, 2, 0, 3)
    norm_parts = jnp.broadcast_to(norm_parts, (nf * nc, nt, 4, depth)).reshape(nf * nc, nt, -1)
    mine = lax.iota(jnp.int32, nt * heads_local) == head
    group_parts = jnp.stack([grad_group_gain, grad_group_bias]).reshape(1, 2, nf * nc, -1)
    group_parts = jnp.where(mine[:, None, None, None], group_parts, 0.0)
    group_parts = group_parts.reshape(nt, heads_local, 2, nf * nc, -1).transpose(3, 0, 2, 1, 4)
    parts = jnp.concatenate([norm_parts, group_parts.reshape(nf * nc, nt, -1)], -1)
    parts = parts.reshape(nf * nc * nt, -1)
    sums = total_small(pad_tile(parts), 5).reshape(-1)[: parts.shape[1]]
    sums, attn_sum, block_out, grad_tokens, early_grads = lax.optimization_barrier(
        (sums, attn_sum, block_out, grad_tokens, early_grads)
    )
    grad_out, grad_swish = early_grads
    grad_query, grad_key, grad_value = finish(
        [attn_sum], [[key_size, key_size, value_size]], [False], 11
    )
    norm_sums = sums[: 4 * depth].reshape(4, depth)
    group_sums = sums[4 * depth :].reshape(2, heads_local, -1)

    return (
        block_out,
        grad_tokens,
        norm_sums[0],
        norm_sums[1],
        grad_query,
        grad_key,
        grad_value,
        grad_swish,
        grad_out,
        group_sums[0],
        group_sums[1],
        norm_sums[2],
        norm_sums[3],
        grad_gelu,
        grad_up,
        grad_down,
    )


def solution(mesh):
    rows = P("fsdp", "ctx", None)
    vector = P(("fsdp", "ctx"))
    tall = P(("fsdp", "ctx"), "tp")
    wide = P("tp", ("fsdp", "ctx"))
    in_specs = (rows, P("fsdp"), rows, vector, vector, tall, tall, tall, tall, wide)
    in_specs += (wide, wide, vector, vector, tall, tall, wide)
    out_specs = (rows, rows, vector, vector, tall, tall, tall, tall, wide)
    out_specs += (wide, wide, vector, vector, tall, tall, wide)
    return jax.shard_map(shards, mesh=mesh, in_specs=in_specs, out_specs=out_specs, check_vma=False)
```

```python
import functools
import math

import jax
import jax.numpy as jnp
from jax import lax
from jax.experimental import pallas as pl
from jax.experimental.layout import Layout, with_layout_constraint
from jax.experimental.pallas import tpu as pltpu
from jax.sharding import PartitionSpec as P

eps = 1e-05
SPARE = 6 << 20
group_floor = 1.0
f32 = jnp.float32
bf16 = jnp.bfloat16


def layer_norm(values, norm_gain, norm_shift):
    centred = values - jnp.mean(values, -1, keepdims=True)
    spread = jnp.mean(centred * centred, -1, keepdims=True)
    return centred * lax.rsqrt(spread + eps) * norm_gain + norm_shift


def turn_tables(positions, half_size):
    frequency = jnp.power(10000.0, -jnp.arange(half_size).astype(f32) / half_size)
    angles = positions.astype(f32)[:, None] * frequency[None, :]
    return jnp.cos(angles), jnp.sin(angles)


def rotate(values, cosine, sine):
    half_size = values.shape[-1] // 2
    first = values[..., :half_size]
    second = values[..., half_size:]
    return jnp.concatenate([first * cosine - second * sine, second * cosine + first * sine], -1)


def rotate_back(values, cosine, sine):
    return rotate(values, cosine, -sine)


def gate_mix(mixed, swish_pre, norm_gain, norm_shift):
    centred = mixed - jnp.mean(mixed, -1, keepdims=True)
    spread = jnp.mean(centred * centred, -1, keepdims=True)
    return jax.nn.silu(swish_pre) * (
        centred * lax.rsqrt(spread + group_floor) * norm_gain + norm_shift
    )


def mlp_mix(gelu_pre, up_pre):
    return jax.nn.gelu(gelu_pre) * up_pre


def product(left, right):
    return jnp.dot(left, right, preferred_element_type=f32)


def product_left(left, right):
    return lax.dot_general(left, right, (((0,), (0,)), ((), ())), preferred_element_type=f32)


def product_right(left, right):
    return lax.dot_general(left, right, (((1,), (1,)), ((), ())), preferred_element_type=f32)


def blocks(spec, left, right):
    return jnp.einsum(spec, left, right, preferred_element_type=f32)


MESH = pl.DeviceIdType.MESH


def beside(f):
    return f + 1 - 2 * (f % 2), (f + 2) % 4, 3 - f


def remote(src, dst, send, recv, device):
    return pltpu.make_async_remote_copy(
        src_ref=src, dst_ref=dst, send_sem=send, recv_sem=recv, device_id=device, device_id_type=MESH
    )


def reorder(src, dst, kind, back):
    nf, nc = lax.axis_size("fsdp"), lax.axis_size("ctx")
    depth = src.shape[-1] // (nf * nc)
    for f in range(nf):
        for c in range(nc):
            plain, mixed = (f * nc + c) * depth, (c * nf + f) * depth
            if back:
                plain, mixed = mixed, plain
            dst[:, mixed : mixed + depth] = src[:, plain : plain + depth].astype(kind)


def gather_steps(plain, out, mixed, keep, send, recv):
    own = plain if mixed is None else mixed
    f, t = lax.axis_index("fsdp"), lax.axis_index("tp")
    fx, fy, fd = beside(f)
    x, y, core = {"fsdp": fx}, {"fsdp": fy}, {"tp": 1 - t}
    half = own.shape[0] // 2

    def part(ref, h):
        return ref.at[pl.ds(h * half, half)]

    def slot(who, h):
        return part(out.at[2 * who + t], h)

    local = pltpu.make_async_copy(own, out.at[2 * f + t], keep)
    first = [
        remote(part(own, 0), slot(f, 0), send.at[0], recv.at[0], x),
        remote(part(own, 1), slot(f, 1), send.at[1], recv.at[3], y),
        remote(part(own, 1), slot(f, 1), send.at[2], recv.at[1], x),
        remote(part(own, 0), slot(f, 0), send.at[3], recv.at[2], y),
        remote(part(own, 0), slot(f, 0), send.at[4], recv.at[6], core),
        remote(part(own, 1), slot(f, 1), send.at[5], recv.at[7], core),
    ]
    sent = list(first)

    def pass_on(who, h, s, r, device):
        copy = remote(slot(who, h), slot(who, h), send.at[s], recv.at[r], device)
        copy.start()
        sent.append(copy)

    def begin():
        if mixed is not None:
            reorder(plain, mixed, mixed.dtype, False)
        local.start()
        for copy in first:
            copy.start()

    def relay():
        first[0].wait_recv()
        pass_on(fx, 0, 6, 4, y)
        pass_on(fx, 0, 7, 8, core)
        first[1].wait_recv()
        pass_on(fy, 1, 8, 5, x)
        pass_on(fy, 1, 9, 11, core)

    def rest():
        first[2].wait_recv()
        pass_on(fx, 1, 10, 9, core)
        first[3].wait_recv()
        pass_on(fy, 0, 11, 10, core)

    def diagonal():
        remote(slot(fd, 0), slot(fd, 0), send.at[12], recv.at[4], y).wait_recv()
        pass_on(fd, 0, 12, 12, core)
        remote(slot(fd, 1), slot(fd, 1), send.at[13], recv.at[5], x).wait_recv()
        pass_on(fd, 1, 13, 13, core)

    def end(crossed=False):
        if not crossed:
            for r in range(6, 14):
                remote(slot(f, 0), slot(f, 0), send.at[0], recv.at[r], core).wait_recv()
            local.wait()
        for copy in sent:
            copy.wait_send()

    return begin, relay, rest, diagonal, end


def in_kernel(width):
    return width // (lax.axis_size("fsdp") * lax.axis_size("ctx")) % 128 == 0


def gather_scratch(own):
    return [
        pltpu.VMEM(own.shape if in_kernel(own.shape[1]) else (16, 128), own.dtype),
        pltpu.SemaphoreType.DMA,
        pltpu.SemaphoreType.DMA((14,)),
        pltpu.SemaphoreType.DMA((14,)),
    ]


def scatter_steps(start, lefts, right, out, mine, sent, theirs, total, diag, last, send, recv):
    f, t = lax.axis_index("fsdp"), lax.axis_index("tp")
    fx, fy, fd = beside(f)
    x, y, core = {"fsdp": fx}, {"fsdp": fy}, {"tp": 1 - t}
    half = out.shape[0] // 2
    order = [fd, fy, fx, f]
    tile = 512

    def part(ref, h):
        return ref.at[pl.ds(h * half, half)]

    crossing = [
        remote(sent.at[i], theirs.at[i], send.at[i], recv.at[i], core) for i in range(4)
    ]
    d0 = remote(part(total.at[0], 0), diag.at[0], send.at[4], recv.at[4], x)
    d1 = remote(part(total.at[0], 1), diag.at[1], send.at[5], recv.at[5], y)
    y1 = remote(part(total.at[1], 1), part(last.at[1], 1), send.at[6], recv.at[6], y)
    x0 = remote(part(total.at[2], 0), part(last.at[0], 0), send.at[7], recv.at[7], x)
    y0 = remote(part(total.at[1], 0), part(last.at[1], 0), send.at[8], recv.at[8], y)
    x1 = remote(part(total.at[2], 1), part(last.at[0], 1), send.at[9], recv.at[9], x)

    def make(block, put):
        def piece(j, carry):
            columns = pl.ds(pl.multiple_of(j * tile, tile), tile)
            at, value = start, 0.0
            for left in lefts:
                size = left.shape[2]
                value += product_right(left[block], right[columns, at : at + size])
                at += size
            put(columns, value)
            return carry

        lax.fori_loop(0, out.shape[1] // tile, piece, 0)

    def cross(i):
        def put(columns, value):
            sent[i, :, columns] = value.astype(sent.dtype)

        make(2 * order[i] + 1 - t, put)
        crossing[i].start()

    def keep(i):
        def put(columns, value):
            mine[:, columns] = value

        make(2 * order[i] + t, put)

    def add(i):
        keep(i)
        crossing[i].wait_recv()
        total[i] = (mine[...] + theirs[i].astype(f32)).astype(total.dtype)

    def diagonal():
        cross(0)
        cross(1)
        add(0)
        d0.start()
        d1.start()

    def straight():
        cross(2)
        add(1)
        y1.start()
        add(2)
        x0.start()
        cross(3)

    def relay():
        d0.wait_recv()
        total[1, :half] = (total[1, :half].astype(f32) + diag[0].astype(f32)).astype(total.dtype)
        y0.start()
        d1.wait_recv()
        total[2, half:] = (total[2, half:].astype(f32) + diag[1].astype(f32)).astype(total.dtype)
        x1.start()
        keep(3)
        crossing[3].wait_recv()
        mine[...] += theirs[3].astype(f32)

    def end():
        for copy in (y1, x0, y0, x1):
            copy.wait_recv()
        mine[...] += last[0].astype(f32) + last[1].astype(f32)
        if in_kernel(out.shape[1]):
            reorder(mine, out, out.dtype, True)
        else:
            out[...] = mine[...]
        for copy in (*crossing, d0, d1, y1, x0, y0, x1):
            copy.wait_send()

    return diagonal, straight, relay, end


def scatter_scratch(rows, width):
    return [
        pltpu.VMEM((rows, width), f32),
        pltpu.VMEM((4, rows, width), bf16),
        pltpu.VMEM((4, rows, width), bf16),
        pltpu.VMEM((3, rows, width), bf16),
        pltpu.VMEM((2, rows // 2, width), bf16),
        pltpu.VMEM((2, rows, width), bf16),
        pltpu.SemaphoreType.DMA((10,)),
        pltpu.SemaphoreType.DMA((10,)),
    ]


def pass_steps(by, local, fade, out, held, send, recv):
    length = lax.axis_size("ctx")
    c = lax.axis_index("ctx")
    first = c == (0 if by > 0 else length - 1)
    last = c == (length - 1 if by > 0 else 0)
    target = lax.rem(c + by + length, length)

    def copy(p):
        return remote(held.at[p], out.at[p], send.at[p], recv.at[p], {"ctx": target})

    def step(p, carry):
        @pl.when(first)
        def _():
            out[p] = jnp.zeros(out.shape[1:], out.dtype)

        @pl.when(jnp.logical_not(first))
        def _():
            copy(p).wait_recv()

        @pl.when(jnp.logical_not(last))
        def _():
            held[p] = (fade[...] * out[p].astype(f32) + local[p]).astype(held.dtype)
            copy(p).start()

        return carry

    def run(quarter):
        count = local.shape[0]
        if quarter < 0:
            lax.fori_loop(0, jnp.where(first, count, 0), step, 0)
        else:
            low, high = quarter * count // 4, (quarter + 1) * count // 4
            lax.fori_loop(jnp.where(first, count, low), jnp.where(first, count, high), step, 0)

    def end():
        @pl.when(jnp.logical_not(last))
        def _():
            def done(p, carry):
                copy(p).wait_send()
                return carry

            lax.fori_loop(0, local.shape[0], done, 0)

    return run, end


def greet_plane(by=0, diagonal=False):
    f, c, t = lax.axis_index("fsdp"), lax.axis_index("ctx"), lax.axis_index("tp")
    length = lax.axis_size("ctx")
    fx, fy, fd = beside(f)
    barrier = pltpu.get_barrier_semaphore()
    peers = [{"fsdp": fx}, {"fsdp": fy}, {"tp": 1 - t}] + [{"fsdp": fd}] * diagonal
    for device in peers:
        pl.semaphore_signal(barrier, inc=1, device_id=device, device_id_type=MESH)
    if by != 0:
        first = c == (0 if by > 0 else length - 1)
        last = c == (length - 1 if by > 0 else 0)
        source = {"ctx": lax.rem(c - by + length, length)}

        @pl.when(jnp.logical_not(first))
        def _():
            pl.semaphore_signal(barrier, inc=1, device_id=source, device_id_type=MESH)

        @pl.when(jnp.logical_not(last))
        def _():
            pl.semaphore_wait(barrier, len(peers) + 1)

        @pl.when(last)
        def _():
            pl.semaphore_wait(barrier, len(peers))
    else:
        pl.semaphore_wait(barrier, len(peers))


def gather_with(own, full, mixed, *scratch):
    return gather_steps(own, full, mixed if in_kernel(own.shape[1]) else None, *scratch)


def gather_kernel(*refs):
    steps = gather_with(*refs)
    greet_plane()
    for step in steps:
        step()


def scatter_kernel(count, start, *refs):
    steps = scatter_steps(start, refs[:count], *refs[count:])
    greet_plane()
    for step in steps:
        step()


def gather_products_kernel(own, left, right, grad, back, full, total, mixed, *scratch):
    f, t = lax.axis_index("fsdp"), lax.axis_index("tp")
    fx, fy, fd = beside(f)
    recv = scratch[2]
    begin, relay, rest, diagonal, end = gather_with(own, full, mixed, *scratch)
    tile = 512

    def use(block, fresh=False):
        back[block] = product(full[block], right[...])

        def piece(j, carry):
            columns = pl.ds(pl.multiple_of(j * tile, tile), tile)
            value = product_left(full[block, :, columns], left[block])
            total[columns, :] = value if fresh else total[columns, :] + value
            return carry

        lax.fori_loop(0, total.shape[0] // tile, piece, 0)

    def crossed(who, r):
        block = full.at[2 * who + 1 - t]
        half = block.shape[0] // 2
        for h in range(2):
            where = block.at[pl.ds(h * half, half)]
            remote(where, where, scratch[1].at[0], recv.at[r + h], {"tp": 1 - t}).wait_recv()

    greet_plane()
    begin()
    pltpu.make_async_copy(full.at[2 * f + t], full.at[2 * f + t], scratch[0]).wait()
    use(2 * f + t, True)
    relay()
    crossed(f, 6)
    use(2 * f + 1 - t)
    rest()
    use(2 * fx + t)
    use(2 * fy + t)
    crossed(fx, 8)
    use(2 * fx + 1 - t)
    crossed(fy, 10)
    use(2 * fy + 1 - t)
    diagonal()
    use(2 * fd + t)
    crossed(fd, 12)
    use(2 * fd + 1 - t)
    end(True)
    grad[...] = total[...].astype(grad.dtype)


def gather_products(own, left, right, collective_id):
    own = ready(own)
    rows, width = own.shape
    size = left.shape[1]
    grad, back = call(
        gather_products_kernel,
        collective_id,
        [
            (jax.ShapeDtypeStruct((width, size), bf16), pltpu.VMEM),
            (jax.ShapeDtypeStruct((8, rows, size), f32), pltpu.VMEM),
        ],
        [vmem()] * 3,
        [
            pltpu.VMEM((8, rows, width), bf16),
            pltpu.VMEM((width, size), f32),
            *gather_scratch(own),
        ],
        own,
        in_eights(left),
        right,
        tight=True,
    )
    return grad, back.reshape(8 * rows, size)


def pass_gather_kernel(by, local, fade, own, out, full, held, send, recv, *scratch):
    begin, relay, rest, diagonal, end = gather_with(own, full, *scratch)
    run, done = pass_steps(by, local, fade, out, held, send, recv)
    greet_plane(by)
    begin()
    run(-1)
    run(0)
    relay()
    run(1)
    rest()
    run(2)
    run(3)
    diagonal()
    end()
    done()


def pass_scatter_kernel(by, start, local, fade, left, right, ff, out, own, *refs):
    gelu_grad, up_grad, down_grad, held, send, recv = refs[:6]
    scratch, hand = refs[6:-3], refs[-3:]
    targets = [[(gelu_grad, False), (up_grad, False), (down_grad, True)]]
    hand_over, take = hand_steps([ff], targets, *hand)
    diagonal, straight, relay, end = scatter_steps(start, [left], right, own, *scratch)
    run, done = pass_steps(by, local, fade, out, held, send, recv)
    greet_plane(by, True)
    run(-1)
    diagonal()
    straight()
    run(0)
    run(1)
    relay()
    hand_over()
    run(2)
    run(3)
    end()
    take()
    done()


def held_bytes(array):
    last = -(-array.shape[-1] // 128) * 128
    return math.prod(array.shape[:-1]) * last * jnp.dtype(array.dtype).itemsize


def call(kernel, collective_id, outs, ins, scratch, *args, tight=False):
    shapes, spaces = zip(*outs)
    limit = 52 << 20
    held = [shape for shape, space in outs if space == pltpu.VMEM]
    held += [arg for arg, spec in zip(args, ins) if spec.memory_space == pltpu.VMEM]
    held += [one for one in scratch if getattr(one, "memory_space", None) == pltpu.VMEM]
    if tight:
        limit = sum(held_bytes(one) for one in held) + SPARE
    return pl.pallas_call(
        kernel,
        out_shape=shapes,
        in_specs=ins,
        out_specs=tuple(pl.BlockSpec(memory_space=space) for space in spaces),
        scratch_shapes=scratch,
        compiler_params=pltpu.CompilerParams(
            collective_id=collective_id, has_side_effects=True, vmem_limit_bytes=limit
        ),
        cost_estimate=pl.CostEstimate(flops=0, bytes_accessed=2_000_000, transcendentals=0),
    )(*args)


def vmem():
    return pl.BlockSpec(memory_space=pltpu.VMEM)


def perm(v):
    nf, nc = lax.axis_size("fsdp"), lax.axis_size("ctx")
    return v.reshape(len(v), nf, nc, -1).transpose(0, 2, 1, 3).reshape(v.shape)


def unperm(v):
    nf, nc = lax.axis_size("fsdp"), lax.axis_size("ctx")
    return v.reshape(len(v), nc, nf, -1).transpose(0, 2, 1, 3).reshape(v.shape)


def gathered(own):
    rows, width = own.shape
    return jax.ShapeDtypeStruct((8, rows, width), own.dtype), pl.ANY


def scattered(left, right):
    return jax.ShapeDtypeStruct((left.shape[0] // 8, right.shape[0]), f32), pltpu.VMEM


def passed(local):
    return jax.ShapeDtypeStruct(local.shape, bf16), pltpu.VMEM


def pass_scratch(local):
    pieces = local.shape[0]
    return [
        pltpu.VMEM(local.shape, bf16),
        pltpu.SemaphoreType.DMA((pieces,)),
        pltpu.SemaphoreType.DMA((pieces,)),
    ]


def in_eights(left):
    return left.reshape(8, -1, left.shape[1])


def ready(own):
    return own if in_kernel(own.shape[1]) else perm(own)


def plain(own):
    return own if in_kernel(own.shape[1]) else unperm(own)


def gather_rows(own, collective_id):
    own = ready(own)
    (out,) = call(gather_kernel, collective_id, [gathered(own)], [vmem()], gather_scratch(own), own)
    return out.reshape(-1, own.shape[1])


def scatter_product(lefts, right, start, collective_id):
    rows, width = lefts[0].shape[0] // 8, right.shape[0]
    (out,) = call(
        functools.partial(scatter_kernel, len(lefts), start),
        collective_id,
        [(jax.ShapeDtypeStruct((rows, width), f32), pltpu.VMEM)],
        [vmem()] * (len(lefts) + 1),
        scatter_scratch(rows, width),
        *(in_eights(left) for left in lefts),
        right,
    )
    return plain(out)


def pass_and_gather(local, fade, own, by, collective_id):
    shape = local.shape
    local = local.reshape(2 * shape[0], -1, shape[2])
    own = ready(own)
    out, full = call(
        functools.partial(pass_gather_kernel, by),
        collective_id,
        [passed(local), gathered(own)],
        [vmem(), vmem(), vmem()],
        pass_scratch(local) + gather_scratch(own),
        local,
        jnp.full((1, local.shape[2]), fade, f32),
        own,
    )
    return out.reshape(shape), full.reshape(-1, own.shape[1])


def feed_forward_kernel(rows, error, weight, inner, low, grads, total):
    step = pl.program_id(0)
    size, tile, deep = inner.shape[1], 512, 1024
    root = (2.0 / jnp.pi) ** 0.5

    def units(j, carry):
        at = pl.multiple_of(j * tile, tile)
        gelu_pre = product(rows[...], weight[:, pl.ds(at, tile)])
        up_pre = product(rows[...], weight[:, pl.ds(at + size, tile)])
        square = gelu_pre * gelu_pre
        bend = jnp.tanh(root * gelu_pre * (1.0 + 0.044715 * square))
        half = 0.5 * (1.0 + bend)
        gelu = gelu_pre * half
        slope = half + 0.5 * gelu_pre * (1.0 - bend * bend) * root * (1.0 + 0.134145 * square)
        inner[:, pl.ds(at, tile)] = (gelu * up_pre).astype(bf16)
        inner_grad = product(error[...], weight[:, pl.ds(at + 2 * size, tile)])
        low[:, pl.ds(at, tile)] = (inner_grad * up_pre * slope).astype(bf16)
        low[:, pl.ds(at + size, tile)] = (inner_grad * gelu).astype(bf16)
        return carry

    lax.fori_loop(0, size // tile, units, 0)

    def depths(first, last):
        def piece(j, carry):
            at = pl.ds(pl.multiple_of(j * deep, deep), deep)
            into = grads if last else total
            for left, right, columns in (
                (rows, low, slice(0, 2 * size)),
                (error, inner, slice(2 * size, 3 * size)),
            ):
                value = product_left(left[:, at], right[...])
                if not first:
                    value += total[at, columns]
                into[at, columns] = value.astype(into.dtype)
            return carry

        lax.fori_loop(0, total.shape[0] // deep, piece, 0)

    steps = pl.num_programs(0)
    pl.when(step == 0)(lambda: depths(True, False))
    pl.when((step > 0) & (step < steps - 1))(lambda: depths(False, False))
    pl.when(step == steps - 1)(lambda: depths(False, True))


def feed_forward(rows, error, weight):
    count, width = rows.shape
    size, block = weight.shape[1] // 3, 512
    whole = pl.BlockSpec(weight.shape, lambda i: (0, 0))

    def some(columns):
        return pl.BlockSpec((block, columns), lambda i: (i, 0))

    return pl.pallas_call(
        feed_forward_kernel,
        grid=(count // block,),
        out_shape=(
            jax.ShapeDtypeStruct((count, size), bf16),
            jax.ShapeDtypeStruct((count, 2 * size), bf16),
            jax.ShapeDtypeStruct(weight.shape, bf16),
        ),
        in_specs=[some(width), some(width), whole],
        out_specs=(some(size), some(2 * size), whole),
        scratch_shapes=[pltpu.VMEM(weight.shape, f32)],
        compiler_params=pltpu.CompilerParams(vmem_limit_bytes=56 << 20),
        cost_estimate=pl.CostEstimate(
            flops=14 * count * width * size, bytes_accessed=40_000_000, transcendentals=count * size
        ),
    )(rows, error, weight)


def pass_and_scatter(local, fade, left, right, start, ff, by, collective_id):
    shape = local.shape
    local = local.reshape(2 * shape[0], -1, shape[2])
    out, own, *grads = call(
        functools.partial(pass_scatter_kernel, by, start),
        collective_id,
        [
            passed(local),
            scattered(left, right),
            *handed(ff, [left.shape[1]] * 2),
            *handed(ff, [left.shape[1]], True),
        ],
        [vmem()] * 5,
        pass_scratch(local)
        + scatter_scratch(left.shape[0] // 8, right.shape[0])
        + hand_scratch([ff]),
        local,
        jnp.full((1, local.shape[2]), fade, f32),
        in_eights(left),
        right,
        ff,
    )
    return out.reshape(shape), plain(own), *(grad.astype(f32) for grad in grads)


def peer_of(place, nc, nt):
    return {"fsdp": place // (nc * nt), "ctx": place // nt % nc, "tp": place % nt}


def line_steps(home, place, arrived, send, recv):
    nf, nc = lax.axis_size("fsdp"), lax.axis_size("ctx")
    f, c = lax.axis_index("fsdp"), lax.axis_index("ctx")
    order = [f, *beside(f)]
    above, below = c < nc - 1, c > 0

    def copy(src, place_of, who, up):
        chunk = place_of * nf + who
        return remote(
            src,
            place(place_of, who),
            send.at[chunk if up else nc * nf + chunk],
            recv.at[chunk],
            {"ctx": lax.rem(c + 1, nc) if up else lax.rem(c + nc - 1, nc)},
        )

    def first(i):
        who = order[i]
        arrived(i)

        @pl.when(above)
        def _():
            copy(home(who), c, who, True).start()

        @pl.when(below)
        def _():
            copy(home(who), c, who, False).start()

    def step(k, carry):
        for who in order:

            @pl.when(c - k >= 0)
            def _():
                copy(place(c - k, who), c - k, who, True).wait_recv()

                @pl.when(above)
                def _():
                    copy(place(c - k, who), c - k, who, True).start()

            @pl.when(c + k < nc)
            def _():
                copy(place(c + k, who), c + k, who, False).wait_recv()

                @pl.when(below)
                def _():
                    copy(place(c + k, who), c + k, who, False).start()

        return carry

    def end():
        def one(other, carry):
            for who in order:

                @pl.when(above & (other <= c))
                def _():
                    copy(place(other, who), other, who, True).wait_send()

                @pl.when(below & (other >= c))
                def _():
                    copy(place(other, who), other, who, False).wait_send()

            return carry

        lax.fori_loop(0, nc, one, 0)

    return first, step, end


def line_scratch():
    count = lax.axis_size("fsdp") * lax.axis_size("ctx")
    return [pltpu.SemaphoreType.DMA((2 * count,)), pltpu.SemaphoreType.DMA((count,))]


def start_kernel(sizes, split, turned, own, small, *refs):
    count = len(sizes)
    weights = list(refs[:count])
    attn, rest, full, everyone = refs[count : count + 4]
    (
        brought,
        untouched,
        fetch,
        turns,
        gains,
        normed,
        mixed,
        gather_keep,
        gather_send,
        gather_recv,
        line_send,
        line_recv,
        keep,
        send,
        recv,
        small_send,
        small_recv,
    ) = refs[count + 4 :]
    nf, nc = lax.axis_size("fsdp"), lax.axis_size("ctx")
    f, c, t = lax.axis_index("fsdp"), lax.axis_index("ctx"), lax.axis_index("tp")
    here, places = f * nc + c, nf * nc
    depth = weights[0].shape[0]
    across = [weights[i] for i in turned]
    for n, i in enumerate(turned):
        weights[i] = turns.at[n]
    rows = normed.shape[0]
    fetched = [
        pltpu.make_async_copy(
            own.at[pl.ds(pl.multiple_of(t * rows, rows), rows)], brought, fetch.at[0]
        )
    ]
    fetched += [
        pltpu.make_async_copy(matrix, untouched.at[n], fetch.at[n + 1])
        for n, matrix in enumerate(across)
    ]
    for copy in fetched:
        copy.start()
    near = beside(f)
    starts = [sum(sizes[:i]) if i < split else sum(sizes[split:i]) for i in range(count)]

    def peer(i):
        other = lax.rem(here + i, places)
        return {"fsdp": other // nc, "ctx": other % nc}

    barrier = pltpu.get_barrier_semaphore()
    pl.semaphore_signal(barrier, inc=1, device_id={"tp": 1 - t}, device_id_type=MESH)

    def hello(i, carry):
        pl.semaphore_signal(barrier, inc=1, device_id=peer(i), device_id_type=MESH)
        return carry

    lax.fori_loop(1, places, hello, 0)
    pl.semaphore_wait(barrier, places)

    def chunk(place_of, who):
        rows = pl.multiple_of((place_of * nf + who) * depth, depth)
        return attn.at[pl.ds(rows, depth)]

    def columns(i, who):
        return weights[i].at[:, pl.ds(pl.multiple_of(who * sizes[i], sizes[i]), sizes[i])]

    def target(i):
        where = chunk(c, f) if i < split else rest.at[f]
        return where.at[:, pl.ds(starts[i], sizes[i])]

    def hand_out(i, n):
        return remote(
            columns(i, near[n]),
            target(i),
            send.at[3 * i + n],
            recv.at[n if i < split else 3 + n],
            {"fsdp": near[n]},
        )

    def hold(i):
        return pltpu.make_async_copy(columns(i, f), target(i), keep.at[0 if i < split else 1])

    for i in range(split):
        hold(i).start()
    for n in range(3):
        for i in range(split):
            hand_out(i, n).start()

    def arrived(i):
        if i == 0:
            pltpu.make_async_copy(chunk(c, f), chunk(c, f), keep.at[0]).wait()
        else:
            who = near[i - 1]
            remote(
                chunk(c, who), chunk(c, who), send.at[0], recv.at[i - 1], {"fsdp": who}
            ).wait_recv()

    first, step, end = line_steps(lambda who: chunk(c, who), chunk, arrived, line_send, line_recv)
    first(0)

    def tell(i):
        return remote(small, everyone.at[here], small_send.at[i], small_recv.at[i], peer(i))

    def go(i, carry):
        tell(i).start()
        return carry

    def told(i, carry):
        tell(i).wait()
        return carry

    lax.fori_loop(1, places, go, 0)
    everyone[here] = small[...]
    first(1)
    lax.fori_loop(1, places, told, 0)
    for i in range(places):
        for j in range(2):
            gains[j : j + 1, i * depth : (i + 1) * depth] = everyone[i, j : j + 1, :depth]
    fetched[0].wait()
    normed[...] = layer_norm(brought[...].astype(f32), gains[0:1, :], gains[1:2, :]).astype(bf16)
    begin, relay, others, diagonal, finish = gather_steps(
        normed, full, mixed, gather_keep, gather_send, gather_recv
    )
    begin()
    first(2)
    first(3)
    step(1, 0)
    relay()
    for n in range(len(turned)):
        fetched[n + 1].wait()
        turns[n] = untouched[n].T
    for i in range(split, count):
        hold(i).start()
        for n in range(3):
            hand_out(i, n).start()
    lax.fori_loop(2, 3, step, 0)
    others()
    diagonal()
    lax.fori_loop(3, nc, step, 0)
    finish()
    pltpu.make_async_copy(rest.at[f], rest.at[f], keep.at[1]).wait()
    for n in range(3):
        where = rest.at[near[n]]
        remote(where, where, send.at[0], recv.at[3 + n], {"fsdp": near[n]}).wait_recv()
    for i in range(count):
        for n in range(3):
            hand_out(i, n).wait_send()
    end()


def start(tokens, small, weights, split, turned, collective_id):
    nf, nc = lax.axis_size("fsdp"), lax.axis_size("ctx")
    rows, width = tokens.shape
    rows //= lax.axis_size("tp")
    depth = weights[0].shape[0]
    sizes = [w.size // depth // nf for w in weights]
    anywhere = pl.BlockSpec(memory_space=pl.ANY)
    count = nf * nc
    return call(
        functools.partial(start_kernel, sizes, split, turned),
        collective_id,
        [
            (jax.ShapeDtypeStruct((width, sum(sizes[:split])), bf16), pl.ANY),
            (jax.ShapeDtypeStruct((nf, depth, sum(sizes[split:])), bf16), pl.ANY),
            (jax.ShapeDtypeStruct((8, rows, width), bf16), pl.ANY),
            (jax.ShapeDtypeStruct((count, *small.shape), f32), pltpu.VMEM),
        ],
        [anywhere, vmem()] + [anywhere] * len(weights),
        [
            pltpu.VMEM((rows, width), bf16),
            pltpu.VMEM((len(turned), *weights[turned[0]].shape), bf16),
            pltpu.SemaphoreType.DMA((len(turned) + 1,)),
            pltpu.VMEM((len(turned), depth, sizes[turned[0]] * nf), bf16),
            pltpu.VMEM((8, width), f32),
            pltpu.VMEM((rows, width), bf16),
            pltpu.VMEM((rows, width), bf16),
            *gather_scratch(tokens)[1:],
            *line_scratch(),
            pltpu.SemaphoreType.DMA((2,)),
            pltpu.SemaphoreType.DMA((3 * len(weights),)),
            pltpu.SemaphoreType.DMA((6,)),
            pltpu.SemaphoreType.DMA((count,)),
            pltpu.SemaphoreType.DMA((count,)),
        ],
        tokens,
        small,
        *weights,
    )


def hand_steps(parts, outs, slots, send, recv):
    f = lax.axis_index("fsdp")
    near = beside(f)
    starts = [sum(part.shape[2] for part in parts[:i]) for i in range(len(parts))]

    def copies(n):
        return [
            remote(
                part.at[near[n]],
                slots.at[n, :, pl.ds(at, part.shape[2])],
                send.at[len(parts) * n + i],
                recv.at[len(parts) * n + i],
                {"fsdp": near[n]},
            )
            for i, (part, at) in enumerate(zip(parts, starts))
        ]

    def begin():
        for n in range(3):
            for copy in copies(n):
                copy.start()

    def put(who, blocks):
        for block, targets in zip(blocks, outs):
            at = 0
            for out, turned in targets:
                size = out.shape[0 if turned else 1] // lax.axis_size("fsdp")
                where = pl.ds(pl.multiple_of(who * size, size), size)
                if turned:
                    out[where, :] = block[:, at : at + size].T
                else:
                    out[:, where] = block[:, at : at + size]
                at += size

    def end():
        put(f, [part[f] for part in parts])
        for n in range(3):
            for copy in copies(n):
                copy.wait()
            put(
                near[n],
                [slots[n, :, at : at + part.shape[2]] for part, at in zip(parts, starts)],
            )

    return begin, end


def hand_scratch(parts):
    size = sum(part.shape[2] for part in parts)
    return [
        pltpu.VMEM((3, parts[0].shape[1], size), bf16),
        pltpu.SemaphoreType.DMA((3 * len(parts),)),
        pltpu.SemaphoreType.DMA((3 * len(parts),)),
    ]


def handed(part, sizes, turned=False):
    nf, depth = part.shape[:2]
    shapes = [(nf * n, depth) if turned else (depth, nf * n) for n in sizes]
    return [(jax.ShapeDtypeStruct(shape, bf16), pltpu.VMEM) for shape in shapes]


def finish_kernel(turned, counts, *refs):
    parts, outs, scratch = refs[: len(turned)], list(refs[len(turned) : -3]), refs[-3:]
    targets = [[(outs.pop(0), turn) for _ in range(n)] for turn, n in zip(turned, counts)]
    begin, end = hand_steps(parts, targets, *scratch)
    greet_fsdp()
    begin()
    end()


def greet_fsdp():
    near = beside(lax.axis_index("fsdp"))
    barrier = pltpu.get_barrier_semaphore()
    for who in near:
        pl.semaphore_signal(barrier, inc=1, device_id={"fsdp": who}, device_id_type=MESH)
    pl.semaphore_wait(barrier, 3)


def finish(parts, sizes, turned, collective_id):
    outs = [one for n in zip(parts, sizes, turned) for one in handed(*n)]
    outs = call(
        functools.partial(finish_kernel, turned, [len(size) for size in sizes]),
        collective_id,
        outs,
        [vmem()] * len(parts),
        hand_scratch(parts),
        *parts,
        tight=True,
    )
    return [out.astype(f32) for out in outs]


def total_steps(parts, out, slots, send, recv):
    nc, nt = lax.axis_size("ctx"), lax.axis_size("tp")
    count = parts.shape[0]
    place = (lax.axis_index("fsdp") * nc + lax.axis_index("ctx")) * nt + lax.axis_index("tp")

    def hello():
        barrier = pltpu.get_barrier_semaphore()

        def one(i, carry):
            other = peer_of(lax.rem(place + i, count), nc, nt)
            pl.semaphore_signal(barrier, inc=1, device_id=other, device_id_type=MESH)
            return carry

        lax.fori_loop(1, count, one, 0)
        pl.semaphore_wait(barrier, count - 1)

    def copy(i):
        other = lax.rem(place + i, count)
        return remote(
            parts.at[other], slots.at[i], send.at[i], recv.at[i], peer_of(other, nc, nt)
        )

    def begin():
        def go(i, carry):
            copy(i).start()
            return carry

        lax.fori_loop(1, count, go, 0)

    def end():
        def add(i, carry):
            copy(i).wait()
            return carry + slots[i]

        out[...] = lax.fori_loop(1, count, add, parts[place])

    return hello, begin, end


def close_kernel(
    parts, first, second, one, two, out, wide, tall, one_both, two_both, slots, send, recv, *scratch
):
    hand, keep, core_send, core_recv = scratch[:3], *scratch[3:]
    t = lax.axis_index("tp")
    hello, begin, end = total_steps(parts, out, slots, send, recv)
    hand_over, take = hand_steps([first, second], [[(wide, True)], [(tall, False)]], *hand)
    hello()
    begin()
    copies = []
    for i, (own, both) in enumerate(((one, one_both), (two, two_both))):
        copies.append(pltpu.make_async_copy(own, both.at[t], keep.at[i]))
        copies.append(
            remote(own, both.at[t], core_send.at[i], core_recv.at[i], {"tp": 1 - t})
        )
    for copy in copies:
        copy.start()
    end()
    for copy in copies:
        copy.wait()
    hand_over()
    take()


def close(parts, first, second, one, two, collective_id):
    count = parts.shape[0]
    both = (jax.ShapeDtypeStruct((2, *one.shape), one.dtype), pltpu.VMEM)
    return call(
        close_kernel,
        collective_id,
        [
            (jax.ShapeDtypeStruct(parts.shape[1:], f32), pltpu.VMEM),
            *handed(first, [first.shape[2]], True),
            *handed(second, [second.shape[2]]),
            both,
            both,
        ],
        [vmem()] * 5,
        [
            pltpu.VMEM(parts.shape, f32),
            pltpu.SemaphoreType.DMA((count,)),
            pltpu.SemaphoreType.DMA((count,)),
            *hand_scratch([first, second]),
            pltpu.SemaphoreType.DMA((2,)),
            pltpu.SemaphoreType.DMA((2,)),
            pltpu.SemaphoreType.DMA((2,)),
        ],
        parts,
        first,
        second,
        one,
        two,
        tight=True,
    )


def shards(
    tokens,
    lengths,
    cotangent,
    pre_gain,
    pre_bias,
    query_weight,
    key_weight,
    value_weight,
    swish_weight,
    out_weight,
    group_gain,
    group_bias,
    mlp_gain,
    mlp_bias,
    gelu_weight,
    up_weight,
    down_weight,
):
    seq_count, span, width = tokens.shape
    nf, nc, nt = lax.axis_size("fsdp"), lax.axis_size("ctx"), lax.axis_size("tp")
    f, c, t = lax.axis_index("fsdp"), lax.axis_index("ctx"), lax.axis_index("tp")
    block_rows = seq_count * span
    own_rows = block_rows // nt
    depth = query_weight.shape[0]
    heads_local = group_gain.shape[0]
    assert heads_local == nf
    key_size = query_weight.shape[1] // heads_local
    value_size = value_weight.shape[1] // heads_local
    hidden_size = gelu_weight.shape[1] // nf
    seqs = nf * seq_count
    rows = seqs * span
    head = t * heads_local + f

    def pad_tile(v):
        return jnp.pad(v, [(0, 0)] * (v.ndim - 1) + [(0, -v.shape[-1] % 1024)]).reshape(
            *v.shape[:-1], 8, -1
        )

    def own_part(v):
        return lax.dynamic_slice_in_dim(v.reshape(block_rows, width), t * own_rows, own_rows, 0)

    def all_depths(mine):
        return lax.all_gather(mine, "ctx", axis=0, tiled=True).reshape(width, -1)

    def padded(v):
        return jnp.pad(v.astype(f32).reshape(-1), (0, 128 - v.size))

    kinds = [pre_gain, pre_bias, mlp_gain, mlp_bias, group_gain, group_bias, lengths]
    small = jnp.stack([padded(v) for v in kinds] + [jnp.zeros(128, f32)])
    weights = [query_weight, key_weight, value_weight, swish_weight]
    weights += [out_weight, gelu_weight, up_weight, down_weight]
    attn_w, rest, normed, small = start(
        tokens.reshape(block_rows, width), small, weights, 4, (4, 7), 0
    )
    small, tokens, cotangent = lax.optimization_barrier((small, tokens, cotangent))
    normed = normed.reshape(rows, width)
    out_t = all_depths(rest[..., :value_size])
    pre_gain_full, pre_bias_full, mlp_gain_full, mlp_bias_full = (
        small[:, i, :depth].reshape(width) for i in range(4)
    )
    group = small[:, 4:6, : group_gain.size].reshape(nf * nc, 2, heads_local, -1)
    group = lax.dynamic_index_in_dim(group, f, 2, False).transpose(1, 0, 2).reshape(2, value_size)
    all_lengths = small.reshape(nf, nc, 8, 128)[:, 0, 6, :seq_count].reshape(seqs)

    inputs = own_part(tokens).astype(f32)
    _, norm_in_back = jax.vjp(layer_norm, inputs, pre_gain_full, pre_bias_full)
    positions = c * span + lax.iota(jnp.int32, span)
    own_ids = t * own_rows + lax.iota(jnp.int32, own_rows)
    own_valid = (c * span + own_ids % span < lengths[own_ids // span]).astype(f32)[:, None]
    error = own_valid * own_part(cotangent).astype(f32)

    pre = product(normed, attn_w)
    valid = (positions.astype(f32)[None, :] < all_lengths[:, None]).astype(f32)[:, :, None]
    cosine, sine = turn_tables(positions, key_size // 2)
    key_scale = key_size ** (-0.5)
    query_pre = pre[:, :key_size].reshape(seqs, span, key_size)
    key_pre = pre[:, key_size : 2 * key_size].reshape(seqs, span, key_size)
    value_pre = pre[:, 2 * key_size : 2 * key_size + value_size]
    swish_pre = pre[:, 2 * key_size + value_size :]
    queries = rotate(query_pre, cosine, sine).astype(bf16)
    keys = (rotate(key_pre, cosine, sine) * key_scale * valid).astype(bf16)
    values = value_pre.astype(bf16).reshape(seqs, span, value_size)

    log_decay = jnp.log1p(-jnp.exp2(-5.0 - head.astype(f32)))
    offsets = jnp.arange(span)
    distance = (offsets[:, None] - offsets[None, :]).astype(f32)
    within_fade = jnp.where(distance >= 0, jnp.exp(jnp.maximum(distance, 0.0) * log_decay), 0.0)
    key_fade = jnp.exp((span - 1 - offsets).astype(f32) * log_decay)[:, None]
    query_fade = jnp.exp((offsets + 1).astype(f32) * log_decay)[:, None]
    block_fade = jnp.exp(span * log_decay)

    keys_faded = (keys.astype(f32) * key_fade).astype(bf16)
    queries_faded = (queries.astype(f32) * query_fade).astype(bf16)
    local_state = blocks("sjd,sje->sde", keys_faded, values)
    error_low = error.astype(bf16)
    entering, error_all = pass_and_gather(local_state, block_fade, error_low, 1, 2)
    rest, entering = lax.optimization_barrier((rest, entering))
    ff_w = all_depths(rest[..., value_size:])
    probs = (blocks("sid,sjd->sij", queries, keys) * within_fade).astype(bf16)
    mixed = blocks("sij,sje->sie", probs, values) + blocks("sid,sde->sie", queries_faded, entering)
    gated_wide, gate_back = jax.vjp(
        gate_mix, mixed.reshape(rows, value_size), swish_pre, group[0], group[1]
    )
    gated = gated_wide.astype(bf16)
    branch = scatter_product([gated], out_t, 0, 1)
    hidden = inputs + branch

    mlp_wide, norm_mid_back = jax.vjp(layer_norm, hidden, mlp_gain_full, mlp_bias_full)
    mlp_in = gather_rows(mlp_wide.astype(bf16), 4)
    inner, ff_low, ff_part = feed_forward(mlp_in, error_all, ff_w)

    def sum_depths(grads):
        grads = with_layout_constraint(grads.astype(bf16), Layout((0, 1)))
        mine = lax.psum_scatter(grads, "ctx", scatter_dimension=0, tiled=True)
        return mine.reshape(nf, depth, -1)

    ff_sum = sum_depths(ff_part)
    mlp_in_grad = scatter_product([ff_low], ff_w, 0, 6)
    hidden_norm_grad, grad_mlp_gain, grad_mlp_bias = norm_mid_back(mlp_in_grad)
    hidden_grad = error + hidden_norm_grad

    out_part, gated_grad = gather_products(hidden_grad.astype(bf16), gated, out_t, 10)
    out_sum = sum_depths(out_part)
    mixed_grad, swish_grad, grad_group_gain, grad_group_bias = gate_back(gated_grad)
    swish_low = swish_grad.astype(bf16)
    mixed_low = mixed_grad.astype(bf16).reshape(seqs, span, value_size)
    score_low = (blocks("sie,sje->sij", mixed_low, values) * within_fade).astype(bf16)
    pulled_state = blocks("sid,sie->sde", queries_faded, mixed_low)
    swish_part = product_left(normed, swish_low).astype(bf16)
    swish_part, pulled_state, ff_sum = lax.optimization_barrier(
        (swish_part, pulled_state, ff_sum)
    )
    later, mlp_out, grad_gelu, grad_up, grad_down = pass_and_scatter(
        pulled_state, block_fade, inner, ff_w, 2 * hidden_size, ff_sum, -1, 3
    )
    out_sum, swish_part, later = lax.optimization_barrier((out_sum, swish_part, later))
    swish_sum = sum_depths(swish_part)
    block_own = (hidden + mlp_out).astype(bf16)
    query_grad = blocks("sij,sjd->sid", score_low, keys) + query_fade * blocks(
        "sie,sde->sid", mixed_low, entering
    )
    key_grad = blocks("sij,sid->sjd", score_low, queries) + key_fade * blocks(
        "sje,sde->sjd", values, later
    )
    value_grad = blocks("sij,sie->sje", probs, mixed_low) + blocks(
        "sjd,sde->sje", keys_faded, later
    )
    query_low = rotate_back(query_grad, cosine, sine).astype(bf16).reshape(rows, key_size)
    key_low = rotate_back(key_grad * key_scale * valid, cosine, sine).astype(bf16)
    low = jnp.concatenate(
        [
            query_low,
            key_low.reshape(rows, key_size),
            value_grad.astype(bf16).reshape(rows, value_size),
        ],
        -1,
    )
    attn_part = product_left(normed, low).astype(bf16)
    attn_part, low = lax.optimization_barrier((attn_part, low))
    attn_sum = sum_depths(attn_part)
    normed_grad = scatter_product([low, swish_low], attn_w, 0, 7)
    swish_sum, normed_grad = lax.optimization_barrier((swish_sum, normed_grad))
    input_norm_grad, grad_pre_gain, grad_pre_bias = norm_in_back(normed_grad)
    tokens_own = (hidden_grad + input_norm_grad).astype(bf16)

    norm_parts = jnp.stack([grad_pre_gain, grad_pre_bias, grad_mlp_gain, grad_mlp_bias])
    norm_parts = norm_parts.reshape(4, nf * nc, 1, depth).transpose(1, 2, 0, 3)
    norm_parts = jnp.broadcast_to(norm_parts, (nf * nc, nt, 4, depth)).reshape(nf * nc, nt, -1)
    mine = lax.iota(jnp.int32, nt * heads_local) == head
    group_parts = jnp.stack([grad_group_gain, grad_group_bias]).reshape(1, 2, nf * nc, -1)
    group_parts = jnp.where(mine[:, None, None, None], group_parts, 0.0)
    group_parts = group_parts.reshape(nt, heads_local, 2, nf * nc, -1).transpose(3, 0, 2, 1, 4)
    parts = jnp.concatenate([norm_parts, group_parts.reshape(nf * nc, nt, -1)], -1)
    parts = parts.reshape(nf * nc * nt, -1)
    sums, grad_out, grad_swish, block_out, grad_tokens = close(
        pad_tile(parts), out_sum, swish_sum, block_own, tokens_own, 5
    )
    block_valid = (positions[None, :] < lengths[:, None]).astype(bf16)[:, :, None]
    block_out = block_out.reshape(tokens.shape) * block_valid
    grad_tokens = grad_tokens.reshape(tokens.shape) * block_valid
    grad_out, grad_swish = grad_out.astype(f32), grad_swish.astype(f32)
    sums, attn_sum, block_out, grad_tokens, grad_out, grad_swish = lax.optimization_barrier(
        (sums, attn_sum, block_out, grad_tokens, grad_out, grad_swish)
    )
    sums = sums.reshape(-1)[: parts.shape[1]]
    grad_query, grad_key, grad_value = finish(
        [attn_sum], [[key_size, key_size, value_size]], [False], 11
    )
    norm_sums = sums[: 4 * depth].reshape(4, depth)
    group_sums = sums[4 * depth :].reshape(2, heads_local, -1)

    return (
        block_out,
        grad_tokens,
        norm_sums[0],
        norm_sums[1],
        grad_query,
        grad_key,
        grad_value,
        grad_swish,
        grad_out,
        group_sums[0],
        group_sums[1],
        norm_sums[2],
        norm_sums[3],
        grad_gelu,
        grad_up,
        grad_down,
    )


def solution(mesh):
    rows = P("fsdp", "ctx", None)
    vector = P(("fsdp", "ctx"))
    tall = P(("fsdp", "ctx"), "tp")
    wide = P("tp", ("fsdp", "ctx"))
    in_specs = (rows, P("fsdp"), rows, vector, vector, tall, tall, tall, tall, wide)
    in_specs += (wide, wide, vector, vector, tall, tall, wide)
    out_specs = (rows, rows, vector, vector, tall, tall, tall, tall, wide)
    out_specs += (wide, wide, vector, vector, tall, tall, wide)
    return jax.shard_map(shards, mesh=mesh, in_specs=in_specs, out_specs=out_specs, check_vma=False)
```

```python
import functools
import math

import jax
import jax.numpy as jnp
from jax import lax
from jax.experimental import pallas as pl
from jax.experimental.layout import Layout, with_layout_constraint
from jax.experimental.pallas import tpu as pltpu
from jax.sharding import PartitionSpec as P

eps = 1e-05
SPARE = 6 << 20
group_floor = 1.0
f32 = jnp.float32
bf16 = jnp.bfloat16


def layer_norm(values, norm_gain, norm_shift):
    centred = values - jnp.mean(values, -1, keepdims=True)
    spread = jnp.mean(centred * centred, -1, keepdims=True)
    return centred * lax.rsqrt(spread + eps) * norm_gain + norm_shift


def turn_tables(positions, half_size):
    frequency = jnp.power(10000.0, -jnp.arange(half_size).astype(f32) / half_size)
    angles = positions.astype(f32)[:, None] * frequency[None, :]
    return jnp.cos(angles), jnp.sin(angles)


def rotate(values, cosine, sine):
    half_size = values.shape[-1] // 2
    first = values[..., :half_size]
    second = values[..., half_size:]
    return jnp.concatenate([first * cosine - second * sine, second * cosine + first * sine], -1)


def rotate_back(values, cosine, sine):
    return rotate(values, cosine, -sine)


def gate_mix(mixed, swish_pre, norm_gain, norm_shift):
    centred = mixed - jnp.mean(mixed, -1, keepdims=True)
    spread = jnp.mean(centred * centred, -1, keepdims=True)
    return jax.nn.silu(swish_pre) * (
        centred * lax.rsqrt(spread + group_floor) * norm_gain + norm_shift
    )


def mlp_mix(gelu_pre, up_pre):
    return jax.nn.gelu(gelu_pre) * up_pre


def product(left, right):
    return jnp.dot(left, right, preferred_element_type=f32)


def product_left(left, right):
    return lax.dot_general(left, right, (((0,), (0,)), ((), ())), preferred_element_type=f32)


def product_right(left, right):
    return lax.dot_general(left, right, (((1,), (1,)), ((), ())), preferred_element_type=f32)


def blocks(spec, left, right):
    return jnp.einsum(spec, left, right, preferred_element_type=f32)


MESH = pl.DeviceIdType.MESH


def beside(f):
    return f + 1 - 2 * (f % 2), (f + 2) % 4, 3 - f


def remote(src, dst, send, recv, device):
    return pltpu.make_async_remote_copy(
        src_ref=src, dst_ref=dst, send_sem=send, recv_sem=recv, device_id=device, device_id_type=MESH
    )


def reorder(src, dst, kind, back):
    nf, nc = lax.axis_size("fsdp"), lax.axis_size("ctx")
    depth = src.shape[-1] // (nf * nc)
    for f in range(nf):
        for c in range(nc):
            plain, mixed = (f * nc + c) * depth, (c * nf + f) * depth
            if back:
                plain, mixed = mixed, plain
            dst[:, mixed : mixed + depth] = src[:, plain : plain + depth].astype(kind)


def gather_steps(plain, out, mixed, keep, send, recv):
    own = plain if mixed is None else mixed
    f, t = lax.axis_index("fsdp"), lax.axis_index("tp")
    fx, fy, fd = beside(f)
    x, y, core = {"fsdp": fx}, {"fsdp": fy}, {"tp": 1 - t}
    half = own.shape[0] // 2

    def part(ref, h):
        return ref.at[pl.ds(h * half, half)]

    def slot(who, h):
        return part(out.at[2 * who + t], h)

    local = pltpu.make_async_copy(own, out.at[2 * f + t], keep)
    first = [
        remote(part(own, 0), slot(f, 0), send.at[0], recv.at[0], x),
        remote(part(own, 1), slot(f, 1), send.at[1], recv.at[3], y),
        remote(part(own, 1), slot(f, 1), send.at[2], recv.at[1], x),
        remote(part(own, 0), slot(f, 0), send.at[3], recv.at[2], y),
        remote(part(own, 0), slot(f, 0), send.at[4], recv.at[6], core),
        remote(part(own, 1), slot(f, 1), send.at[5], recv.at[7], core),
    ]
    sent = list(first)

    def pass_on(who, h, s, r, device):
        copy = remote(slot(who, h), slot(who, h), send.at[s], recv.at[r], device)
        copy.start()
        sent.append(copy)

    def begin():
        if mixed is not None:
            reorder(plain, mixed, mixed.dtype, False)
        local.start()
        for copy in first:
            copy.start()

    def relay():
        first[0].wait_recv()
        pass_on(fx, 0, 6, 4, y)
        pass_on(fx, 0, 7, 8, core)
        first[1].wait_recv()
        pass_on(fy, 1, 8, 5, x)
        pass_on(fy, 1, 9, 11, core)

    def rest():
        first[2].wait_recv()
        pass_on(fx, 1, 10, 9, core)
        first[3].wait_recv()
        pass_on(fy, 0, 11, 10, core)

    def diagonal():
        remote(slot(fd, 0), slot(fd, 0), send.at[12], recv.at[4], y).wait_recv()
        pass_on(fd, 0, 12, 12, core)
        remote(slot(fd, 1), slot(fd, 1), send.at[13], recv.at[5], x).wait_recv()
        pass_on(fd, 1, 13, 13, core)

    def end(crossed=False):
        if not crossed:
            for r in range(6, 14):
                remote(slot(f, 0), slot(f, 0), send.at[0], recv.at[r], core).wait_recv()
            local.wait()
        for copy in sent:
            copy.wait_send()

    return begin, relay, rest, diagonal, end


def in_kernel(width):
    return width // (lax.axis_size("fsdp") * lax.axis_size("ctx")) % 128 == 0


def gather_scratch(own):
    return [
        pltpu.VMEM(own.shape if in_kernel(own.shape[1]) else (16, 128), own.dtype),
        pltpu.SemaphoreType.DMA,
        pltpu.SemaphoreType.DMA((14,)),
        pltpu.SemaphoreType.DMA((14,)),
    ]


def scatter_steps(start, lefts, right, out, mine, sent, theirs, total, diag, last, send, recv):
    f, t = lax.axis_index("fsdp"), lax.axis_index("tp")
    fx, fy, fd = beside(f)
    x, y, core = {"fsdp": fx}, {"fsdp": fy}, {"tp": 1 - t}
    half = out.shape[0] // 2
    order = [fd, fy, fx, f]
    tile = 512

    def part(ref, h):
        return ref.at[pl.ds(h * half, half)]

    crossing = [
        remote(sent.at[i], theirs.at[i], send.at[i], recv.at[i], core) for i in range(4)
    ]
    d0 = remote(part(total.at[0], 0), diag.at[0], send.at[4], recv.at[4], x)
    d1 = remote(part(total.at[0], 1), diag.at[1], send.at[5], recv.at[5], y)
    y1 = remote(part(total.at[1], 1), part(last.at[1], 1), send.at[6], recv.at[6], y)
    x0 = remote(part(total.at[2], 0), part(last.at[0], 0), send.at[7], recv.at[7], x)
    y0 = remote(part(total.at[1], 0), part(last.at[1], 0), send.at[8], recv.at[8], y)
    x1 = remote(part(total.at[2], 1), part(last.at[0], 1), send.at[9], recv.at[9], x)

    def make(block, put):
        def piece(j, carry):
            columns = pl.ds(pl.multiple_of(j * tile, tile), tile)
            at, value = start, 0.0
            for left in lefts:
                size = left.shape[2]
                value += product_right(left[block], right[columns, at : at + size])
                at += size
            put(columns, value)
            return carry

        lax.fori_loop(0, out.shape[1] // tile, piece, 0)

    def cross(i):
        def put(columns, value):
            sent[i, :, columns] = value.astype(sent.dtype)

        make(2 * order[i] + 1 - t, put)
        crossing[i].start()

    def keep(i):
        def put(columns, value):
            mine[:, columns] = value

        make(2 * order[i] + t, put)

    def add(i):
        keep(i)
        crossing[i].wait_recv()
        total[i] = (mine[...] + theirs[i].astype(f32)).astype(total.dtype)

    def diagonal():
        cross(0)
        cross(1)
        add(0)
        d0.start()
        d1.start()

    def straight():
        cross(2)
        add(1)
        y1.start()
        add(2)
        x0.start()
        cross(3)

    def relay():
        d0.wait_recv()
        total[1, :half] = (total[1, :half].astype(f32) + diag[0].astype(f32)).astype(total.dtype)
        y0.start()
        d1.wait_recv()
        total[2, half:] = (total[2, half:].astype(f32) + diag[1].astype(f32)).astype(total.dtype)
        x1.start()
        keep(3)
        crossing[3].wait_recv()
        mine[...] += theirs[3].astype(f32)

    def end():
        for copy in (y1, x0, y0, x1):
            copy.wait_recv()
        mine[...] += last[0].astype(f32) + last[1].astype(f32)
        if in_kernel(out.shape[1]):
            reorder(mine, out, out.dtype, True)
        else:
            out[...] = mine[...]
        for copy in (*crossing, d0, d1, y1, x0, y0, x1):
            copy.wait_send()

    return diagonal, straight, relay, end


def scatter_scratch(rows, width):
    return [
        pltpu.VMEM((rows, width), f32),
        pltpu.VMEM((4, rows, width), bf16),
        pltpu.VMEM((4, rows, width), bf16),
        pltpu.VMEM((3, rows, width), bf16),
        pltpu.VMEM((2, rows // 2, width), bf16),
        pltpu.VMEM((2, rows, width), bf16),
        pltpu.SemaphoreType.DMA((10,)),
        pltpu.SemaphoreType.DMA((10,)),
    ]


def pass_steps(by, local, fade, out, held, send, recv):
    length = lax.axis_size("ctx")
    c = lax.axis_index("ctx")
    first = c == (0 if by > 0 else length - 1)
    last = c == (length - 1 if by > 0 else 0)
    target = lax.rem(c + by + length, length)

    def copy(p):
        return remote(held.at[p], out.at[p], send.at[p], recv.at[p], {"ctx": target})

    def step(p, carry):
        @pl.when(first)
        def _():
            out[p] = jnp.zeros(out.shape[1:], out.dtype)

        @pl.when(jnp.logical_not(first))
        def _():
            copy(p).wait_recv()

        @pl.when(jnp.logical_not(last))
        def _():
            held[p] = (fade[...] * out[p].astype(f32) + local[p]).astype(held.dtype)
            copy(p).start()

        return carry

    def run(quarter):
        count = local.shape[0]
        if quarter < 0:
            lax.fori_loop(0, jnp.where(first, count, 0), step, 0)
        else:
            low, high = quarter * count // 4, (quarter + 1) * count // 4
            lax.fori_loop(jnp.where(first, count, low), jnp.where(first, count, high), step, 0)

    def end():
        @pl.when(jnp.logical_not(last))
        def _():
            def done(p, carry):
                copy(p).wait_send()
                return carry

            lax.fori_loop(0, local.shape[0], done, 0)

    return run, end


def greet_plane(by=0, diagonal=False):
    f, c, t = lax.axis_index("fsdp"), lax.axis_index("ctx"), lax.axis_index("tp")
    length = lax.axis_size("ctx")
    fx, fy, fd = beside(f)
    barrier = pltpu.get_barrier_semaphore()
    peers = [{"fsdp": fx}, {"fsdp": fy}, {"tp": 1 - t}] + [{"fsdp": fd}] * diagonal
    for device in peers:
        pl.semaphore_signal(barrier, inc=1, device_id=device, device_id_type=MESH)
    if by != 0:
        first = c == (0 if by > 0 else length - 1)
        last = c == (length - 1 if by > 0 else 0)
        source = {"ctx": lax.rem(c - by + length, length)}

        @pl.when(jnp.logical_not(first))
        def _():
            pl.semaphore_signal(barrier, inc=1, device_id=source, device_id_type=MESH)

        @pl.when(jnp.logical_not(last))
        def _():
            pl.semaphore_wait(barrier, len(peers) + 1)

        @pl.when(last)
        def _():
            pl.semaphore_wait(barrier, len(peers))
    else:
        pl.semaphore_wait(barrier, len(peers))


def gather_with(own, full, mixed, *scratch):
    return gather_steps(own, full, mixed if in_kernel(own.shape[1]) else None, *scratch)


def gather_kernel(*refs):
    steps = gather_with(*refs)
    greet_plane()
    for step in steps:
        step()


def scatter_kernel(count, start, *refs):
    steps = scatter_steps(start, refs[:count], *refs[count:])
    greet_plane()
    for step in steps:
        step()


def gather_products_kernel(own, left, right, grad, back, full, total, mixed, *scratch):
    f, t = lax.axis_index("fsdp"), lax.axis_index("tp")
    fx, fy, fd = beside(f)
    recv = scratch[2]
    begin, relay, rest, diagonal, end = gather_with(own, full, mixed, *scratch)
    tile = 512

    def use(block, fresh=False):
        back[block] = product(full[block], right[...])

        def piece(j, carry):
            columns = pl.ds(pl.multiple_of(j * tile, tile), tile)
            value = product_left(full[block, :, columns], left[block])
            total[columns, :] = value if fresh else total[columns, :] + value
            return carry

        lax.fori_loop(0, total.shape[0] // tile, piece, 0)

    def crossed(who, r):
        block = full.at[2 * who + 1 - t]
        half = block.shape[0] // 2
        for h in range(2):
            where = block.at[pl.ds(h * half, half)]
            remote(where, where, scratch[1].at[0], recv.at[r + h], {"tp": 1 - t}).wait_recv()

    greet_plane()
    begin()
    pltpu.make_async_copy(full.at[2 * f + t], full.at[2 * f + t], scratch[0]).wait()
    use(2 * f + t, True)
    relay()
    crossed(f, 6)
    use(2 * f + 1 - t)
    rest()
    use(2 * fx + t)
    use(2 * fy + t)
    crossed(fx, 8)
    use(2 * fx + 1 - t)
    crossed(fy, 10)
    use(2 * fy + 1 - t)
    diagonal()
    use(2 * fd + t)
    crossed(fd, 12)
    use(2 * fd + 1 - t)
    end(True)
    grad[...] = total[...].astype(grad.dtype)


def gather_products(own, left, right, collective_id):
    own = ready(own)
    rows, width = own.shape
    size = left.shape[1]
    grad, back = call(
        gather_products_kernel,
        collective_id,
        [
            (jax.ShapeDtypeStruct((width, size), bf16), pltpu.VMEM),
            (jax.ShapeDtypeStruct((8, rows, size), f32), pltpu.VMEM),
        ],
        [vmem()] * 3,
        [
            pltpu.VMEM((8, rows, width), bf16),
            pltpu.VMEM((width, size), f32),
            *gather_scratch(own),
        ],
        own,
        in_eights(left),
        right,
        tight=True,
    )
    return grad, back.reshape(8 * rows, size)


def pass_gather_kernel(by, local, fade, own, out, full, held, send, recv, *scratch):
    begin, relay, rest, diagonal, end = gather_with(own, full, *scratch)
    run, done = pass_steps(by, local, fade, out, held, send, recv)
    greet_plane(by)
    run(-1)
    begin()
    run(0)
    relay()
    run(1)
    rest()
    run(2)
    run(3)
    diagonal()
    end()
    done()


def pass_scatter_kernel(by, start, local, fade, left, right, ff, out, own, *refs):
    gelu_grad, up_grad, down_grad, held, send, recv = refs[:6]
    scratch, hand = refs[6:-3], refs[-3:]
    targets = [[(gelu_grad, False), (up_grad, False), (down_grad, True)]]
    hand_over, take = hand_steps([ff], targets, *hand)
    diagonal, straight, relay, end = scatter_steps(start, [left], right, own, *scratch)
    run, done = pass_steps(by, local, fade, out, held, send, recv)
    greet_plane(by, True)
    run(-1)
    diagonal()
    straight()
    hand_over()
    run(0)
    relay()
    run(1)
    run(2)
    run(3)
    end()
    take()
    done()


def held_bytes(array):
    last = -(-array.shape[-1] // 128) * 128
    return math.prod(array.shape[:-1]) * last * jnp.dtype(array.dtype).itemsize


def call(kernel, collective_id, outs, ins, scratch, *args, tight=False):
    shapes, spaces = zip(*outs)
    limit = 52 << 20
    held = [shape for shape, space in outs if space == pltpu.VMEM]
    held += [arg for arg, spec in zip(args, ins) if spec.memory_space == pltpu.VMEM]
    held += [one for one in scratch if getattr(one, "memory_space", None) == pltpu.VMEM]
    if tight:
        limit = sum(held_bytes(one) for one in held) + SPARE
    return pl.pallas_call(
        kernel,
        out_shape=shapes,
        in_specs=ins,
        out_specs=tuple(pl.BlockSpec(memory_space=space) for space in spaces),
        scratch_shapes=scratch,
        compiler_params=pltpu.CompilerParams(
            collective_id=collective_id, has_side_effects=True, vmem_limit_bytes=limit
        ),
        cost_estimate=pl.CostEstimate(flops=0, bytes_accessed=2_000_000, transcendentals=0),
    )(*args)


def vmem():
    return pl.BlockSpec(memory_space=pltpu.VMEM)


def perm(v):
    nf, nc = lax.axis_size("fsdp"), lax.axis_size("ctx")
    return v.reshape(len(v), nf, nc, -1).transpose(0, 2, 1, 3).reshape(v.shape)


def unperm(v):
    nf, nc = lax.axis_size("fsdp"), lax.axis_size("ctx")
    return v.reshape(len(v), nc, nf, -1).transpose(0, 2, 1, 3).reshape(v.shape)


def gathered(own):
    rows, width = own.shape
    return jax.ShapeDtypeStruct((8, rows, width), own.dtype), pl.ANY


def scattered(left, right):
    return jax.ShapeDtypeStruct((left.shape[0] // 8, right.shape[0]), f32), pltpu.VMEM


def passed(local):
    return jax.ShapeDtypeStruct(local.shape, bf16), pltpu.VMEM


def pass_scratch(local):
    pieces = local.shape[0]
    return [
        pltpu.VMEM(local.shape, bf16),
        pltpu.SemaphoreType.DMA((pieces,)),
        pltpu.SemaphoreType.DMA((pieces,)),
    ]


def in_eights(left):
    return left.reshape(8, -1, left.shape[1])


def ready(own):
    return own if in_kernel(own.shape[1]) else perm(own)


def plain(own):
    return own if in_kernel(own.shape[1]) else unperm(own)


def gather_rows(own, collective_id):
    own = ready(own)
    (out,) = call(gather_kernel, collective_id, [gathered(own)], [vmem()], gather_scratch(own), own)
    return out.reshape(-1, own.shape[1])


def scatter_product(lefts, right, start, collective_id):
    rows, width = lefts[0].shape[0] // 8, right.shape[0]
    (out,) = call(
        functools.partial(scatter_kernel, len(lefts), start),
        collective_id,
        [(jax.ShapeDtypeStruct((rows, width), f32), pltpu.VMEM)],
        [vmem()] * (len(lefts) + 1),
        scatter_scratch(rows, width),
        *(in_eights(left) for left in lefts),
        right,
    )
    return plain(out)


def pass_and_gather(local, fade, own, by, collective_id):
    shape = local.shape
    local = local.reshape(4 * shape[0], -1, shape[2])
    own = ready(own)
    out, full = call(
        functools.partial(pass_gather_kernel, by),
        collective_id,
        [passed(local), gathered(own)],
        [vmem(), vmem(), vmem()],
        pass_scratch(local) + gather_scratch(own),
        local,
        jnp.full((1, local.shape[2]), fade, f32),
        own,
    )
    return out.reshape(shape), full.reshape(-1, own.shape[1])


def feed_forward_kernel(rows, error, weight, inner, low, grads, total):
    step = pl.program_id(0)
    size, tile, deep = inner.shape[1], 512, 1024
    root = (2.0 / jnp.pi) ** 0.5

    def units(j, carry):
        at = pl.multiple_of(j * tile, tile)
        gelu_pre = product(rows[...], weight[:, pl.ds(at, tile)])
        up_pre = product(rows[...], weight[:, pl.ds(at + size, tile)])
        square = gelu_pre * gelu_pre
        bend = jnp.tanh(root * gelu_pre * (1.0 + 0.044715 * square))
        half = 0.5 * (1.0 + bend)
        gelu = gelu_pre * half
        slope = half + 0.5 * gelu_pre * (1.0 - bend * bend) * root * (1.0 + 0.134145 * square)
        inner[:, pl.ds(at, tile)] = (gelu * up_pre).astype(bf16)
        inner_grad = product(error[...], weight[:, pl.ds(at + 2 * size, tile)])
        low[:, pl.ds(at, tile)] = (inner_grad * up_pre * slope).astype(bf16)
        low[:, pl.ds(at + size, tile)] = (inner_grad * gelu).astype(bf16)
        return carry

    lax.fori_loop(0, size // tile, units, 0)

    def depths(first, last):
        def piece(j, carry):
            at = pl.ds(pl.multiple_of(j * deep, deep), deep)
            into = grads if last else total
            for left, right, columns in (
                (rows, low, slice(0, 2 * size)),
                (error, inner, slice(2 * size, 3 * size)),
            ):
                value = product_left(left[:, at], right[...])
                if not first:
                    value += total[at, columns]
                into[at, columns] = value.astype(into.dtype)
            return carry

        lax.fori_loop(0, total.shape[0] // deep, piece, 0)

    steps = pl.num_programs(0)
    pl.when(step == 0)(lambda: depths(True, False))
    pl.when((step > 0) & (step < steps - 1))(lambda: depths(False, False))
    pl.when(step == steps - 1)(lambda: depths(False, True))


def feed_forward(rows, error, weight):
    count, width = rows.shape
    size, block = weight.shape[1] // 3, 512
    whole = pl.BlockSpec(weight.shape, lambda i: (0, 0))

    def some(columns):
        return pl.BlockSpec((block, columns), lambda i: (i, 0))

    return pl.pallas_call(
        feed_forward_kernel,
        grid=(count // block,),
        out_shape=(
            jax.ShapeDtypeStruct((count, size), bf16),
            jax.ShapeDtypeStruct((count, 2 * size), bf16),
            jax.ShapeDtypeStruct(weight.shape, bf16),
        ),
        in_specs=[some(width), some(width), whole],
        out_specs=(some(size), some(2 * size), whole),
        scratch_shapes=[pltpu.VMEM(weight.shape, f32)],
        compiler_params=pltpu.CompilerParams(vmem_limit_bytes=56 << 20),
        cost_estimate=pl.CostEstimate(
            flops=14 * count * width * size, bytes_accessed=40_000_000, transcendentals=count * size
        ),
    )(rows, error, weight)


def pass_and_scatter(local, fade, left, right, start, ff, by, collective_id):
    shape = local.shape
    local = local.reshape(4 * shape[0], -1, shape[2])
    out, own, *grads = call(
        functools.partial(pass_scatter_kernel, by, start),
        collective_id,
        [
            passed(local),
            scattered(left, right),
            *handed(ff, [left.shape[1]] * 2),
            *handed(ff, [left.shape[1]], True),
        ],
        [vmem()] * 5,
        pass_scratch(local)
        + scatter_scratch(left.shape[0] // 8, right.shape[0])
        + hand_scratch([ff]),
        local,
        jnp.full((1, local.shape[2]), fade, f32),
        in_eights(left),
        right,
        ff,
    )
    return out.reshape(shape), plain(own), *(grad.astype(f32) for grad in grads)


def peer_of(place, nc, nt):
    return {"fsdp": place // (nc * nt), "ctx": place // nt % nc, "tp": place % nt}


def line_steps(home, place, arrived, send, recv):
    nf, nc = lax.axis_size("fsdp"), lax.axis_size("ctx")
    f, c = lax.axis_index("fsdp"), lax.axis_index("ctx")
    order = [f, *beside(f)]
    above, below = c < nc - 1, c > 0

    def copy(src, place_of, who, up):
        chunk = place_of * nf + who
        return remote(
            src,
            place(place_of, who),
            send.at[chunk if up else nc * nf + chunk],
            recv.at[chunk],
            {"ctx": lax.rem(c + 1, nc) if up else lax.rem(c + nc - 1, nc)},
        )

    def first(i):
        who = order[i]
        arrived(i)

        @pl.when(above)
        def _():
            copy(home(who), c, who, True).start()

        @pl.when(below)
        def _():
            copy(home(who), c, who, False).start()

    def step(k, carry):
        for who in order:

            @pl.when(c - k >= 0)
            def _():
                copy(place(c - k, who), c - k, who, True).wait_recv()

                @pl.when(above)
                def _():
                    copy(place(c - k, who), c - k, who, True).start()

            @pl.when(c + k < nc)
            def _():
                copy(place(c + k, who), c + k, who, False).wait_recv()

                @pl.when(below)
                def _():
                    copy(place(c + k, who), c + k, who, False).start()

        return carry

    def end():
        def one(other, carry):
            for who in order:

                @pl.when(above & (other <= c))
                def _():
                    copy(place(other, who), other, who, True).wait_send()

                @pl.when(below & (other >= c))
                def _():
                    copy(place(other, who), other, who, False).wait_send()

            return carry

        lax.fori_loop(0, nc, one, 0)

    return first, step, end


def line_scratch():
    count = lax.axis_size("fsdp") * lax.axis_size("ctx")
    return [pltpu.SemaphoreType.DMA((2 * count,)), pltpu.SemaphoreType.DMA((count,))]


def start_kernel(sizes, split, turned, own, small, *refs):
    count = len(sizes)
    weights = list(refs[:count])
    attn, rest, full, everyone = refs[count : count + 4]
    (
        brought,
        untouched,
        fetch,
        turns,
        gains,
        normed,
        mixed,
        gather_keep,
        gather_send,
        gather_recv,
        line_send,
        line_recv,
        keep,
        send,
        recv,
        small_send,
        small_recv,
    ) = refs[count + 4 :]
    nf, nc = lax.axis_size("fsdp"), lax.axis_size("ctx")
    f, c, t = lax.axis_index("fsdp"), lax.axis_index("ctx"), lax.axis_index("tp")
    here, places = f * nc + c, nf * nc
    depth = weights[0].shape[0]
    across = [weights[i] for i in turned]
    for n, i in enumerate(turned):
        weights[i] = turns.at[n]
    rows = normed.shape[0]
    fetched = [
        pltpu.make_async_copy(
            own.at[pl.ds(pl.multiple_of(t * rows, rows), rows)], brought, fetch.at[0]
        )
    ]
    fetched += [
        pltpu.make_async_copy(matrix, untouched.at[n], fetch.at[n + 1])
        for n, matrix in enumerate(across)
    ]
    for copy in fetched:
        copy.start()
    near = beside(f)
    starts = [sum(sizes[:i]) if i < split else sum(sizes[split:i]) for i in range(count)]

    def peer(i):
        other = lax.rem(here + i, places)
        return {"fsdp": other // nc, "ctx": other % nc}

    barrier = pltpu.get_barrier_semaphore()
    pl.semaphore_signal(barrier, inc=1, device_id={"tp": 1 - t}, device_id_type=MESH)

    def hello(i, carry):
        pl.semaphore_signal(barrier, inc=1, device_id=peer(i), device_id_type=MESH)
        return carry

    lax.fori_loop(1, places, hello, 0)
    pl.semaphore_wait(barrier, places)

    def chunk(place_of, who):
        rows = pl.multiple_of((place_of * nf + who) * depth, depth)
        return attn.at[pl.ds(rows, depth)]

    def columns(i, who):
        return weights[i].at[:, pl.ds(pl.multiple_of(who * sizes[i], sizes[i]), sizes[i])]

    def target(i):
        where = chunk(c, f) if i < split else rest.at[f]
        return where.at[:, pl.ds(starts[i], sizes[i])]

    def hand_out(i, n):
        return remote(
            columns(i, near[n]),
            target(i),
            send.at[3 * i + n],
            recv.at[n if i < split else 3 + n],
            {"fsdp": near[n]},
        )

    def hold(i):
        return pltpu.make_async_copy(columns(i, f), target(i), keep.at[0 if i < split else 1])

    for i in range(split):
        hold(i).start()
    for n in range(3):
        for i in range(split):
            hand_out(i, n).start()

    def arrived(i):
        if i == 0:
            pltpu.make_async_copy(chunk(c, f), chunk(c, f), keep.at[0]).wait()
        else:
            who = near[i - 1]
            remote(
                chunk(c, who), chunk(c, who), send.at[0], recv.at[i - 1], {"fsdp": who}
            ).wait_recv()

    first, step, end = line_steps(lambda who: chunk(c, who), chunk, arrived, line_send, line_recv)
    first(0)

    def tell(i):
        return remote(small, everyone.at[here], small_send.at[i], small_recv.at[i], peer(i))

    def go(i, carry):
        tell(i).start()
        return carry

    def told(i, carry):
        tell(i).wait()
        return carry

    lax.fori_loop(1, places, go, 0)
    everyone[here] = small[...]
    first(1)
    lax.fori_loop(1, places, told, 0)
    for i in range(places):
        for j in range(2):
            gains[j : j + 1, i * depth : (i + 1) * depth] = everyone[i, j : j + 1, :depth]
    fetched[0].wait()
    normed[...] = layer_norm(brought[...].astype(f32), gains[0:1, :], gains[1:2, :]).astype(bf16)
    begin, relay, others, diagonal, finish = gather_steps(
        normed, full, mixed, gather_keep, gather_send, gather_recv
    )
    begin()
    first(2)
    first(3)
    step(1, 0)
    relay()
    for n in range(len(turned)):
        fetched[n + 1].wait()
        turns[n] = untouched[n].T
    for i in range(split, count):
        hold(i).start()
        for n in range(3):
            hand_out(i, n).start()
    lax.fori_loop(2, 3, step, 0)
    others()
    diagonal()
    lax.fori_loop(3, nc, step, 0)
    finish()
    pltpu.make_async_copy(rest.at[f], rest.at[f], keep.at[1]).wait()
    for n in range(3):
        where = rest.at[near[n]]
        remote(where, where, send.at[0], recv.at[3 + n], {"fsdp": near[n]}).wait_recv()
    for i in range(count):
        for n in range(3):
            hand_out(i, n).wait_send()
    end()


def start(tokens, small, weights, split, turned, collective_id):
    nf, nc = lax.axis_size("fsdp"), lax.axis_size("ctx")
    rows, width = tokens.shape
    rows //= lax.axis_size("tp")
    depth = weights[0].shape[0]
    sizes = [w.size // depth // nf for w in weights]
    anywhere = pl.BlockSpec(memory_space=pl.ANY)
    count = nf * nc
    return call(
        functools.partial(start_kernel, sizes, split, turned),
        collective_id,
        [
            (jax.ShapeDtypeStruct((width, sum(sizes[:split])), bf16), pl.ANY),
            (jax.ShapeDtypeStruct((nf, depth, sum(sizes[split:])), bf16), pl.ANY),
            (jax.ShapeDtypeStruct((8, rows, width), bf16), pl.ANY),
            (jax.ShapeDtypeStruct((count, *small.shape), f32), pltpu.VMEM),
        ],
        [anywhere, vmem()] + [anywhere] * len(weights),
        [
            pltpu.VMEM((rows, width), bf16),
            pltpu.VMEM((len(turned), *weights[turned[0]].shape), bf16),
            pltpu.SemaphoreType.DMA((len(turned) + 1,)),
            pltpu.VMEM((len(turned), depth, sizes[turned[0]] * nf), bf16),
            pltpu.VMEM((8, width), f32),
            pltpu.VMEM((rows, width), bf16),
            pltpu.VMEM((rows, width), bf16),
            *gather_scratch(tokens)[1:],
            *line_scratch(),
            pltpu.SemaphoreType.DMA((2,)),
            pltpu.SemaphoreType.DMA((3 * len(weights),)),
            pltpu.SemaphoreType.DMA((6,)),
            pltpu.SemaphoreType.DMA((count,)),
            pltpu.SemaphoreType.DMA((count,)),
        ],
        tokens,
        small,
        *weights,
    )


def hand_steps(parts, outs, slots, send, recv):
    f = lax.axis_index("fsdp")
    near = beside(f)
    starts = [sum(part.shape[2] for part in parts[:i]) for i in range(len(parts))]

    def copies(n):
        return [
            remote(
                part.at[near[n]],
                slots.at[n, :, pl.ds(at, part.shape[2])],
                send.at[len(parts) * n + i],
                recv.at[len(parts) * n + i],
                {"fsdp": near[n]},
            )
            for i, (part, at) in enumerate(zip(parts, starts))
        ]

    def begin():
        for n in range(3):
            for copy in copies(n):
                copy.start()

    def put(who, blocks):
        for block, targets in zip(blocks, outs):
            at = 0
            for out, turned in targets:
                size = out.shape[0 if turned else 1] // lax.axis_size("fsdp")
                where = pl.ds(pl.multiple_of(who * size, size), size)
                if turned:
                    out[where, :] = block[:, at : at + size].T
                else:
                    out[:, where] = block[:, at : at + size]
                at += size

    def end():
        put(f, [part[f] for part in parts])
        for n in range(3):
            for copy in copies(n):
                copy.wait()
            put(
                near[n],
                [slots[n, :, at : at + part.shape[2]] for part, at in zip(parts, starts)],
            )

    return begin, end


def hand_scratch(parts):
    size = sum(part.shape[2] for part in parts)
    return [
        pltpu.VMEM((3, parts[0].shape[1], size), bf16),
        pltpu.SemaphoreType.DMA((3 * len(parts),)),
        pltpu.SemaphoreType.DMA((3 * len(parts),)),
    ]


def handed(part, sizes, turned=False):
    nf, depth = part.shape[:2]
    shapes = [(nf * n, depth) if turned else (depth, nf * n) for n in sizes]
    return [(jax.ShapeDtypeStruct(shape, bf16), pltpu.VMEM) for shape in shapes]


def finish_kernel(turned, counts, *refs):
    parts, outs, scratch = refs[: len(turned)], list(refs[len(turned) : -3]), refs[-3:]
    targets = [[(outs.pop(0), turn) for _ in range(n)] for turn, n in zip(turned, counts)]
    begin, end = hand_steps(parts, targets, *scratch)
    greet_fsdp()
    begin()
    end()


def greet_fsdp():
    near = beside(lax.axis_index("fsdp"))
    barrier = pltpu.get_barrier_semaphore()
    for who in near:
        pl.semaphore_signal(barrier, inc=1, device_id={"fsdp": who}, device_id_type=MESH)
    pl.semaphore_wait(barrier, 3)


def finish(parts, sizes, turned, collective_id):
    outs = [one for n in zip(parts, sizes, turned) for one in handed(*n)]
    outs = call(
        functools.partial(finish_kernel, turned, [len(size) for size in sizes]),
        collective_id,
        outs,
        [vmem()] * len(parts),
        hand_scratch(parts),
        *parts,
        tight=True,
    )
    return [out.astype(f32) for out in outs]


def total_steps(parts, out, slots, send, recv):
    nc, nt = lax.axis_size("ctx"), lax.axis_size("tp")
    count = parts.shape[0]
    place = (lax.axis_index("fsdp") * nc + lax.axis_index("ctx")) * nt + lax.axis_index("tp")

    def hello():
        barrier = pltpu.get_barrier_semaphore()

        def one(i, carry):
            other = peer_of(lax.rem(place + i, count), nc, nt)
            pl.semaphore_signal(barrier, inc=1, device_id=other, device_id_type=MESH)
            return carry

        lax.fori_loop(1, count, one, 0)
        pl.semaphore_wait(barrier, count - 1)

    def copy(i):
        other = lax.rem(place + i, count)
        return remote(
            parts.at[other], slots.at[i], send.at[i], recv.at[i], peer_of(other, nc, nt)
        )

    def begin():
        def go(i, carry):
            copy(i).start()
            return carry

        lax.fori_loop(1, count, go, 0)

    def end():
        def add(i, carry):
            copy(i).wait()
            return carry + slots[i]

        out[...] = lax.fori_loop(1, count, add, parts[place])

    return hello, begin, end


def close_kernel(
    parts, first, second, one, two, out, wide, tall, one_both, two_both, slots, send, recv, *scratch
):
    hand, keep, core_send, core_recv = scratch[:3], *scratch[3:]
    t = lax.axis_index("tp")
    hello, begin, end = total_steps(parts, out, slots, send, recv)
    hand_over, take = hand_steps([first, second], [[(wide, True)], [(tall, False)]], *hand)
    hello()
    begin()
    copies = []
    for i, (own, both) in enumerate(((one, one_both), (two, two_both))):
        copies.append(pltpu.make_async_copy(own, both.at[t], keep.at[i]))
        copies.append(
            remote(own, both.at[t], core_send.at[i], core_recv.at[i], {"tp": 1 - t})
        )
    for copy in copies:
        copy.start()
    end()
    for copy in copies:
        copy.wait()
    hand_over()
    take()


def close(parts, first, second, one, two, collective_id):
    count = parts.shape[0]
    both = (jax.ShapeDtypeStruct((2, *one.shape), one.dtype), pltpu.VMEM)
    return call(
        close_kernel,
        collective_id,
        [
            (jax.ShapeDtypeStruct(parts.shape[1:], f32), pltpu.VMEM),
            *handed(first, [first.shape[2]], True),
            *handed(second, [second.shape[2]]),
            both,
            both,
        ],
        [vmem()] * 5,
        [
            pltpu.VMEM(parts.shape, f32),
            pltpu.SemaphoreType.DMA((count,)),
            pltpu.SemaphoreType.DMA((count,)),
            *hand_scratch([first, second]),
            pltpu.SemaphoreType.DMA((2,)),
            pltpu.SemaphoreType.DMA((2,)),
            pltpu.SemaphoreType.DMA((2,)),
        ],
        parts,
        first,
        second,
        one,
        two,
        tight=True,
    )


def shards(
    tokens,
    lengths,
    cotangent,
    pre_gain,
    pre_bias,
    query_weight,
    key_weight,
    value_weight,
    swish_weight,
    out_weight,
    group_gain,
    group_bias,
    mlp_gain,
    mlp_bias,
    gelu_weight,
    up_weight,
    down_weight,
):
    seq_count, span, width = tokens.shape
    nf, nc, nt = lax.axis_size("fsdp"), lax.axis_size("ctx"), lax.axis_size("tp")
    f, c, t = lax.axis_index("fsdp"), lax.axis_index("ctx"), lax.axis_index("tp")
    block_rows = seq_count * span
    own_rows = block_rows // nt
    depth = query_weight.shape[0]
    heads_local = group_gain.shape[0]
    assert heads_local == nf
    key_size = query_weight.shape[1] // heads_local
    value_size = value_weight.shape[1] // heads_local
    hidden_size = gelu_weight.shape[1] // nf
    seqs = nf * seq_count
    rows = seqs * span
    head = t * heads_local + f

    def pad_tile(v):
        return jnp.pad(v, [(0, 0)] * (v.ndim - 1) + [(0, -v.shape[-1] % 1024)]).reshape(
            *v.shape[:-1], 8, -1
        )

    def own_part(v):
        return lax.dynamic_slice_in_dim(v.reshape(block_rows, width), t * own_rows, own_rows, 0)

    def all_depths(mine):
        return lax.all_gather(mine, "ctx", axis=0, tiled=True).reshape(width, -1)

    def padded(v):
        return jnp.pad(v.astype(f32).reshape(-1), (0, 128 - v.size))

    kinds = [pre_gain, pre_bias, mlp_gain, mlp_bias, group_gain, group_bias, lengths]
    small = jnp.stack([padded(v) for v in kinds] + [jnp.zeros(128, f32)])
    weights = [query_weight, key_weight, value_weight, swish_weight]
    weights += [out_weight, gelu_weight, up_weight, down_weight]
    attn_w, rest, normed, small = start(
        tokens.reshape(block_rows, width), small, weights, 4, (4, 7), 0
    )
    small, tokens, cotangent = lax.optimization_barrier((small, tokens, cotangent))
    normed = normed.reshape(rows, width)
    out_t = all_depths(rest[..., :value_size])
    pre_gain_full, pre_bias_full, mlp_gain_full, mlp_bias_full = (
        small[:, i, :depth].reshape(width) for i in range(4)
    )
    group = small[:, 4:6, : group_gain.size].reshape(nf * nc, 2, heads_local, -1)
    group = lax.dynamic_index_in_dim(group, f, 2, False).transpose(1, 0, 2).reshape(2, value_size)
    all_lengths = small.reshape(nf, nc, 8, 128)[:, 0, 6, :seq_count].reshape(seqs)

    inputs = own_part(tokens).astype(f32)
    _, norm_in_back = jax.vjp(layer_norm, inputs, pre_gain_full, pre_bias_full)
    positions = c * span + lax.iota(jnp.int32, span)
    own_ids = t * own_rows + lax.iota(jnp.int32, own_rows)
    own_valid = (c * span + own_ids % span < lengths[own_ids // span]).astype(f32)[:, None]
    error = own_valid * own_part(cotangent).astype(f32)

    pre = product(normed, attn_w)
    valid = (positions.astype(f32)[None, :] < all_lengths[:, None]).astype(f32)[:, :, None]
    cosine, sine = turn_tables(positions, key_size // 2)
    key_scale = key_size ** (-0.5)
    query_pre = pre[:, :key_size].reshape(seqs, span, key_size)
    key_pre = pre[:, key_size : 2 * key_size].reshape(seqs, span, key_size)
    value_pre = pre[:, 2 * key_size : 2 * key_size + value_size]
    swish_pre = pre[:, 2 * key_size + value_size :]
    queries = rotate(query_pre, cosine, sine).astype(bf16)
    keys = (rotate(key_pre, cosine, sine) * key_scale * valid).astype(bf16)
    values = value_pre.astype(bf16).reshape(seqs, span, value_size)

    log_decay = jnp.log1p(-jnp.exp2(-5.0 - head.astype(f32)))
    offsets = jnp.arange(span)
    distance = (offsets[:, None] - offsets[None, :]).astype(f32)
    within_fade = jnp.where(distance >= 0, jnp.exp(jnp.maximum(distance, 0.0) * log_decay), 0.0)
    key_fade = jnp.exp((span - 1 - offsets).astype(f32) * log_decay)[:, None]
    query_fade = jnp.exp((offsets + 1).astype(f32) * log_decay)[:, None]
    block_fade = jnp.exp(span * log_decay)

    keys_faded = (keys.astype(f32) * key_fade).astype(bf16)
    queries_faded = (queries.astype(f32) * query_fade).astype(bf16)
    local_state = blocks("sjd,sje->sde", keys_faded, values)
    error_low = error.astype(bf16)
    entering, error_all = pass_and_gather(local_state, block_fade, error_low, 1, 2)
    rest, entering = lax.optimization_barrier((rest, entering))
    ff_w = all_depths(rest[..., value_size:])
    probs = (blocks("sid,sjd->sij", queries, keys) * within_fade).astype(bf16)
    mixed = blocks("sij,sje->sie", probs, values) + blocks("sid,sde->sie", queries_faded, entering)
    gated_wide, gate_back = jax.vjp(
        gate_mix, mixed.reshape(rows, value_size), swish_pre, group[0], group[1]
    )
    gated = gated_wide.astype(bf16)
    branch = scatter_product([gated], out_t, 0, 1)
    hidden = inputs + branch

    mlp_wide, norm_mid_back = jax.vjp(layer_norm, hidden, mlp_gain_full, mlp_bias_full)
    mlp_in = gather_rows(mlp_wide.astype(bf16), 4)
    inner, ff_low, ff_part = feed_forward(mlp_in, error_all, ff_w)

    def sum_depths(grads):
        grads = with_layout_constraint(grads.astype(bf16), Layout((0, 1)))
        mine = lax.psum_scatter(grads, "ctx", scatter_dimension=0, tiled=True)
        return mine.reshape(nf, depth, -1)

    ff_sum = sum_depths(ff_part)
    mlp_in_grad = scatter_product([ff_low], ff_w, 0, 6)
    hidden_norm_grad, grad_mlp_gain, grad_mlp_bias = norm_mid_back(mlp_in_grad)
    hidden_grad = error + hidden_norm_grad

    out_part, gated_grad = gather_products(hidden_grad.astype(bf16), gated, out_t, 10)
    out_sum = sum_depths(out_part)
    mixed_grad, swish_grad, grad_group_gain, grad_group_bias = gate_back(gated_grad)
    swish_low = swish_grad.astype(bf16)
    mixed_low = mixed_grad.astype(bf16).reshape(seqs, span, value_size)
    score_low = (blocks("sie,sje->sij", mixed_low, values) * within_fade).astype(bf16)
    pulled_state = blocks("sid,sie->sde", queries_faded, mixed_low)
    swish_part = product_left(normed, swish_low).astype(bf16)
    swish_part, pulled_state, ff_sum = lax.optimization_barrier(
        (swish_part, pulled_state, ff_sum)
    )
    later, mlp_out, grad_gelu, grad_up, grad_down = pass_and_scatter(
        pulled_state, block_fade, inner, ff_w, 2 * hidden_size, ff_sum, -1, 3
    )
    out_sum, swish_part, later = lax.optimization_barrier((out_sum, swish_part, later))
    swish_sum = sum_depths(swish_part)
    block_own = (hidden + mlp_out).astype(bf16)
    query_grad = blocks("sij,sjd->sid", score_low, keys) + query_fade * blocks(
        "sie,sde->sid", mixed_low, entering
    )
    key_grad = blocks("sij,sid->sjd", score_low, queries) + key_fade * blocks(
        "sje,sde->sjd", values, later
    )
    value_grad = blocks("sij,sie->sje", probs, mixed_low) + blocks(
        "sjd,sde->sje", keys_faded, later
    )
    query_low = rotate_back(query_grad, cosine, sine).astype(bf16).reshape(rows, key_size)
    key_low = rotate_back(key_grad * key_scale * valid, cosine, sine).astype(bf16)
    low = jnp.concatenate(
        [
            query_low,
            key_low.reshape(rows, key_size),
            value_grad.astype(bf16).reshape(rows, value_size),
        ],
        -1,
    )
    attn_part = product_left(normed, low).astype(bf16)
    attn_part, low = lax.optimization_barrier((attn_part, low))
    attn_sum = sum_depths(attn_part)
    normed_grad = scatter_product([low, swish_low], attn_w, 0, 7)
    swish_sum, normed_grad = lax.optimization_barrier((swish_sum, normed_grad))
    input_norm_grad, grad_pre_gain, grad_pre_bias = norm_in_back(normed_grad)
    tokens_own = (hidden_grad + input_norm_grad).astype(bf16)

    norm_parts = jnp.stack([grad_pre_gain, grad_pre_bias, grad_mlp_gain, grad_mlp_bias])
    norm_parts = norm_parts.reshape(4, nf * nc, 1, depth).transpose(1, 2, 0, 3)
    norm_parts = jnp.broadcast_to(norm_parts, (nf * nc, nt, 4, depth)).reshape(nf * nc, nt, -1)
    mine = lax.iota(jnp.int32, nt * heads_local) == head
    group_parts = jnp.stack([grad_group_gain, grad_group_bias]).reshape(1, 2, nf * nc, -1)
    group_parts = jnp.where(mine[:, None, None, None], group_parts, 0.0)
    group_parts = group_parts.reshape(nt, heads_local, 2, nf * nc, -1).transpose(3, 0, 2, 1, 4)
    parts = jnp.concatenate([norm_parts, group_parts.reshape(nf * nc, nt, -1)], -1)
    parts = parts.reshape(nf * nc * nt, -1)
    sums, grad_out, grad_swish, block_out, grad_tokens = close(
        pad_tile(parts), out_sum, swish_sum, block_own, tokens_own, 5
    )
    block_valid = (positions[None, :] < lengths[:, None]).astype(bf16)[:, :, None]
    block_out = block_out.reshape(tokens.shape) * block_valid
    grad_tokens = grad_tokens.reshape(tokens.shape) * block_valid
    grad_out, grad_swish = grad_out.astype(f32), grad_swish.astype(f32)
    sums, attn_sum, block_out, grad_tokens, grad_out, grad_swish = lax.optimization_barrier(
        (sums, attn_sum, block_out, grad_tokens, grad_out, grad_swish)
    )
    sums = sums.reshape(-1)[: parts.shape[1]]
    grad_query, grad_key, grad_value = finish(
        [attn_sum], [[key_size, key_size, value_size]], [False], 11
    )
    norm_sums = sums[: 4 * depth].reshape(4, depth)
    group_sums = sums[4 * depth :].reshape(2, heads_local, -1)

    return (
        block_out,
        grad_tokens,
        norm_sums[0],
        norm_sums[1],
        grad_query,
        grad_key,
        grad_value,
        grad_swish,
        grad_out,
        group_sums[0],
        group_sums[1],
        norm_sums[2],
        norm_sums[3],
        grad_gelu,
        grad_up,
        grad_down,
    )


def solution(mesh):
    rows = P("fsdp", "ctx", None)
    vector = P(("fsdp", "ctx"))
    tall = P(("fsdp", "ctx"), "tp")
    wide = P("tp", ("fsdp", "ctx"))
    in_specs = (rows, P("fsdp"), rows, vector, vector, tall, tall, tall, tall, wide)
    in_specs += (wide, wide, vector, vector, tall, tall, wide)
    out_specs = (rows, rows, vector, vector, tall, tall, tall, tall, wide)
    out_specs += (wide, wide, vector, vector, tall, tall, wide)
    return jax.shard_map(shards, mesh=mesh, in_specs=in_specs, out_specs=out_specs, check_vma=False)
```

```python
import functools
import math

import jax
import jax.numpy as jnp
from jax import lax
from jax.experimental import pallas as pl
from jax.experimental.layout import Layout, with_layout_constraint
from jax.experimental.pallas import tpu as pltpu
from jax.sharding import PartitionSpec as P

eps = 1e-05
SPARE = 6 << 20
group_floor = 1.0
f32 = jnp.float32
bf16 = jnp.bfloat16


def layer_norm(values, norm_gain, norm_shift):
    centred = values - jnp.mean(values, -1, keepdims=True)
    spread = jnp.mean(centred * centred, -1, keepdims=True)
    return centred * lax.rsqrt(spread + eps) * norm_gain + norm_shift


def turn_tables(positions, half_size):
    frequency = jnp.power(10000.0, -jnp.arange(half_size).astype(f32) / half_size)
    angles = positions.astype(f32)[:, None] * frequency[None, :]
    return jnp.cos(angles), jnp.sin(angles)


def rotate(values, cosine, sine):
    half_size = values.shape[-1] // 2
    first = values[..., :half_size]
    second = values[..., half_size:]
    return jnp.concatenate([first * cosine - second * sine, second * cosine + first * sine], -1)


def rotate_back(values, cosine, sine):
    return rotate(values, cosine, -sine)


def gate_mix(mixed, swish_pre, norm_gain, norm_shift):
    centred = mixed - jnp.mean(mixed, -1, keepdims=True)
    spread = jnp.mean(centred * centred, -1, keepdims=True)
    return jax.nn.silu(swish_pre) * (
        centred * lax.rsqrt(spread + group_floor) * norm_gain + norm_shift
    )


def mlp_mix(gelu_pre, up_pre):
    return jax.nn.gelu(gelu_pre) * up_pre


def product(left, right):
    return jnp.dot(left, right, preferred_element_type=f32)


def product_left(left, right):
    return lax.dot_general(left, right, (((0,), (0,)), ((), ())), preferred_element_type=f32)


def product_right(left, right):
    return lax.dot_general(left, right, (((1,), (1,)), ((), ())), preferred_element_type=f32)


def blocks(spec, left, right):
    return jnp.einsum(spec, left, right, preferred_element_type=f32)


MESH = pl.DeviceIdType.MESH


def beside(f):
    return f + 1 - 2 * (f % 2), (f + 2) % 4, 3 - f


def remote(src, dst, send, recv, device):
    return pltpu.make_async_remote_copy(
        src_ref=src, dst_ref=dst, send_sem=send, recv_sem=recv, device_id=device, device_id_type=MESH
    )


def reorder(src, dst, kind, back):
    nf, nc = lax.axis_size("fsdp"), lax.axis_size("ctx")
    depth = src.shape[-1] // (nf * nc)
    for f in range(nf):
        for c in range(nc):
            plain, mixed = (f * nc + c) * depth, (c * nf + f) * depth
            if back:
                plain, mixed = mixed, plain
            dst[:, mixed : mixed + depth] = src[:, plain : plain + depth].astype(kind)


def gather_steps(plain, out, mixed, keep, send, recv):
    own = plain if mixed is None else mixed
    f, t = lax.axis_index("fsdp"), lax.axis_index("tp")
    fx, fy, fd = beside(f)
    x, y, core = {"fsdp": fx}, {"fsdp": fy}, {"tp": 1 - t}
    half = own.shape[0] // 2

    def part(ref, h):
        return ref.at[pl.ds(h * half, half)]

    def slot(who, h):
        return part(out.at[2 * who + t], h)

    local = pltpu.make_async_copy(own, out.at[2 * f + t], keep)
    first = [
        remote(part(own, 0), slot(f, 0), send.at[0], recv.at[0], x),
        remote(part(own, 1), slot(f, 1), send.at[1], recv.at[3], y),
        remote(part(own, 1), slot(f, 1), send.at[2], recv.at[1], x),
        remote(part(own, 0), slot(f, 0), send.at[3], recv.at[2], y),
        remote(part(own, 0), slot(f, 0), send.at[4], recv.at[6], core),
        remote(part(own, 1), slot(f, 1), send.at[5], recv.at[7], core),
    ]
    sent = list(first)

    def pass_on(who, h, s, r, device):
        copy = remote(slot(who, h), slot(who, h), send.at[s], recv.at[r], device)
        copy.start()
        sent.append(copy)

    def begin():
        if mixed is not None:
            reorder(plain, mixed, mixed.dtype, False)
        local.start()
        for copy in first:
            copy.start()

    def relay():
        first[0].wait_recv()
        pass_on(fx, 0, 6, 4, y)
        pass_on(fx, 0, 7, 8, core)
        first[1].wait_recv()
        pass_on(fy, 1, 8, 5, x)
        pass_on(fy, 1, 9, 11, core)

    def rest():
        first[2].wait_recv()
        pass_on(fx, 1, 10, 9, core)
        first[3].wait_recv()
        pass_on(fy, 0, 11, 10, core)

    def diagonal():
        remote(slot(fd, 0), slot(fd, 0), send.at[12], recv.at[4], y).wait_recv()
        pass_on(fd, 0, 12, 12, core)
        remote(slot(fd, 1), slot(fd, 1), send.at[13], recv.at[5], x).wait_recv()
        pass_on(fd, 1, 13, 13, core)

    def end(crossed=False):
        if not crossed:
            for r in range(6, 14):
                remote(slot(f, 0), slot(f, 0), send.at[0], recv.at[r], core).wait_recv()
            local.wait()
        for copy in sent:
            copy.wait_send()

    return begin, relay, rest, diagonal, end


def in_kernel(width):
    return width // (lax.axis_size("fsdp") * lax.axis_size("ctx")) % 128 == 0


def gather_scratch(own):
    return [
        pltpu.VMEM(own.shape if in_kernel(own.shape[1]) else (16, 128), own.dtype),
        pltpu.SemaphoreType.DMA,
        pltpu.SemaphoreType.DMA((14,)),
        pltpu.SemaphoreType.DMA((14,)),
    ]


def scatter_steps(start, lefts, right, out, mine, sent, theirs, total, diag, last, send, recv):
    f, t = lax.axis_index("fsdp"), lax.axis_index("tp")
    fx, fy, fd = beside(f)
    x, y, core = {"fsdp": fx}, {"fsdp": fy}, {"tp": 1 - t}
    half = out.shape[0] // 2
    order = [fd, fy, fx, f]
    tile = 512

    def part(ref, h):
        return ref.at[pl.ds(h * half, half)]

    crossing = [
        remote(sent.at[i], theirs.at[i], send.at[i], recv.at[i], core) for i in range(4)
    ]
    d0 = remote(part(total.at[0], 0), diag.at[0], send.at[4], recv.at[4], x)
    d1 = remote(part(total.at[0], 1), diag.at[1], send.at[5], recv.at[5], y)
    y1 = remote(part(total.at[1], 1), part(last.at[1], 1), send.at[6], recv.at[6], y)
    x0 = remote(part(total.at[2], 0), part(last.at[0], 0), send.at[7], recv.at[7], x)
    y0 = remote(part(total.at[1], 0), part(last.at[1], 0), send.at[8], recv.at[8], y)
    x1 = remote(part(total.at[2], 1), part(last.at[0], 1), send.at[9], recv.at[9], x)

    def make(block, put):
        def piece(j, carry):
            columns = pl.ds(pl.multiple_of(j * tile, tile), tile)
            at, value = start, 0.0
            for left in lefts:
                size = left.shape[2]
                value += product_right(left[block], right[columns, at : at + size])
                at += size
            put(columns, value)
            return carry

        lax.fori_loop(0, out.shape[1] // tile, piece, 0)

    def cross(i):
        def put(columns, value):
            sent[i, :, columns] = value.astype(sent.dtype)

        make(2 * order[i] + 1 - t, put)
        crossing[i].start()

    def keep(i):
        def put(columns, value):
            mine[:, columns] = value

        make(2 * order[i] + t, put)

    def add(i):
        keep(i)
        crossing[i].wait_recv()
        total[i] = (mine[...] + theirs[i].astype(f32)).astype(total.dtype)

    def diagonal():
        cross(0)
        cross(1)
        add(0)
        d0.start()
        d1.start()

    def straight():
        cross(2)
        add(1)
        y1.start()
        add(2)
        x0.start()
        cross(3)

    def relay():
        d0.wait_recv()
        total[1, :half] = (total[1, :half].astype(f32) + diag[0].astype(f32)).astype(total.dtype)
        y0.start()
        d1.wait_recv()
        total[2, half:] = (total[2, half:].astype(f32) + diag[1].astype(f32)).astype(total.dtype)
        x1.start()
        keep(3)
        crossing[3].wait_recv()
        mine[...] += theirs[3].astype(f32)

    def end():
        for copy in (y1, x0, y0, x1):
            copy.wait_recv()
        mine[...] += last[0].astype(f32) + last[1].astype(f32)
        if in_kernel(out.shape[1]):
            reorder(mine, out, out.dtype, True)
        else:
            out[...] = mine[...]
        for copy in (*crossing, d0, d1, y1, x0, y0, x1):
            copy.wait_send()

    return diagonal, straight, relay, end


def scatter_scratch(rows, width):
    return [
        pltpu.VMEM((rows, width), f32),
        pltpu.VMEM((4, rows, width), bf16),
        pltpu.VMEM((4, rows, width), bf16),
        pltpu.VMEM((3, rows, width), bf16),
        pltpu.VMEM((2, rows // 2, width), bf16),
        pltpu.VMEM((2, rows, width), bf16),
        pltpu.SemaphoreType.DMA((10,)),
        pltpu.SemaphoreType.DMA((10,)),
    ]


def pass_steps(by, local, fade, out, held, send, recv):
    length = lax.axis_size("ctx")
    c = lax.axis_index("ctx")
    first = c == (0 if by > 0 else length - 1)
    last = c == (length - 1 if by > 0 else 0)
    target = lax.rem(c + by + length, length)

    def copy(p):
        return remote(held.at[p], out.at[p], send.at[p], recv.at[p], {"ctx": target})

    def step(p, carry):
        @pl.when(first)
        def _():
            out[p] = jnp.zeros(out.shape[1:], out.dtype)

        @pl.when(jnp.logical_not(first))
        def _():
            copy(p).wait_recv()

        @pl.when(jnp.logical_not(last))
        def _():
            held[p] = (fade[...] * out[p].astype(f32) + local[p]).astype(held.dtype)
            copy(p).start()

        return carry

    def run(quarter):
        count = local.shape[0]
        if quarter < 0:
            lax.fori_loop(0, jnp.where(first, count, 0), step, 0)
        else:
            low, high = quarter * count // 4, (quarter + 1) * count // 4
            lax.fori_loop(jnp.where(first, count, low), jnp.where(first, count, high), step, 0)

    def end():
        @pl.when(jnp.logical_not(last))
        def _():
            def done(p, carry):
                copy(p).wait_send()
                return carry

            lax.fori_loop(0, local.shape[0], done, 0)

    return run, end


def greet_plane(by=0, diagonal=False):
    f, c, t = lax.axis_index("fsdp"), lax.axis_index("ctx"), lax.axis_index("tp")
    length = lax.axis_size("ctx")
    fx, fy, fd = beside(f)
    barrier = pltpu.get_barrier_semaphore()
    peers = [{"fsdp": fx}, {"fsdp": fy}, {"tp": 1 - t}] + [{"fsdp": fd}] * diagonal
    for device in peers:
        pl.semaphore_signal(barrier, inc=1, device_id=device, device_id_type=MESH)
    if by != 0:
        first = c == (0 if by > 0 else length - 1)
        last = c == (length - 1 if by > 0 else 0)
        source = {"ctx": lax.rem(c - by + length, length)}

        @pl.when(jnp.logical_not(first))
        def _():
            pl.semaphore_signal(barrier, inc=1, device_id=source, device_id_type=MESH)

        @pl.when(jnp.logical_not(last))
        def _():
            pl.semaphore_wait(barrier, len(peers) + 1)

        @pl.when(last)
        def _():
            pl.semaphore_wait(barrier, len(peers))
    else:
        pl.semaphore_wait(barrier, len(peers))


def gather_with(own, full, mixed, *scratch):
    return gather_steps(own, full, mixed if in_kernel(own.shape[1]) else None, *scratch)


def gather_kernel(*refs):
    steps = gather_with(*refs)
    greet_plane()
    for step in steps:
        step()


def scatter_kernel(count, start, *refs):
    steps = scatter_steps(start, refs[:count], *refs[count:])
    greet_plane()
    for step in steps:
        step()


def gather_products_kernel(own, left, right, grad, back, full, total, mixed, *scratch):
    f, t = lax.axis_index("fsdp"), lax.axis_index("tp")
    fx, fy, fd = beside(f)
    recv = scratch[2]
    begin, relay, rest, diagonal, end = gather_with(own, full, mixed, *scratch)
    tile = 512

    def use(block, fresh=False):
        back[block] = product(full[block], right[...])

        def piece(j, carry):
            columns = pl.ds(pl.multiple_of(j * tile, tile), tile)
            value = product_left(full[block, :, columns], left[block])
            total[columns, :] = value if fresh else total[columns, :] + value
            return carry

        lax.fori_loop(0, total.shape[0] // tile, piece, 0)

    def crossed(who, r):
        block = full.at[2 * who + 1 - t]
        half = block.shape[0] // 2
        for h in range(2):
            where = block.at[pl.ds(h * half, half)]
            remote(where, where, scratch[1].at[0], recv.at[r + h], {"tp": 1 - t}).wait_recv()

    greet_plane()
    begin()
    pltpu.make_async_copy(full.at[2 * f + t], full.at[2 * f + t], scratch[0]).wait()
    use(2 * f + t, True)
    relay()
    crossed(f, 6)
    use(2 * f + 1 - t)
    rest()
    use(2 * fx + t)
    use(2 * fy + t)
    crossed(fx, 8)
    use(2 * fx + 1 - t)
    crossed(fy, 10)
    use(2 * fy + 1 - t)
    diagonal()
    use(2 * fd + t)
    crossed(fd, 12)
    use(2 * fd + 1 - t)
    end(True)
    grad[...] = total[...].astype(grad.dtype)


def gather_products(own, left, right, collective_id):
    own = ready(own)
    rows, width = own.shape
    size = left.shape[1]
    grad, back = call(
        gather_products_kernel,
        collective_id,
        [
            (jax.ShapeDtypeStruct((width, size), bf16), pltpu.VMEM),
            (jax.ShapeDtypeStruct((8, rows, size), f32), pltpu.VMEM),
        ],
        [vmem()] * 3,
        [
            pltpu.VMEM((8, rows, width), bf16),
            pltpu.VMEM((width, size), f32),
            *gather_scratch(own),
        ],
        own,
        in_eights(left),
        right,
        tight=True,
    )
    return grad, back.reshape(8 * rows, size)


def pass_gather_kernel(by, local, fade, own, out, full, held, send, recv, *scratch):
    begin, relay, rest, diagonal, end = gather_with(own, full, *scratch)
    run, done = pass_steps(by, local, fade, out, held, send, recv)
    greet_plane(by)
    run(-1)
    begin()
    run(0)
    relay()
    run(1)
    rest()
    run(2)
    run(3)
    diagonal()
    end()
    done()


def pass_scatter_kernel(by, start, local, fade, left, right, ff, out, own, *refs):
    gelu_grad, up_grad, down_grad, held, send, recv = refs[:6]
    scratch, hand = refs[6:-3], refs[-3:]
    targets = [[(gelu_grad, False), (up_grad, False), (down_grad, True)]]
    hand_over, take = hand_steps([ff], targets, *hand)
    diagonal, straight, relay, end = scatter_steps(start, [left], right, own, *scratch)
    run, done = pass_steps(by, local, fade, out, held, send, recv)
    greet_plane(by, True)
    run(-1)
    diagonal()
    straight()
    hand_over()
    run(0)
    relay()
    run(1)
    run(2)
    run(3)
    end()
    take()
    done()


def held_bytes(array):
    last = -(-array.shape[-1] // 128) * 128
    return math.prod(array.shape[:-1]) * last * jnp.dtype(array.dtype).itemsize


def call(kernel, collective_id, outs, ins, scratch, *args, tight=False):
    shapes, spaces = zip(*outs)
    limit = 52 << 20
    held = [shape for shape, space in outs if space == pltpu.VMEM]
    held += [arg for arg, spec in zip(args, ins) if spec.memory_space == pltpu.VMEM]
    held += [one for one in scratch if getattr(one, "memory_space", None) == pltpu.VMEM]
    if tight:
        limit = sum(held_bytes(one) for one in held) + SPARE
    return pl.pallas_call(
        kernel,
        out_shape=shapes,
        in_specs=ins,
        out_specs=tuple(pl.BlockSpec(memory_space=space) for space in spaces),
        scratch_shapes=scratch,
        compiler_params=pltpu.CompilerParams(
            collective_id=collective_id, has_side_effects=True, vmem_limit_bytes=limit
        ),
        cost_estimate=pl.CostEstimate(flops=0, bytes_accessed=2_000_000, transcendentals=0),
    )(*args)


def vmem():
    return pl.BlockSpec(memory_space=pltpu.VMEM)


def perm(v):
    nf, nc = lax.axis_size("fsdp"), lax.axis_size("ctx")
    return v.reshape(len(v), nf, nc, -1).transpose(0, 2, 1, 3).reshape(v.shape)


def unperm(v):
    nf, nc = lax.axis_size("fsdp"), lax.axis_size("ctx")
    return v.reshape(len(v), nc, nf, -1).transpose(0, 2, 1, 3).reshape(v.shape)


def gathered(own):
    rows, width = own.shape
    return jax.ShapeDtypeStruct((8, rows, width), own.dtype), pl.ANY


def scattered(left, right):
    return jax.ShapeDtypeStruct((left.shape[0] // 8, right.shape[0]), f32), pltpu.VMEM


def passed(local):
    return jax.ShapeDtypeStruct(local.shape, bf16), pltpu.VMEM


def pass_scratch(local):
    pieces = local.shape[0]
    return [
        pltpu.VMEM(local.shape, bf16),
        pltpu.SemaphoreType.DMA((pieces,)),
        pltpu.SemaphoreType.DMA((pieces,)),
    ]


def in_eights(left):
    return left.reshape(8, -1, left.shape[1])


def ready(own):
    return own if in_kernel(own.shape[1]) else perm(own)


def plain(own):
    return own if in_kernel(own.shape[1]) else unperm(own)


def gather_rows(own, collective_id):
    own = ready(own)
    (out,) = call(gather_kernel, collective_id, [gathered(own)], [vmem()], gather_scratch(own), own)
    return out.reshape(-1, own.shape[1])


def scatter_product(lefts, right, start, collective_id):
    rows, width = lefts[0].shape[0] // 8, right.shape[0]
    (out,) = call(
        functools.partial(scatter_kernel, len(lefts), start),
        collective_id,
        [(jax.ShapeDtypeStruct((rows, width), f32), pltpu.VMEM)],
        [vmem()] * (len(lefts) + 1),
        scatter_scratch(rows, width),
        *(in_eights(left) for left in lefts),
        right,
    )
    return plain(out)


def pass_and_gather(local, fade, own, by, collective_id):
    shape = local.shape
    local = local.reshape(4 * shape[0], -1, shape[2])
    own = ready(own)
    out, full = call(
        functools.partial(pass_gather_kernel, by),
        collective_id,
        [passed(local), gathered(own)],
        [vmem(), vmem(), vmem()],
        pass_scratch(local) + gather_scratch(own),
        local,
        jnp.full((1, local.shape[2]), fade, f32),
        own,
    )
    return out.reshape(shape), full.reshape(-1, own.shape[1])


def feed_forward_kernel(rows, error, weight, inner, low, grads, total):
    step = pl.program_id(0)
    size, tile, deep = inner.shape[1], 512, 1024
    root = (2.0 / jnp.pi) ** 0.5

    def units(j, carry):
        at = pl.multiple_of(j * tile, tile)
        gelu_pre = product(rows[...], weight[:, pl.ds(at, tile)])
        up_pre = product(rows[...], weight[:, pl.ds(at + size, tile)])
        square = gelu_pre * gelu_pre
        bend = jnp.tanh(root * gelu_pre * (1.0 + 0.044715 * square))
        half = 0.5 * (1.0 + bend)
        gelu = gelu_pre * half
        slope = half + 0.5 * gelu_pre * (1.0 - bend * bend) * root * (1.0 + 0.134145 * square)
        inner[:, pl.ds(at, tile)] = (gelu * up_pre).astype(bf16)
        inner_grad = product(error[...], weight[:, pl.ds(at + 2 * size, tile)])
        low[:, pl.ds(at, tile)] = (inner_grad * up_pre * slope).astype(bf16)
        low[:, pl.ds(at + size, tile)] = (inner_grad * gelu).astype(bf16)
        return carry

    lax.fori_loop(0, size // tile, units, 0)

    def depths(first, last):
        def piece(j, carry):
            at = pl.ds(pl.multiple_of(j * deep, deep), deep)
            into = grads if last else total
            for left, right, columns in (
                (rows, low, slice(0, 2 * size)),
                (error, inner, slice(2 * size, 3 * size)),
            ):
                value = product_left(left[:, at], right[...])
                if not first:
                    value += total[at, columns]
                into[at, columns] = value.astype(into.dtype)
            return carry

        lax.fori_loop(0, total.shape[0] // deep, piece, 0)

    steps = pl.num_programs(0)
    pl.when(step == 0)(lambda: depths(True, False))
    pl.when((step > 0) & (step < steps - 1))(lambda: depths(False, False))
    pl.when(step == steps - 1)(lambda: depths(False, True))


def feed_forward(rows, error, weight):
    count, width = rows.shape
    size, block = weight.shape[1] // 3, 512
    whole = pl.BlockSpec(weight.shape, lambda i: (0, 0))

    def some(columns):
        return pl.BlockSpec((block, columns), lambda i: (i, 0))

    return pl.pallas_call(
        feed_forward_kernel,
        grid=(count // block,),
        out_shape=(
            jax.ShapeDtypeStruct((count, size), bf16),
            jax.ShapeDtypeStruct((count, 2 * size), bf16),
            jax.ShapeDtypeStruct(weight.shape, bf16),
        ),
        in_specs=[some(width), some(width), whole],
        out_specs=(some(size), some(2 * size), whole),
        scratch_shapes=[pltpu.VMEM(weight.shape, f32)],
        compiler_params=pltpu.CompilerParams(vmem_limit_bytes=56 << 20),
        cost_estimate=pl.CostEstimate(
            flops=14 * count * width * size, bytes_accessed=40_000_000, transcendentals=count * size
        ),
    )(rows, error, weight)


def pass_and_scatter(local, fade, left, right, start, ff, by, collective_id):
    shape = local.shape
    local = local.reshape(8 * shape[0], -1, shape[2])
    out, own, *grads = call(
        functools.partial(pass_scatter_kernel, by, start),
        collective_id,
        [
            passed(local),
            scattered(left, right),
            *handed(ff, [left.shape[1]] * 2),
            *handed(ff, [left.shape[1]], True),
        ],
        [vmem()] * 5,
        pass_scratch(local)
        + scatter_scratch(left.shape[0] // 8, right.shape[0])
        + hand_scratch([ff]),
        local,
        jnp.full((1, local.shape[2]), fade, f32),
        in_eights(left),
        right,
        ff,
    )
    return out.reshape(shape), plain(own), *(grad.astype(f32) for grad in grads)


def peer_of(place, nc, nt):
    return {"fsdp": place // (nc * nt), "ctx": place // nt % nc, "tp": place % nt}


def line_steps(home, place, arrived, send, recv):
    nf, nc = lax.axis_size("fsdp"), lax.axis_size("ctx")
    f, c = lax.axis_index("fsdp"), lax.axis_index("ctx")
    order = [f, *beside(f)]
    above, below = c < nc - 1, c > 0

    def copy(src, place_of, who, up):
        chunk = place_of * nf + who
        return remote(
            src,
            place(place_of, who),
            send.at[chunk if up else nc * nf + chunk],
            recv.at[chunk],
            {"ctx": lax.rem(c + 1, nc) if up else lax.rem(c + nc - 1, nc)},
        )

    def first(i):
        who = order[i]
        arrived(i)

        @pl.when(above)
        def _():
            copy(home(who), c, who, True).start()

        @pl.when(below)
        def _():
            copy(home(who), c, who, False).start()

    def step(k, carry):
        for who in order:

            @pl.when(c - k >= 0)
            def _():
                copy(place(c - k, who), c - k, who, True).wait_recv()

                @pl.when(above)
                def _():
                    copy(place(c - k, who), c - k, who, True).start()

            @pl.when(c + k < nc)
            def _():
                copy(place(c + k, who), c + k, who, False).wait_recv()

                @pl.when(below)
                def _():
                    copy(place(c + k, who), c + k, who, False).start()

        return carry

    def end():
        def one(other, carry):
            for who in order:

                @pl.when(above & (other <= c))
                def _():
                    copy(place(other, who), other, who, True).wait_send()

                @pl.when(below & (other >= c))
                def _():
                    copy(place(other, who), other, who, False).wait_send()

            return carry

        lax.fori_loop(0, nc, one, 0)

    return first, step, end


def line_scratch():
    count = lax.axis_size("fsdp") * lax.axis_size("ctx")
    return [pltpu.SemaphoreType.DMA((2 * count,)), pltpu.SemaphoreType.DMA((count,))]


def start_kernel(sizes, split, turned, own, small, *refs):
    count = len(sizes)
    weights = list(refs[:count])
    attn, rest, full, everyone = refs[count : count + 4]
    (
        brought,
        untouched,
        fetch,
        turns,
        gains,
        normed,
        mixed,
        gather_keep,
        gather_send,
        gather_recv,
        line_send,
        line_recv,
        keep,
        send,
        recv,
        small_send,
        small_recv,
    ) = refs[count + 4 :]
    nf, nc = lax.axis_size("fsdp"), lax.axis_size("ctx")
    f, c, t = lax.axis_index("fsdp"), lax.axis_index("ctx"), lax.axis_index("tp")
    here, places = f * nc + c, nf * nc
    depth = weights[0].shape[0]
    across = [weights[i] for i in turned]
    for n, i in enumerate(turned):
        weights[i] = turns.at[n]
    rows = normed.shape[0]
    fetched = [
        pltpu.make_async_copy(
            own.at[pl.ds(pl.multiple_of(t * rows, rows), rows)], brought, fetch.at[0]
        )
    ]
    fetched += [
        pltpu.make_async_copy(matrix, untouched.at[n], fetch.at[n + 1])
        for n, matrix in enumerate(across)
    ]
    for copy in fetched:
        copy.start()
    near = beside(f)
    starts = [sum(sizes[:i]) if i < split else sum(sizes[split:i]) for i in range(count)]

    def peer(i):
        other = lax.rem(here + i, places)
        return {"fsdp": other // nc, "ctx": other % nc}

    barrier = pltpu.get_barrier_semaphore()
    pl.semaphore_signal(barrier, inc=1, device_id={"tp": 1 - t}, device_id_type=MESH)

    def hello(i, carry):
        pl.semaphore_signal(barrier, inc=1, device_id=peer(i), device_id_type=MESH)
        return carry

    lax.fori_loop(1, places, hello, 0)
    pl.semaphore_wait(barrier, places)

    def chunk(place_of, who):
        rows = pl.multiple_of((place_of * nf + who) * depth, depth)
        return attn.at[pl.ds(rows, depth)]

    def columns(i, who):
        return weights[i].at[:, pl.ds(pl.multiple_of(who * sizes[i], sizes[i]), sizes[i])]

    def target(i):
        where = chunk(c, f) if i < split else rest.at[f]
        return where.at[:, pl.ds(starts[i], sizes[i])]

    def hand_out(i, n):
        return remote(
            columns(i, near[n]),
            target(i),
            send.at[3 * i + n],
            recv.at[n if i < split else 3 + n],
            {"fsdp": near[n]},
        )

    def hold(i):
        return pltpu.make_async_copy(columns(i, f), target(i), keep.at[0 if i < split else 1])

    for i in range(split):
        hold(i).start()
    for n in range(3):
        for i in range(split):
            hand_out(i, n).start()

    def arrived(i):
        if i == 0:
            pltpu.make_async_copy(chunk(c, f), chunk(c, f), keep.at[0]).wait()
        else:
            who = near[i - 1]
            remote(
                chunk(c, who), chunk(c, who), send.at[0], recv.at[i - 1], {"fsdp": who}
            ).wait_recv()

    first, step, end = line_steps(lambda who: chunk(c, who), chunk, arrived, line_send, line_recv)
    first(0)

    def tell(i):
        return remote(small, everyone.at[here], small_send.at[i], small_recv.at[i], peer(i))

    def go(i, carry):
        tell(i).start()
        return carry

    def told(i, carry):
        tell(i).wait()
        return carry

    lax.fori_loop(1, places, go, 0)
    everyone[here] = small[...]
    first(1)
    lax.fori_loop(1, places, told, 0)
    for i in range(places):
        for j in range(2):
            gains[j : j + 1, i * depth : (i + 1) * depth] = everyone[i, j : j + 1, :depth]
    fetched[0].wait()
    normed[...] = layer_norm(brought[...].astype(f32), gains[0:1, :], gains[1:2, :]).astype(bf16)
    begin, relay, others, diagonal, finish = gather_steps(
        normed, full, mixed, gather_keep, gather_send, gather_recv
    )
    begin()
    first(2)
    first(3)
    step(1, 0)
    relay()
    for n in range(len(turned)):
        fetched[n + 1].wait()
        turns[n] = untouched[n].T
    for i in range(split, count):
        hold(i).start()
        for n in range(3):
            hand_out(i, n).start()
    lax.fori_loop(2, 3, step, 0)
    others()
    diagonal()
    lax.fori_loop(3, nc, step, 0)
    finish()
    pltpu.make_async_copy(rest.at[f], rest.at[f], keep.at[1]).wait()
    for n in range(3):
        where = rest.at[near[n]]
        remote(where, where, send.at[0], recv.at[3 + n], {"fsdp": near[n]}).wait_recv()
    for i in range(count):
        for n in range(3):
            hand_out(i, n).wait_send()
    end()


def start(tokens, small, weights, split, turned, collective_id):
    nf, nc = lax.axis_size("fsdp"), lax.axis_size("ctx")
    rows, width = tokens.shape
    rows //= lax.axis_size("tp")
    depth = weights[0].shape[0]
    sizes = [w.size // depth // nf for w in weights]
    anywhere = pl.BlockSpec(memory_space=pl.ANY)
    count = nf * nc
    return call(
        functools.partial(start_kernel, sizes, split, turned),
        collective_id,
        [
            (jax.ShapeDtypeStruct((width, sum(sizes[:split])), bf16), pl.ANY),
            (jax.ShapeDtypeStruct((nf, depth, sum(sizes[split:])), bf16), pl.ANY),
            (jax.ShapeDtypeStruct((8, rows, width), bf16), pl.ANY),
            (jax.ShapeDtypeStruct((count, *small.shape), f32), pltpu.VMEM),
        ],
        [anywhere, vmem()] + [anywhere] * len(weights),
        [
            pltpu.VMEM((rows, width), bf16),
            pltpu.VMEM((len(turned), *weights[turned[0]].shape), bf16),
            pltpu.SemaphoreType.DMA((len(turned) + 1,)),
            pltpu.VMEM((len(turned), depth, sizes[turned[0]] * nf), bf16),
            pltpu.VMEM((8, width), f32),
            pltpu.VMEM((rows, width), bf16),
            pltpu.VMEM((rows, width), bf16),
            *gather_scratch(tokens)[1:],
            *line_scratch(),
            pltpu.SemaphoreType.DMA((2,)),
            pltpu.SemaphoreType.DMA((3 * len(weights),)),
            pltpu.SemaphoreType.DMA((6,)),
            pltpu.SemaphoreType.DMA((count,)),
            pltpu.SemaphoreType.DMA((count,)),
        ],
        tokens,
        small,
        *weights,
    )


def hand_steps(parts, outs, slots, send, recv):
    f = lax.axis_index("fsdp")
    near = beside(f)
    starts = [sum(part.shape[2] for part in parts[:i]) for i in range(len(parts))]

    def copies(n):
        return [
            remote(
                part.at[near[n]],
                slots.at[n, :, pl.ds(at, part.shape[2])],
                send.at[len(parts) * n + i],
                recv.at[len(parts) * n + i],
                {"fsdp": near[n]},
            )
            for i, (part, at) in enumerate(zip(parts, starts))
        ]

    def begin():
        for n in range(3):
            for copy in copies(n):
                copy.start()

    def put(who, blocks):
        for block, targets in zip(blocks, outs):
            at = 0
            for out, turned in targets:
                size = out.shape[0 if turned else 1] // lax.axis_size("fsdp")
                where = pl.ds(pl.multiple_of(who * size, size), size)
                if turned:
                    out[where, :] = block[:, at : at + size].T
                else:
                    out[:, where] = block[:, at : at + size]
                at += size

    def end():
        put(f, [part[f] for part in parts])
        for n in range(3):
            for copy in copies(n):
                copy.wait()
            put(
                near[n],
                [slots[n, :, at : at + part.shape[2]] for part, at in zip(parts, starts)],
            )

    return begin, end


def hand_scratch(parts):
    size = sum(part.shape[2] for part in parts)
    return [
        pltpu.VMEM((3, parts[0].shape[1], size), bf16),
        pltpu.SemaphoreType.DMA((3 * len(parts),)),
        pltpu.SemaphoreType.DMA((3 * len(parts),)),
    ]


def handed(part, sizes, turned=False):
    nf, depth = part.shape[:2]
    shapes = [(nf * n, depth) if turned else (depth, nf * n) for n in sizes]
    return [(jax.ShapeDtypeStruct(shape, bf16), pltpu.VMEM) for shape in shapes]


def finish_kernel(turned, counts, *refs):
    parts, outs, scratch = refs[: len(turned)], list(refs[len(turned) : -3]), refs[-3:]
    targets = [[(outs.pop(0), turn) for _ in range(n)] for turn, n in zip(turned, counts)]
    begin, end = hand_steps(parts, targets, *scratch)
    greet_fsdp()
    begin()
    end()


def greet_fsdp():
    near = beside(lax.axis_index("fsdp"))
    barrier = pltpu.get_barrier_semaphore()
    for who in near:
        pl.semaphore_signal(barrier, inc=1, device_id={"fsdp": who}, device_id_type=MESH)
    pl.semaphore_wait(barrier, 3)


def finish(parts, sizes, turned, collective_id):
    outs = [one for n in zip(parts, sizes, turned) for one in handed(*n)]
    outs = call(
        functools.partial(finish_kernel, turned, [len(size) for size in sizes]),
        collective_id,
        outs,
        [vmem()] * len(parts),
        hand_scratch(parts),
        *parts,
        tight=True,
    )
    return [out.astype(f32) for out in outs]


def total_steps(parts, out, slots, send, recv):
    nc, nt = lax.axis_size("ctx"), lax.axis_size("tp")
    count = parts.shape[0]
    place = (lax.axis_index("fsdp") * nc + lax.axis_index("ctx")) * nt + lax.axis_index("tp")

    def hello():
        barrier = pltpu.get_barrier_semaphore()

        def one(i, carry):
            other = peer_of(lax.rem(place + i, count), nc, nt)
            pl.semaphore_signal(barrier, inc=1, device_id=other, device_id_type=MESH)
            return carry

        lax.fori_loop(1, count, one, 0)
        pl.semaphore_wait(barrier, count - 1)

    def copy(i):
        other = lax.rem(place + i, count)
        return remote(
            parts.at[other], slots.at[i], send.at[i], recv.at[i], peer_of(other, nc, nt)
        )

    def begin():
        def go(i, carry):
            copy(i).start()
            return carry

        lax.fori_loop(1, count, go, 0)

    def end():
        def add(i, carry):
            copy(i).wait()
            return carry + slots[i]

        out[...] = lax.fori_loop(1, count, add, parts[place])

    return hello, begin, end


def close_kernel(
    parts, first, second, one, two, out, wide, tall, one_both, two_both, slots, send, recv, *scratch
):
    hand, keep, core_send, core_recv = scratch[:3], *scratch[3:]
    t = lax.axis_index("tp")
    hello, begin, end = total_steps(parts, out, slots, send, recv)
    hand_over, take = hand_steps([first, second], [[(wide, True)], [(tall, False)]], *hand)
    hello()
    begin()
    copies = []
    for i, (own, both) in enumerate(((one, one_both), (two, two_both))):
        copies.append(pltpu.make_async_copy(own, both.at[t], keep.at[i]))
        copies.append(
            remote(own, both.at[t], core_send.at[i], core_recv.at[i], {"tp": 1 - t})
        )
    for copy in copies:
        copy.start()
    end()
    for copy in copies:
        copy.wait()
    hand_over()
    take()


def close(parts, first, second, one, two, collective_id):
    count = parts.shape[0]
    both = (jax.ShapeDtypeStruct((2, *one.shape), one.dtype), pltpu.VMEM)
    return call(
        close_kernel,
        collective_id,
        [
            (jax.ShapeDtypeStruct(parts.shape[1:], f32), pltpu.VMEM),
            *handed(first, [first.shape[2]], True),
            *handed(second, [second.shape[2]]),
            both,
            both,
        ],
        [vmem()] * 5,
        [
            pltpu.VMEM(parts.shape, f32),
            pltpu.SemaphoreType.DMA((count,)),
            pltpu.SemaphoreType.DMA((count,)),
            *hand_scratch([first, second]),
            pltpu.SemaphoreType.DMA((2,)),
            pltpu.SemaphoreType.DMA((2,)),
            pltpu.SemaphoreType.DMA((2,)),
        ],
        parts,
        first,
        second,
        one,
        two,
        tight=True,
    )


def shards(
    tokens,
    lengths,
    cotangent,
    pre_gain,
    pre_bias,
    query_weight,
    key_weight,
    value_weight,
    swish_weight,
    out_weight,
    group_gain,
    group_bias,
    mlp_gain,
    mlp_bias,
    gelu_weight,
    up_weight,
    down_weight,
):
    seq_count, span, width = tokens.shape
    nf, nc, nt = lax.axis_size("fsdp"), lax.axis_size("ctx"), lax.axis_size("tp")
    f, c, t = lax.axis_index("fsdp"), lax.axis_index("ctx"), lax.axis_index("tp")
    block_rows = seq_count * span
    own_rows = block_rows // nt
    depth = query_weight.shape[0]
    heads_local = group_gain.shape[0]
    assert heads_local == nf
    key_size = query_weight.shape[1] // heads_local
    value_size = value_weight.shape[1] // heads_local
    hidden_size = gelu_weight.shape[1] // nf
    seqs = nf * seq_count
    rows = seqs * span
    head = t * heads_local + f

    def pad_tile(v):
        return jnp.pad(v, [(0, 0)] * (v.ndim - 1) + [(0, -v.shape[-1] % 1024)]).reshape(
            *v.shape[:-1], 8, -1
        )

    def own_part(v):
        return lax.dynamic_slice_in_dim(v.reshape(block_rows, width), t * own_rows, own_rows, 0)

    def all_depths(mine):
        return lax.all_gather(mine, "ctx", axis=0, tiled=True).reshape(width, -1)

    def padded(v):
        return jnp.pad(v.astype(f32).reshape(-1), (0, 128 - v.size))

    kinds = [pre_gain, pre_bias, mlp_gain, mlp_bias, group_gain, group_bias, lengths]
    small = jnp.stack([padded(v) for v in kinds] + [jnp.zeros(128, f32)])
    weights = [query_weight, key_weight, value_weight, swish_weight]
    weights += [out_weight, gelu_weight, up_weight, down_weight]
    attn_w, rest, normed, small = start(
        tokens.reshape(block_rows, width), small, weights, 4, (4, 7), 0
    )
    small, tokens, cotangent = lax.optimization_barrier((small, tokens, cotangent))
    normed = normed.reshape(rows, width)
    out_t = all_depths(rest[..., :value_size])
    pre_gain_full, pre_bias_full, mlp_gain_full, mlp_bias_full = (
        small[:, i, :depth].reshape(width) for i in range(4)
    )
    group = small[:, 4:6, : group_gain.size].reshape(nf * nc, 2, heads_local, -1)
    group = lax.dynamic_index_in_dim(group, f, 2, False).transpose(1, 0, 2).reshape(2, value_size)
    all_lengths = small.reshape(nf, nc, 8, 128)[:, 0, 6, :seq_count].reshape(seqs)

    inputs = own_part(tokens).astype(f32)
    _, norm_in_back = jax.vjp(layer_norm, inputs, pre_gain_full, pre_bias_full)
    positions = c * span + lax.iota(jnp.int32, span)
    own_ids = t * own_rows + lax.iota(jnp.int32, own_rows)
    own_valid = (c * span + own_ids % span < lengths[own_ids // span]).astype(f32)[:, None]
    error = own_valid * own_part(cotangent).astype(f32)

    pre = product(normed, attn_w)
    valid = (positions.astype(f32)[None, :] < all_lengths[:, None]).astype(f32)[:, :, None]
    cosine, sine = turn_tables(positions, key_size // 2)
    key_scale = key_size ** (-0.5)
    query_pre = pre[:, :key_size].reshape(seqs, span, key_size)
    key_pre = pre[:, key_size : 2 * key_size].reshape(seqs, span, key_size)
    value_pre = pre[:, 2 * key_size : 2 * key_size + value_size]
    swish_pre = pre[:, 2 * key_size + value_size :]
    queries = rotate(query_pre, cosine, sine).astype(bf16)
    keys = (rotate(key_pre, cosine, sine) * key_scale * valid).astype(bf16)
    values = value_pre.astype(bf16).reshape(seqs, span, value_size)

    log_decay = jnp.log1p(-jnp.exp2(-5.0 - head.astype(f32)))
    offsets = jnp.arange(span)
    distance = (offsets[:, None] - offsets[None, :]).astype(f32)
    within_fade = jnp.where(distance >= 0, jnp.exp(jnp.maximum(distance, 0.0) * log_decay), 0.0)
    key_fade = jnp.exp((span - 1 - offsets).astype(f32) * log_decay)[:, None]
    query_fade = jnp.exp((offsets + 1).astype(f32) * log_decay)[:, None]
    block_fade = jnp.exp(span * log_decay)

    keys_faded = (keys.astype(f32) * key_fade).astype(bf16)
    queries_faded = (queries.astype(f32) * query_fade).astype(bf16)
    local_state = blocks("sjd,sje->sde", keys_faded, values)
    error_low = error.astype(bf16)
    entering, error_all = pass_and_gather(local_state, block_fade, error_low, 1, 2)
    rest, entering = lax.optimization_barrier((rest, entering))
    ff_w = all_depths(rest[..., value_size:])
    probs = (blocks("sid,sjd->sij", queries, keys) * within_fade).astype(bf16)
    mixed = blocks("sij,sje->sie", probs, values) + blocks("sid,sde->sie", queries_faded, entering)
    gated_wide, gate_back = jax.vjp(
        gate_mix, mixed.reshape(rows, value_size), swish_pre, group[0], group[1]
    )
    gated = gated_wide.astype(bf16)
    branch = scatter_product([gated], out_t, 0, 1)
    hidden = inputs + branch

    mlp_wide, norm_mid_back = jax.vjp(layer_norm, hidden, mlp_gain_full, mlp_bias_full)
    mlp_in = gather_rows(mlp_wide.astype(bf16), 4)
    inner, ff_low, ff_part = feed_forward(mlp_in, error_all, ff_w)

    def sum_depths(grads):
        grads = with_layout_constraint(grads.astype(bf16), Layout((0, 1)))
        mine = lax.psum_scatter(grads, "ctx", scatter_dimension=0, tiled=True)
        return mine.reshape(nf, depth, -1)

    ff_sum = sum_depths(ff_part)
    mlp_in_grad = scatter_product([ff_low], ff_w, 0, 6)
    hidden_norm_grad, grad_mlp_gain, grad_mlp_bias = norm_mid_back(mlp_in_grad)
    hidden_grad = error + hidden_norm_grad

    out_part, gated_grad = gather_products(hidden_grad.astype(bf16), gated, out_t, 10)
    out_sum = sum_depths(out_part)
    mixed_grad, swish_grad, grad_group_gain, grad_group_bias = gate_back(gated_grad)
    swish_low = swish_grad.astype(bf16)
    mixed_low = mixed_grad.astype(bf16).reshape(seqs, span, value_size)
    score_low = (blocks("sie,sje->sij", mixed_low, values) * within_fade).astype(bf16)
    pulled_state = blocks("sid,sie->sde", queries_faded, mixed_low)
    swish_part = product_left(normed, swish_low).astype(bf16)
    swish_part, pulled_state, ff_sum = lax.optimization_barrier(
        (swish_part, pulled_state, ff_sum)
    )
    later, mlp_out, grad_gelu, grad_up, grad_down = pass_and_scatter(
        pulled_state, block_fade, inner, ff_w, 2 * hidden_size, ff_sum, -1, 3
    )
    out_sum, swish_part, later = lax.optimization_barrier((out_sum, swish_part, later))
    swish_sum = sum_depths(swish_part)
    block_own = (hidden + mlp_out).astype(bf16)
    query_grad = blocks("sij,sjd->sid", score_low, keys) + query_fade * blocks(
        "sie,sde->sid", mixed_low, entering
    )
    key_grad = blocks("sij,sid->sjd", score_low, queries) + key_fade * blocks(
        "sje,sde->sjd", values, later
    )
    value_grad = blocks("sij,sie->sje", probs, mixed_low) + blocks(
        "sjd,sde->sje", keys_faded, later
    )
    query_low = rotate_back(query_grad, cosine, sine).astype(bf16).reshape(rows, key_size)
    key_low = rotate_back(key_grad * key_scale * valid, cosine, sine).astype(bf16)
    low = jnp.concatenate(
        [
            query_low,
            key_low.reshape(rows, key_size),
            value_grad.astype(bf16).reshape(rows, value_size),
        ],
        -1,
    )
    attn_part = product_left(normed, low).astype(bf16)
    attn_part, low = lax.optimization_barrier((attn_part, low))
    attn_sum = sum_depths(attn_part)
    normed_grad = scatter_product([low, swish_low], attn_w, 0, 7)
    swish_sum, normed_grad = lax.optimization_barrier((swish_sum, normed_grad))
    input_norm_grad, grad_pre_gain, grad_pre_bias = norm_in_back(normed_grad)
    tokens_own = (hidden_grad + input_norm_grad).astype(bf16)

    norm_parts = jnp.stack([grad_pre_gain, grad_pre_bias, grad_mlp_gain, grad_mlp_bias])
    norm_parts = norm_parts.reshape(4, nf * nc, 1, depth).transpose(1, 2, 0, 3)
    norm_parts = jnp.broadcast_to(norm_parts, (nf * nc, nt, 4, depth)).reshape(nf * nc, nt, -1)
    mine = lax.iota(jnp.int32, nt * heads_local) == head
    group_parts = jnp.stack([grad_group_gain, grad_group_bias]).reshape(1, 2, nf * nc, -1)
    group_parts = jnp.where(mine[:, None, None, None], group_parts, 0.0)
    group_parts = group_parts.reshape(nt, heads_local, 2, nf * nc, -1).transpose(3, 0, 2, 1, 4)
    parts = jnp.concatenate([norm_parts, group_parts.reshape(nf * nc, nt, -1)], -1)
    parts = parts.reshape(nf * nc * nt, -1)
    sums, grad_out, grad_swish, block_out, grad_tokens = close(
        pad_tile(parts), out_sum, swish_sum, block_own, tokens_own, 5
    )
    block_valid = (positions[None, :] < lengths[:, None]).astype(bf16)[:, :, None]
    block_out = block_out.reshape(tokens.shape) * block_valid
    grad_tokens = grad_tokens.reshape(tokens.shape) * block_valid
    grad_out, grad_swish = grad_out.astype(f32), grad_swish.astype(f32)
    sums, attn_sum, block_out, grad_tokens, grad_out, grad_swish = lax.optimization_barrier(
        (sums, attn_sum, block_out, grad_tokens, grad_out, grad_swish)
    )
    sums = sums.reshape(-1)[: parts.shape[1]]
    grad_query, grad_key, grad_value = finish(
        [attn_sum], [[key_size, key_size, value_size]], [False], 11
    )
    norm_sums = sums[: 4 * depth].reshape(4, depth)
    group_sums = sums[4 * depth :].reshape(2, heads_local, -1)

    return (
        block_out,
        grad_tokens,
        norm_sums[0],
        norm_sums[1],
        grad_query,
        grad_key,
        grad_value,
        grad_swish,
        grad_out,
        group_sums[0],
        group_sums[1],
        norm_sums[2],
        norm_sums[3],
        grad_gelu,
        grad_up,
        grad_down,
    )


def solution(mesh):
    rows = P("fsdp", "ctx", None)
    vector = P(("fsdp", "ctx"))
    tall = P(("fsdp", "ctx"), "tp")
    wide = P("tp", ("fsdp", "ctx"))
    in_specs = (rows, P("fsdp"), rows, vector, vector, tall, tall, tall, tall, wide)
    in_specs += (wide, wide, vector, vector, tall, tall, wide)
    out_specs = (rows, rows, vector, vector, tall, tall, tall, tall, wide)
    out_specs += (wide, wide, vector, vector, tall, tall, wide)
    return jax.shard_map(shards, mesh=mesh, in_specs=in_specs, out_specs=out_specs, check_vma=False)
```
